256 devices in a mesh: seq: 32 (over x, y, core), user: 8 (over z).
Axes of the slice: x: 4, y: 4, z: 8, core: 2. Of those that a mesh axis runs over, the one named last changes fastest.
Arguments:
- tokens: bfloat16 [8, 8192, 1024], P('user', 'seq'), may hold values from -6 to 6
- w_query: bfloat16 [1024, 1024], replicated, may hold values from -0.1875 to 0.1875
- w_key: bfloat16 [1024, 1024], replicated, may hold values from -0.1875 to 0.1875
- w_value: bfloat16 [1024, 1024], replicated, may hold values from -0.1875 to 0.1875
- w_out: bfloat16 [1024, 1024], replicated, may hold values from -0.1875 to 0.1875
- norm_gain: float32 [1024], replicated, may hold values from 0.3 to 3
- lengths: int32 [8], P('user'), may hold values from 2048 to 8192, as said below
- d_mixed: bfloat16 [8, 8192, 1024], P('user', 'seq'), may hold values from -6 to 6
Outputs:
- mixed_out: bfloat16 [8, 8192, 1024], P('user', 'seq')
- d_tokens: bfloat16 [8, 8192, 1024], P('user', 'seq')
- d_weights: float32 [2, 1048576], P(None, ('seq', 'user'))
- d_gain: float32 [1024], replicated
The draws below stay inside these ranges and needn't reach their ends.
Inputs may be any that keep to these rules, and one draw needn't show every extreme that they name: `lengths`: valid events come first in each history and padding follows; some user has all 8192 events and some user has 2048.
All inputs are finite; a program needn't handle non-finite values.
Results may differ from the reference program's by a relative error of at most 0.0058.
Values sent between devices are 32-bit elements; how exact they have to be, the bound alone decides.
No kernel may reach another device: no remote copies, remote signals or barrier semaphores. Data moves between devices by JAX's collectives and lax.ppermute only.
A program may use at most 128 MiB of HBM per device.

```python
import math
import jax
import jax.numpy as jnp
from jax import lax

HEADS = 16
HD = 64
D = 1024
LENGTH = 8192
USERS = 8


def draw_lengths(key, part):
    key = jax.random.fold_in(key, 7)
    key_base, key_long, key_short = jax.random.split(key, 3)
    base_len = jax.random.randint(key_base, (USERS,), LENGTH // 4, LENGTH + 1)
    longest = jax.random.randint(key_long, (), 0, USERS)
    shortest = (longest + 1 + jax.random.randint(key_short, (), 0, USERS - 1)) % USERS
    user_index = jnp.arange(USERS)
    base_len = jnp.where(user_index == longest, LENGTH, base_len)
    base_len = jnp.where(user_index == shortest, LENGTH // 4, base_len)
    return base_len.astype(jnp.int32)


def raised(entries, stream_key, source, target, blocks, factor):
    owner, partner = [(jnp.arange(entries.shape[position]) // (entries.shape[position] // blocks)).reshape([-1 if axis == position else 1 for axis in range(entries.ndim)]) for position in (source, target)]
    chosen = jax.random.permutation(stream_key, blocks)[partner]
    strong = (owner == chosen) | (owner == (partner + blocks // 2) % blocks)
    return jnp.where(strong, factor * entries, entries)


def block_scale(stream_key, extent, cuts, least, largest):
    loudness, own = 1.0, jax.random.fold_in(stream_key, 6)
    for axis_at, blocks in cuts:
        heights = jnp.exp(jax.random.uniform(jax.random.fold_in(own, axis_at), (blocks,), jnp.float32, least / len(cuts), largest / len(cuts)))
        loudness = loudness * jnp.repeat(heights, extent[axis_at] // blocks).reshape([-1 if axis == axis_at else 1 for axis in range(len(extent))])
    return loudness


def normal_values(stream_key, extent, spread, reach, cuts=(), held_as=jnp.bfloat16):
    values = spread * jax.random.normal(stream_key, extent, jnp.float32)
    if cuts:
        values = values * block_scale(stream_key, extent, cuts, -0.22, 0.18)
    return jnp.clip(values, -reach, reach).astype(held_as)


def bell_draw_with(key, extent, scale, limit, cuts, heavy, dtype=jnp.bfloat16):
    entries = scale * jax.random.normal(key, extent, jnp.float32)
    if cuts:
        entries = entries * block_scale(key, extent, cuts, -0.22, 0.18)
    return jnp.clip(raised(entries, jax.random.fold_in(key, 3), *heavy), -limit, limit).astype(dtype)


def setup_inputs(seed: int = 0) -> dict:
    splits = jax.random.split(jax.random.key(seed), 9)
    return {
        "tokens": bell_draw_with(splits[0], (USERS, LENGTH, D), 1.0, 6.0, ((0, 8), (1, 32)), (1, 2, 32, 2.75)),
        "w_query": normal_values(splits[1], (D, D), D ** -0.5, 0.1875),
        "w_key": normal_values(splits[2], (D, D), D ** -0.5, 0.1875),
        "w_value": normal_values(splits[3], (D, D), D ** -0.5, 0.1875),
        "w_out": normal_values(splits[4], (D, D), D ** -0.5, 0.1875),
        "norm_gain": jnp.clip(jnp.exp(jax.random.uniform(splits[5], (D,), jnp.float32, math.log(0.3), math.log(3.0))), 0.3, 3.0),
        "lengths": draw_lengths(jax.random.fold_in(splits[8], 71), 0),
        "d_mixed": normal_values(splits[7], (USERS, LENGTH, D), 1.0, 6.0, ((0, 8), (1, 32))),
    }


EPS = 1e-05
PRECISE = lax.Precision.HIGHEST

def feature(raw_values):
    return jax.nn.elu(raw_values) + 1.0

def elu_slope(raw_values):
    return jnp.where(raw_values > 0, 1.0, jnp.exp(jnp.minimum(raw_values, 0.0)))

def one_user(inputs, w_query, w_key, w_value, w_out, norm_gain):
    tokens_u, valid_mask, grad_u = inputs
    block_rows = min(512, LENGTH)
    nblocks = LENGTH // block_rows
    query_proj = jnp.dot(tokens_u, w_query, preferred_element_type=jnp.float32).reshape(LENGTH, HEADS, HD)
    key_proj = jnp.dot(tokens_u, w_key, preferred_element_type=jnp.float32).reshape(LENGTH, HEADS, HD)
    value_proj = jnp.dot(tokens_u, w_value, preferred_element_type=jnp.float32).reshape(LENGTH, HEADS, HD)
    query_bf = lax.optimization_barrier(feature(query_proj).astype(jnp.bfloat16))
    key_bf = lax.optimization_barrier((feature(key_proj) * valid_mask[:, None, None]).astype(jnp.bfloat16))
    value_bf = lax.optimization_barrier(value_proj.astype(jnp.bfloat16))
    query_feat = query_bf.astype(jnp.float32).reshape(nblocks, block_rows, HEADS, HD)
    key_feat = key_bf.astype(jnp.float32).reshape(nblocks, block_rows, HEADS, HD)
    value_blk = value_bf.astype(jnp.float32).reshape(nblocks, block_rows, HEADS, HD)
    causal = (jnp.arange(block_rows)[:, None] >= jnp.arange(block_rows)[None, :]).astype(jnp.float32)
    zero_state = jnp.zeros((HEADS, HD, HD), jnp.float32)

    def forward(state, pieces):
        q_blk, k_blk, v_blk = pieces
        scores = jnp.einsum('the,she->hts', q_blk, k_blk, precision=PRECISE) * causal
        numerator = jnp.einsum('hts,shf->thf', scores, v_blk, precision=PRECISE)
        numerator = numerator + jnp.einsum('the,hef->thf', q_blk, state, precision=PRECISE)
        new_state = state + jnp.einsum('the,thf->hef', k_blk, v_blk, precision=PRECISE)
        return (new_state, (numerator, state))
    _, (numerator, earlier) = lax.scan(forward, zero_state, (query_feat, key_feat, value_blk))
    numerator = numerator.reshape(LENGTH, HEADS, HD)
    inv_rms = lax.rsqrt(lax.optimization_barrier(jnp.mean(numerator * numerator, axis=-1, keepdims=True)) + EPS)
    normed = (numerator * inv_rms).reshape(LENGTH, D)
    attended = (normed * norm_gain * valid_mask[:, None]).astype(jnp.bfloat16)
    mixed_out = jnp.dot(attended, w_out, preferred_element_type=jnp.float32).astype(jnp.bfloat16)
    d_output = jnp.dot(grad_u, w_out.T, preferred_element_type=jnp.float32)
    gain_part = lax.optimization_barrier(jnp.sum(d_output * valid_mask[:, None] * normed, axis=0))
    gated_grad = (d_output * valid_mask[:, None] * norm_gain).reshape(LENGTH, HEADS, HD)
    d_numer = inv_rms * gated_grad - inv_rms ** 3 * numerator * lax.optimization_barrier(jnp.mean(gated_grad * numerator, axis=-1, keepdims=True))
    grad_blk = d_numer.reshape(nblocks, block_rows, HEADS, HD)

    def backward(later_grad, pieces):
        q_blk, k_blk, v_blk, g_blk, state_prev = pieces
        scores = jnp.einsum('the,she->hts', q_blk, k_blk, precision=PRECISE) * causal
        weights = jnp.einsum('thf,shf->hts', g_blk, v_blk, precision=PRECISE) * causal
        d_fq = jnp.einsum('thf,hef->the', g_blk, state_prev, precision=PRECISE)
        d_fq = d_fq + jnp.einsum('hts,she->the', weights, k_blk, precision=PRECISE)
        d_fk = jnp.einsum('hts,the->she', weights, q_blk, precision=PRECISE)
        d_fk = d_fk + jnp.einsum('shf,hef->she', v_blk, later_grad, precision=PRECISE)
        d_fv = jnp.einsum('hts,thf->shf', scores, g_blk, precision=PRECISE)
        d_fv = d_fv + jnp.einsum('she,hef->shf', k_blk, later_grad, precision=PRECISE)
        new_grad = later_grad + jnp.einsum('the,thf->hef', q_blk, g_blk, precision=PRECISE)
        return (new_grad, (d_fq, d_fk, d_fv))
    _, (d_fq, d_fk, d_fv) = lax.scan(backward, zero_state, (query_feat, key_feat, value_blk, grad_blk, earlier), reverse=True)
    d_fq = d_fq.reshape(LENGTH, HEADS, HD)
    d_fk = d_fk.reshape(LENGTH, HEADS, HD)
    d_fv = d_fv.reshape(LENGTH, HEADS, HD)
    d_query = (d_fq * elu_slope(query_proj)).astype(jnp.bfloat16).reshape(LENGTH, D)
    d_key = (d_fk * valid_mask[:, None, None] * elu_slope(key_proj)).astype(jnp.bfloat16).reshape(LENGTH, D)
    d_value = d_fv.astype(jnp.bfloat16).reshape(LENGTH, D)
    d_tok = jnp.dot(d_query, w_query.T, preferred_element_type=jnp.float32)
    d_tok = d_tok + jnp.dot(d_key, w_key.T, preferred_element_type=jnp.float32)
    d_tok = d_tok + jnp.dot(d_value, w_value.T, preferred_element_type=jnp.float32)
    return (mixed_out, d_tok.astype(jnp.bfloat16), d_query, d_key, gain_part)

def reference(tokens, w_query, w_key, w_value, w_out, norm_gain, lengths, d_mixed):
    valid_mask = (jnp.arange(LENGTH).astype(jnp.int32)[None, :] < lengths[:, None]).astype(jnp.float32)

    def per_user(inputs):
        return one_user(inputs, w_query, w_key, w_value, w_out, norm_gain)
    mixed_out, d_tokens, d_query, d_key, gain_part = lax.map(per_user, (tokens, valid_mask, d_mixed))
    flat_tokens = tokens.reshape(USERS * LENGTH, D)
    grad_q = jnp.dot(flat_tokens.T, d_query.reshape(USERS * LENGTH, D), preferred_element_type=jnp.float32)
    grad_k = jnp.dot(flat_tokens.T, d_key.reshape(USERS * LENGTH, D), preferred_element_type=jnp.float32)
    d_weights = jnp.stack([grad_q, grad_k]).reshape(2, D * D)
    d_gain = lax.optimization_barrier(jnp.sum(gain_part, axis=0))
    return (mixed_out, d_tokens, d_weights, d_gain)
```

```python
import functools

import jax
import jax.numpy as jnp
from jax import lax
from jax.experimental import pallas as pl
from jax.experimental.pallas import tpu as pltpu
from jax.sharding import Mesh, PartitionSpec as P

EPS = 1e-05
HD = 64
GL = 256
F32 = jnp.float32
BF = jnp.bfloat16
NN = (((1,), (0,)), ((), ()))
NT = (((1,), (1,)), ((), ()))
TN = (((0,), (0,)), ((), ()))
SEQ = ("x", "y", "c")
VMEM_LIMIT = 48 * 1024 * 1024


def dot(a, b, dims=NN):
    return lax.dot_general(a, b, dims, preferred_element_type=F32)


def split(v):
    hi = v.astype(BF)
    return hi, (v - hi.astype(F32)).astype(BF)


def lanes(shape):
    return lax.broadcasted_iota(jnp.int32, shape, 1)


def rows(shape):
    return lax.broadcasted_iota(jnp.int32, shape, 0)


def head_masks(shape):
    which = lanes(shape) // HD
    return [which == h for h in range(GL // HD)]


def pick(mask, v):
    return jnp.where(mask, v, jnp.zeros_like(v))


def pack_state(full):
    out = []
    for p in range(GL // 128):
        blk = full[128 * p:128 * p + 128, 128 * p:128 * p + 128]
        out.append(jnp.where(lanes((HD, 128)) < HD, blk[:HD], blk[HD:]))
    return jnp.concatenate(out, axis=0)


def unpack_state(st):
    zero = jnp.zeros((128, 128), st.dtype)
    blks = []
    for p in range(GL // 128):
        a = st[HD * p:HD * p + HD]
        first = lanes((HD, 128)) < HD
        blks.append(jnp.concatenate([pick(first, a), pick(~first, a)], axis=0))
    return jnp.concatenate(
        [
            jnp.concatenate([blks[0], zero], axis=1),
            jnp.concatenate([zero, blks[1]], axis=1),
        ],
        axis=0,
    )


def valid_rows(nv_ref, count):
    return (rows((count, 1)) < nv_ref[0]).astype(F32)


def features(raw):
    ex = jnp.exp(jnp.minimum(raw, 0.0))
    up = raw > 0
    return jnp.where(up, raw + 1.0, ex), jnp.where(up, 1.0, ex)


def head_mean(v):
    same = (rows((GL, GL)) // HD == lanes((GL, GL)) // HD).astype(BF)
    hi, lo = split(v)
    return (dot(hi, same) + dot(lo, same)) * (1.0 / HD)


def kv_kernel(nv_ref, tok, wk, wv, fk_o, fv_o, sk_o, st_o):
    n = tok.shape[0]
    valid = valid_rows(nv_ref, n)
    feat, slope = features(dot(tok[...], wk[...]))
    fk = (feat * valid).astype(BF)
    fv = dot(tok[...], wv[...]).astype(BF)
    fk_o[...] = fk
    fv_o[...] = fv
    sk_o[...] = slope * valid
    st_o[...] = pack_state(dot(fk, fv, TN))


def turn_kernel(core_ref, tok, own_o, par_o):
    n = own_o.shape[0]
    for which, out in ((core_ref[0], own_o), (1 - core_ref[0], par_o)):
        r = rows((n, 1))
        col = (r // 32) * 64 + which * 32 + r % 32
        one_hot = (lanes((n, tok.shape[1])) == col).astype(BF)
        out[...] = dot(one_hot, tok[...], NT).astype(out.dtype)


def q_kernel(tok, wq, dm, wo, fk, fv, fq_o, fqt_o, sq_o, do_o, nl_o):
    n = tok.shape[0]
    feat, slope = features(dot(tok[...], wq[...]))
    fq = feat.astype(BF)
    fq_o[...] = fq
    sq_o[...] = slope
    eye = (rows((GL, GL)) == lanes((GL, GL))).astype(BF)
    fqt_o[...] = dot(eye, fq, NT).astype(BF)
    do_o[...] = dot(dm[...], wo[...], NT)
    causal = rows((n, n)) >= lanes((n, n))
    total = jnp.zeros((n, GL), F32)
    for m in head_masks((n, GL)):
        hi, lo = split(pick(causal, dot(pick(m, fq), fk[...], NT)))
        vm = pick(m, fv[...])
        total = total + dot(hi, vm) + dot(lo, vm)
    nl_o[...] = total


def norm_kernel(nv_ref, nl, st, fq, fqt, do, gain, at_o, dn_o, rs_o, gp_o):
    n = nl.shape[0]
    valid = valid_rows(nv_ref, n)
    s_hi, s_lo = split(unpack_state(st[...]))
    numer = nl[...] + dot(fq[...], s_hi) + dot(fq[...], s_lo)
    inv = lax.rsqrt(head_mean(numer * numer) + EPS)
    normed = numer * inv
    at_o[...] = (normed * gain[...] * valid).astype(BF)
    dov = do[...] * valid
    gp_o[...] = jnp.sum((dov * normed).reshape(n // 8, 8, GL), axis=0)
    g = dov * gain[...]
    dn = inv * (g - normed * head_mean(g * normed))
    dn_o[...] = dn
    d_hi, d_lo = split(dn)
    rs_o[...] = pack_state(dot(fqt[...], d_hi) + dot(fqt[...], d_lo))


def dq_kernel(dn, st, fk, fv, sq, gp, dq_o, send_o):
    n = dn.shape[0]
    s_hi, s_lo = split(unpack_state(st[...]))
    d_hi, d_lo = split(dn[...])
    total = dot(d_hi, s_hi, NT) + dot(d_lo, s_hi, NT) + dot(d_hi, s_lo, NT)
    causal = rows((n, n)) >= lanes((n, n))
    for m in head_masks((n, GL)):
        vm = pick(m, fv[...])
        hi, lo = split(pick(causal, dot(d_hi, vm, NT) + dot(d_lo, vm, NT)))
        km = pick(m, fk[...])
        total = total + dot(hi, km) + dot(lo, km)
    dq = (total * sq[...]).astype(BF)
    dq_o[...] = dq
    send_o[0:n, :] = dq.astype(F32)
    send_o[n:n + 8, :] = gp[...]


def local_kernel(at, wo, dn, fq, fk, fv, mo_o, lk_o, lv_o):
    n = dn.shape[0]
    mo_o[...] = dot(at[...], wo[...]).astype(BF)
    d_hi, d_lo = split(dn[...])
    later = lanes((n, n)) >= rows((n, n))
    tk = jnp.zeros((n, GL), F32)
    tv = jnp.zeros((n, GL), F32)
    for m in head_masks((n, GL)):
        vm = pick(m, fv[...])
        hi, lo = split(pick(later, dot(vm, d_hi, NT) + dot(vm, d_lo, NT)))
        qm = pick(m, fq[...])
        tk = tk + dot(hi, qm) + dot(lo, qm)
        hi, lo = split(pick(later, dot(pick(m, fk[...]), fq[...], NT)))
        dm = pick(m, d_hi)
        tv = tv + dot(hi, dm) + dot(lo, dm) + dot(hi, pick(m, d_lo))
    lk_o[...] = tk
    lv_o[...] = tv


def dk_kernel(lk, fv, st, sk, dk_o, send_o):
    r_hi, r_lo = split(unpack_state(st[...]))
    total = lk[...] + dot(fv[...], r_hi, NT) + dot(fv[...], r_lo, NT)
    dk = (total * sk[...]).astype(BF)
    dk_o[...] = dk
    send_o[...] = dk.astype(F32)


def dtok_kernel(lv, fk, st, dq, dk, wq, wk, wv, dt_o, acc):
    r_hi, r_lo = split(unpack_state(st[...]))
    dv = (lv[...] + dot(fk[...], r_hi) + dot(fk[...], r_lo)).astype(BF)
    term = dot(dq[...], wq[...], NT) + dot(dk[...], wk[...], NT) + dot(dv, wv[...], NT)

    @pl.when(pl.program_id(0) == 0)
    def _():
        acc[...] = term

    @pl.when(pl.program_id(0) > 0)
    def _():
        acc[...] += term

    @pl.when(pl.program_id(0) == pl.num_programs(0) - 1)
    def _():
        dt_o[...] = acc[...].astype(BF)


def wgrad_kernel(own_t, par_t, own, par, out):
    n = own.shape[0]
    k, m = out.shape[0], out.shape[1]
    res = dot(own_t[...], own[...]) + dot(par_t[...].astype(BF), par[0:n, :].astype(BF))
    out[...] = res.reshape(k, m, res.shape[1])


def wgrad_gain_kernel(own_t, par_t, own, par, gp, out):
    n, width = own.shape
    k, m = out.shape[0], out.shape[1]
    res = dot(own_t[...], own[...]) + dot(par_t[...].astype(BF), par[0:n, :].astype(BF))
    out[:, :, 0:width] = res.reshape(k, m, width)
    g = jnp.sum(gp[...] + par[n:n + 8, :], axis=0, keepdims=True)
    tile = jnp.concatenate([g[:, 128 * i:128 * i + 128] for i in range(width // 128)], axis=0)
    tile = jnp.concatenate([tile, jnp.zeros((m - width // 128, 128), F32)], axis=0)
    for i in range(k):
        out[i, :, width:width + 128] = tile


def prefix_kernel(backward, v, out):
    count = v.shape[0]
    order = range(count - 1, -1, -1) if backward else range(count)
    total = jnp.zeros(v.shape[1:], F32)
    for i in order:
        out[i] = total
        total = total + v[i]


def sum_kernel(v, out):
    total = v[0]
    for i in range(1, v.shape[0]):
        total = total + v[i]
    out[...] = total


def join_kernel(q, k, out):
    ksum = k[0]
    for i in range(1, k.shape[0]):
        ksum = ksum + k[i]
    width = k.shape[2]
    each = k.shape[1] // out.shape[0]
    for u in range(out.shape[0]):
        out[u, 0:each, 0:width] = q[each * u:each * u + each, 0:width]
        out[u, each:2 * each, 0:width] = ksum[each * u:each * u + each]
        out[u, :, width:width + 128] = q[0:8, width:width + 128]


def final_kernel(v, dw_o, dg_o):
    total = v[0]
    for i in range(1, v.shape[0]):
        total = total + v[i]
    width = v.shape[2] - 128
    each = v.shape[1] // 2
    for which in range(2):
        for i in range(each):
            r = which * each + i
            dw_o[which:which + 1, width * i:width * i + width] = total[r:r + 1, 0:width]
    dg_o[...] = total[:, width:width + 128]


def call(kernel, grid, in_specs, outs, name, flops, scratch=()):
    out_shape = [jax.ShapeDtypeStruct(s, d) for s, d, _ in outs]
    return pl.pallas_call(
        kernel,
        grid=grid,
        in_specs=in_specs,
        out_specs=[spec for _, _, spec in outs],
        out_shape=out_shape,
        scratch_shapes=list(scratch),
        name=name,
        cost_estimate=pl.CostEstimate(flops=flops, bytes_accessed=4 << 20, transcendentals=0),
        compiler_params=pltpu.CompilerParams(vmem_limit_bytes=VMEM_LIMIT),
    )


SMEM = pl.BlockSpec(memory_space=pltpu.SMEM)


def whole(shape):
    return pl.BlockSpec(shape, lambda *_: (0,) * len(shape))


def col(r, w=GL):
    return pl.BlockSpec((r, w), lambda g: (0, g))


def row(r, w):
    return pl.BlockSpec((r, w), lambda g: (g, 0))


def on_device(tokens, w_query, w_key, w_value, w_out, norm_gain, lengths, d_mixed):
    _, n, d = tokens.shape
    tok = tokens.reshape(n, d)
    dm = d_mixed.reshape(n, d)
    groups = d // GL
    nseq = lax.axis_size(SEQ)
    nxy = lax.axis_size(("x", "y"))
    nu = lax.axis_size("u")
    nv = lengths - lax.axis_index(SEQ) * n
    core = jnp.full((1,), lax.axis_index("c"), jnp.int32)
    gain = norm_gain.reshape(1, d)
    act = lambda dt: ((n, d), dt, col(n))
    st_rows = d // 2
    state = ((st_rows, 128), F32, row(128, 128))
    big = 2 * n * d * d

    fk, fv, sk, st1 = call(
        kv_kernel, (groups,), [SMEM, whole((n, d)), col(d), col(d)],
        [act(BF), act(BF), act(F32), state], "kv", 2 * big,
    )(nv, tok, w_key, w_value)

    def scan(st, backward, name):
        parts = lax.all_to_all(st.reshape(nseq, st_rows // nseq, 128), SEQ, 0, 0, tiled=True)
        shape = parts.shape
        (mine,) = call(
            functools.partial(prefix_kernel, backward), (), [whole(shape)],
            [(shape, F32, whole(shape))], name, 1 << 20,
        )(parts)
        back = lax.all_to_all(mine, SEQ, 0, 0, tiled=True)
        return back.reshape(st_rows, 128)

    st_in = scan(st1, False, "prefix")

    half = d // 2
    own_t, par_send = call(
        turn_kernel, (), [SMEM, whole((n, d))],
        [((half, n), BF, whole((half, n))), ((half, n), F32, whole((half, n)))],
        "turn", big,
    )(core, tok)
    swap = [(0, 1), (1, 0)]
    par_t = lax.ppermute(par_send, "c", swap)

    fq, fqt, sq, do, nl = call(
        q_kernel, (groups,),
        [whole((n, d)), col(d), whole((n, d)), row(GL, d), col(n), col(n)],
        [act(BF), ((d, n), BF, row(GL, n)), act(F32), act(F32), act(F32)],
        "query", 4 * big,
    )(tok, w_query, dm, w_out, fk, fv)

    at, dn, rs, gp = call(
        norm_kernel, (groups,),
        [SMEM, col(n), row(128, 128), col(n), row(GL, n), col(n), col(1)],
        [act(BF), act(F32), state, ((8, d), F32, col(8))], "norm", big,
    )(nv, nl, st_in, fq, fqt, do, gain)

    r_in = scan(rs, True, "suffix")

    dq, dq_send = call(
        dq_kernel, (groups,),
        [col(n), row(128, 128), col(n), col(n), col(n), col(8)],
        [act(BF), ((n + 8, d), F32, col(n + 8))], "dquery", 2 * big,
    )(dn, st_in, fk, fv, sq, gp)
    dq_par = lax.ppermute(dq_send, "c", swap)

    steps = 4
    gshape = (nxy, half // nxy, d + 128)
    (gq,) = call(
        wgrad_gain_kernel, (steps,),
        [row(half // steps, n), row(half // steps, n), whole((n, d)), whole((n + 8, d)), whole((8, d))],
        [(gshape, F32, pl.BlockSpec((nxy // steps,) + gshape[1:], lambda g: (g, 0, 0)))],
        "wgradq", 2 * big,
    )(own_t, par_t, dq, dq_par, gp)
    gq = lax.all_to_all(gq, ("x", "y"), 0, 0, tiled=True)
    (gq,) = call(
        sum_kernel, (), [whole(gshape)], [(gshape[1:], F32, whole(gshape[1:]))], "sumq", 1 << 22
    )(gq)

    mo, lk, lv = call(
        local_kernel, (groups,),
        [whole((n, d)), col(d), col(n), col(n), col(n), col(n)],
        [act(BF), act(F32), act(F32)], "local", 4 * big,
    )(at, w_out, dn, fq, fk, fv)

    dk, dk_send = call(
        dk_kernel, (groups,), [col(n), col(n), row(128, 128), col(n)],
        [act(BF), act(F32)], "dkey", big // 2,
    )(lk, fv, r_in, sk)
    dk_par = lax.ppermute(dk_send, "c", swap)

    kshape = (nxy, half // nxy, d)
    (gk,) = call(
        wgrad_kernel, (steps,),
        [row(half // steps, n), row(half // steps, n), whole((n, d)), whole((n, d))],
        [(kshape, F32, pl.BlockSpec((nxy // steps,) + kshape[1:], lambda g: (g, 0, 0)))],
        "wgradk", 2 * big,
    )(own_t, par_t, dk, dk_par)
    gk = lax.all_to_all(gk, ("x", "y"), 0, 0, tiled=True)

    (dt,) = call(
        dtok_kernel, (groups,),
        [col(n), col(n), row(128, 128), col(n), col(n), col(d), col(d), col(d)],
        [((n, d), BF, whole((n, d)))], "dtok", 4 * big,
        scratch=[pltpu.VMEM((n, d), F32)],
    )(lv, fk, r_in, dq, dk, w_query, w_key, w_value)

    each = half // nxy // nu
    jshape = (nu, 2 * each, d + 128)
    (both,) = call(
        join_kernel, (), [whole(gshape[1:]), whole(kshape)], [(jshape, F32, whole(jshape))],
        "join", 1 << 22,
    )(gq, gk)
    both = lax.all_to_all(both, "u", 0, 0, tiled=True)
    dw, dg = call(
        final_kernel, (), [whole(jshape)],
        [((2, each * d), F32, whole((2, each * d))), ((8, 128), F32, whole((8, 128)))],
        "final", 1 << 20,
    )(both)
    return mo.reshape(1, n, d), dt.reshape(1, n, d), dw, dg.reshape(d)


def solution(mesh):
    fine = Mesh(mesh.devices.reshape(4, 4, 2, 8), ("x", "y", "c", "u"))
    acts = P("u", SEQ, None)
    placed = (acts, P(), P(), P(), P(), P(), P("u"), acts)
    return jax.shard_map(
        on_device,
        mesh=fine,
        in_specs=placed,
        out_specs=(acts, acts, P(None, ("x", "y", "c", "u")), P()),
        check_vma=False,
    )
```

```python
import functools

import jax
import jax.numpy as jnp
from jax import lax
from jax.experimental import pallas as pl
from jax.experimental.pallas import tpu as pltpu
from jax.sharding import Mesh, PartitionSpec as P

EPS = 1e-05
HD = 64
GL = 256
F32 = jnp.float32
BF = jnp.bfloat16
NN = (((1,), (0,)), ((), ()))
NT = (((1,), (1,)), ((), ()))
TN = (((0,), (0,)), ((), ()))
SEQ = ("x", "y", "c")
VMEM_LIMIT = 64 * 1024 * 1024


def dot(a, b, dims=NN):
    return lax.dot_general(a, b, dims, preferred_element_type=F32)


def split(v):
    hi = v.astype(BF)
    return hi, (v - hi.astype(F32)).astype(BF)


def lanes(shape):
    return lax.broadcasted_iota(jnp.int32, shape, 1)


def rows(shape):
    return lax.broadcasted_iota(jnp.int32, shape, 0)


def head_masks(shape):
    which = lanes(shape) // HD
    return [which == h for h in range(GL // HD)]


def pick(mask, v):
    return jnp.where(mask, v, jnp.zeros_like(v))


def pack_state(full):
    out = []
    for p in range(GL // 128):
        blk = full[128 * p:128 * p + 128, 128 * p:128 * p + 128]
        out.append(jnp.where(lanes((HD, 128)) < HD, blk[:HD], blk[HD:]))
    return jnp.concatenate(out, axis=0)


def unpack_state(st):
    zero = jnp.zeros((128, 128), st.dtype)
    blks = []
    for p in range(GL // 128):
        a = st[HD * p:HD * p + HD]
        first = lanes((HD, 128)) < HD
        blks.append(jnp.concatenate([pick(first, a), pick(~first, a)], axis=0))
    return jnp.concatenate(
        [
            jnp.concatenate([blks[0], zero], axis=1),
            jnp.concatenate([zero, blks[1]], axis=1),
        ],
        axis=0,
    )


def valid_rows(nv_ref, count):
    return (rows((count, 1)) < nv_ref[0]).astype(F32)


def features(raw):
    ex = jnp.exp(jnp.minimum(raw, 0.0))
    up = raw > 0
    return jnp.where(up, raw + 1.0, ex), jnp.where(up, 1.0, ex)


def head_mean(v):
    same = (rows((GL, GL)) // HD == lanes((GL, GL)) // HD).astype(BF)
    hi, lo = split(v)
    return (dot(hi, same) + dot(lo, same)) * (1.0 / HD)


def kv_kernel(nv_ref, tok, wk, wv, fk_o, fv_o, sk_o, st_o):
    n = tok.shape[0]
    valid = valid_rows(nv_ref, n)
    feat, slope = features(dot(tok[...], wk[...]))
    fk = (feat * valid).astype(BF)
    fv = dot(tok[...], wv[...]).astype(BF)
    fk_o[...] = fk
    fv_o[...] = fv
    sk_o[...] = slope * valid
    st_o[...] = pack_state(dot(fk, fv, TN))


def turn_kernel(core_ref, tok, own_o, par_o):
    n = own_o.shape[0]
    for which, out in ((core_ref[0], own_o), (1 - core_ref[0], par_o)):
        r = rows((n, 1))
        col = (r // 32) * 64 + which * 32 + r % 32
        one_hot = (lanes((n, tok.shape[1])) == col).astype(BF)
        out[...] = dot(one_hot, tok[...], NT).astype(out.dtype)


def q_kernel(tok, wq, dm, wo, fq_o, fqt_o, sq_o, do_o):
    feat, slope = features(dot(tok[...], wq[...]))
    fq = feat.astype(BF)
    fq_o[...] = fq
    sq_o[...] = slope
    eye = (rows((GL, GL)) == lanes((GL, GL))).astype(BF)
    fqt_o[...] = dot(eye, fq, NT).astype(BF)
    do_o[...] = dot(dm[...], wo[...], NT)


def numer_kernel(fq, fk, fv, nl_o):
    n = fq.shape[0]
    causal = rows((n, n)) >= lanes((n, n))
    total = jnp.zeros((n, GL), F32)
    for m in head_masks((n, GL)):
        hi, lo = split(pick(causal, dot(pick(m, fq[...]), fk[...], NT)))
        vm = pick(m, fv[...])
        total = total + dot(hi, vm) + dot(lo, vm)
    nl_o[...] = total


def norm_kernel(nv_ref, nl, st, fq, fqt, do, gain, at_o, dn_o, rs_o, gp_o):
    n = nl.shape[0]
    valid = valid_rows(nv_ref, n)
    s_hi, s_lo = split(unpack_state(st[...]))
    numer = nl[...] + dot(fq[...], s_hi) + dot(fq[...], s_lo)
    inv = lax.rsqrt(head_mean(numer * numer) + EPS)
    normed = numer * inv
    at_o[...] = (normed * gain[...] * valid).astype(BF)
    dov = do[...] * valid
    gp_o[...] = jnp.sum((dov * normed).reshape(n // 8, 8, GL), axis=0)
    g = dov * gain[...]
    dn = inv * (g - normed * head_mean(g * normed))
    dn_o[...] = dn
    d_hi, d_lo = split(dn)
    rs_o[...] = pack_state(dot(fqt[...], d_hi) + dot(fqt[...], d_lo))


def dq_kernel(dn, st, fk, fv, sq, gp, dq_o, send_o):
    n = dn.shape[0]
    s_hi, s_lo = split(unpack_state(st[...]))
    d_hi, d_lo = split(dn[...])
    total = dot(d_hi, s_hi, NT) + dot(d_lo, s_hi, NT) + dot(d_hi, s_lo, NT)
    causal = rows((n, n)) >= lanes((n, n))
    for m in head_masks((n, GL)):
        vm = pick(m, fv[...])
        hi, lo = split(pick(causal, dot(d_hi, vm, NT) + dot(d_lo, vm, NT)))
        km = pick(m, fk[...])
        total = total + dot(hi, km) + dot(lo, km)
    dq = (total * sq[...]).astype(BF)
    dq_o[...] = dq
    send_o[0:n, :] = dq.astype(F32)
    send_o[n:n + 8, :] = gp[...]


def local_k_kernel(dn, fq, fv, lk_o):
    n = dn.shape[0]
    d_hi, d_lo = split(dn[...])
    later = lanes((n, n)) >= rows((n, n))
    tk = jnp.zeros((n, GL), F32)
    for m in head_masks((n, GL)):
        vm = pick(m, fv[...])
        hi, lo = split(pick(later, dot(vm, d_hi, NT) + dot(vm, d_lo, NT)))
        qm = pick(m, fq[...])
        tk = tk + dot(hi, qm) + dot(lo, qm)
    lk_o[...] = tk


def local_v_kernel(at, wo, dn, fq, fk, mo_o, lv_o):
    n = dn.shape[0]
    mo_o[...] = dot(at[...], wo[...]).astype(BF)
    d_hi, d_lo = split(dn[...])
    later = lanes((n, n)) >= rows((n, n))
    tv = jnp.zeros((n, GL), F32)
    for m in head_masks((n, GL)):
        hi, lo = split(pick(later, dot(pick(m, fk[...]), fq[...], NT)))
        dm = pick(m, d_hi)
        tv = tv + dot(hi, dm) + dot(lo, dm) + dot(hi, pick(m, d_lo))
    lv_o[...] = tv


def dk_kernel(lk, fv, st, sk, dk_o, send_o):
    r_hi, r_lo = split(unpack_state(st[...]))
    total = lk[...] + dot(fv[...], r_hi, NT) + dot(fv[...], r_lo, NT)
    dk = (total * sk[...]).astype(BF)
    dk_o[...] = dk
    send_o[...] = dk.astype(F32)


def dtok_kernel(lv, fk, st, dq, dk, wq, wk, wv, dt_o, acc):
    r_hi, r_lo = split(unpack_state(st[...]))
    dv = (lv[...] + dot(fk[...], r_hi) + dot(fk[...], r_lo)).astype(BF)
    term = dot(dq[...], wq[...], NT) + dot(dk[...], wk[...], NT) + dot(dv, wv[...], NT)

    @pl.when(pl.program_id(0) == 0)
    def _():
        acc[...] = term

    @pl.when(pl.program_id(0) > 0)
    def _():
        acc[...] += term

    @pl.when(pl.program_id(0) == pl.num_programs(0) - 1)
    def _():
        dt_o[...] = acc[...].astype(BF)


def wgrad_kernel(own_t, par_t, own, par, out):
    n = own.shape[0]
    k, m = out.shape[0], out.shape[1]
    res = dot(own_t[...], own[...]) + dot(par_t[...].astype(BF), par[0:n, :].astype(BF))
    out[...] = res.reshape(k, m, res.shape[1])


def wgrad_gain_kernel(own_t, par_t, own, par, gp, out):
    n, width = own.shape
    k, m = out.shape[0], out.shape[1]
    res = dot(own_t[...], own[...]) + dot(par_t[...].astype(BF), par[0:n, :].astype(BF))
    out[:, :, 0:width] = res.reshape(k, m, width)
    g = jnp.sum(gp[...] + par[n:n + 8, :], axis=0, keepdims=True)
    tile = jnp.concatenate([g[:, 128 * i:128 * i + 128] for i in range(width // 128)], axis=0)
    tile = jnp.concatenate([tile, jnp.zeros((m - width // 128, 128), F32)], axis=0)
    for i in range(k):
        out[i, :, width:width + 128] = tile


def prefix_kernel(backward, v, out):
    count = v.shape[0]
    order = range(count - 1, -1, -1) if backward else range(count)
    total = jnp.zeros(v.shape[1:], F32)
    for i in order:
        out[i] = total
        total = total + v[i]


def join_kernel(q, k, out):
    ksum = k[0]
    for i in range(1, k.shape[0]):
        ksum = ksum + k[i]
    width = k.shape[2]
    each = k.shape[1] // out.shape[0]
    for u in range(out.shape[0]):
        out[u, 0:each, 0:width] = q[each * u:each * u + each, 0:width]
        out[u, each:2 * each, 0:width] = ksum[each * u:each * u + each]
        out[u, :, width:width + 128] = q[0:8, width:width + 128]


def final_kernel(v, dw_o, dg_o):
    total = v[0]
    for i in range(1, v.shape[0]):
        total = total + v[i]
    width = v.shape[2] - 128
    each = v.shape[1] // 2
    for which in range(2):
        for i in range(each):
            r = which * each + i
            dw_o[which:which + 1, width * i:width * i + width] = total[r:r + 1, 0:width]
    dg_o[...] = total[:, width:width + 128]


def call(kernel, grid, in_specs, outs, name, flops, scratch=()):
    out_shape = [jax.ShapeDtypeStruct(s, d) for s, d, _ in outs]
    return pl.pallas_call(
        kernel,
        grid=grid,
        in_specs=in_specs,
        out_specs=[spec for _, _, spec in outs],
        out_shape=out_shape,
        scratch_shapes=list(scratch),
        name=name,
        cost_estimate=pl.CostEstimate(flops=flops, bytes_accessed=4 << 20, transcendentals=0),
        compiler_params=pltpu.CompilerParams(vmem_limit_bytes=VMEM_LIMIT),
    )


SMEM = pl.BlockSpec(memory_space=pltpu.SMEM)


def whole(shape):
    return pl.BlockSpec(shape, lambda *_: (0,) * len(shape))


def col(r, w=GL):
    return pl.BlockSpec((r, w), lambda g: (0, g))


def row(r, w):
    return pl.BlockSpec((r, w), lambda g: (g, 0))


def on_device(tokens, w_query, w_key, w_value, w_out, norm_gain, lengths, d_mixed):
    _, n, d = tokens.shape
    tok = tokens.reshape(n, d)
    dm = d_mixed.reshape(n, d)
    groups = d // GL
    nseq = lax.axis_size(SEQ)
    nxy = lax.axis_size(("x", "y"))
    nu = lax.axis_size("u")
    nv = lengths - lax.axis_index(SEQ) * n
    core = jnp.full((1,), lax.axis_index("c"), jnp.int32)
    gain = norm_gain.reshape(1, d)
    act = lambda dt: ((n, d), dt, col(n))
    st_rows = d // 2
    state = ((st_rows, 128), F32, row(128, 128))
    big = 2 * n * d * d

    fk, fv, sk, st1 = call(
        kv_kernel, (groups,), [SMEM, whole((n, d)), col(d), col(d)],
        [act(BF), act(BF), act(F32), state], "kv", 2 * big,
    )(nv, tok, w_key, w_value)

    tie = lax.optimization_barrier

    def to_parts(st):
        return lax.all_to_all(st.reshape(nseq, st_rows // nseq, 128), SEQ, 0, 0, tiled=True)

    def run(parts, backward, name):
        shape = parts.shape
        (mine,) = call(
            functools.partial(prefix_kernel, backward), (), [whole(shape)],
            [(shape, F32, whole(shape))], name, 1 << 20,
        )(parts)
        return mine

    def from_parts(mine):
        return lax.all_to_all(mine, SEQ, 0, 0, tiled=True).reshape(st_rows, 128)

    parts = to_parts(st1)
    tok_1, _ = tie((tok, st1))
    half = d // 2
    own_t, par_send = call(
        turn_kernel, (), [SMEM, whole((n, d))],
        [((half, n), BF, whole((half, n))), ((half, n), F32, whole((half, n)))],
        "turn", big,
    )(core, tok_1)
    swap = [(0, 1), (1, 0)]
    par_t = lax.ppermute(par_send, "c", swap)
    fq, fqt, sq, do = call(
        q_kernel, (groups,), [whole((n, d)), col(d), whole((n, d)), row(GL, d)],
        [act(BF), ((d, n), BF, row(GL, n)), act(F32), act(F32)], "query", 2 * big,
    )(tok_1, w_query, dm, w_out)
    parts, fq, own_t = tie((parts, fq, own_t))
    mine = run(parts, False, "prefix")

    st_in = from_parts(mine)
    fq_2, _ = tie((fq, mine))
    (nl,) = call(
        numer_kernel, (groups,), [col(n), col(n), col(n)], [act(F32)], "numer", 2 * big,
    )(fq_2, fk, fv)

    at, dn, rs, gp = call(
        norm_kernel, (groups,),
        [SMEM, col(n), row(128, 128), col(n), row(GL, n), col(n), col(1)],
        [act(BF), act(F32), state, ((8, d), F32, col(8))], "norm", big,
    )(nv, nl, st_in, fq, fqt, do, gain)

    parts = to_parts(rs)
    dn_3, _ = tie((dn, rs))
    dq, dq_send = call(
        dq_kernel, (groups,),
        [col(n), row(128, 128), col(n), col(n), col(n), col(8)],
        [act(BF), ((n + 8, d), F32, col(n + 8))], "dquery", 2 * big,
    )(dn_3, st_in, fk, fv, sq, gp)
    parts, dq, dq_send = tie((parts, dq, dq_send))
    mine = run(parts, True, "suffix")

    r_in = from_parts(mine)
    dq_send, dn_4, _ = tie((dq_send, dn, mine))
    dq_par = lax.ppermute(dq_send, "c", swap)
    (lk,) = call(
        local_k_kernel, (groups,), [col(n), col(n), col(n)], [act(F32)], "localk", 2 * big,
    )(dn_4, fq, fv)
    dk, dk_send = call(
        dk_kernel, (groups,), [col(n), col(n), row(128, 128), col(n)],
        [act(BF), act(F32)], "dkey", big // 2,
    )(lk, fv, r_in, sk)

    dk_par = lax.ppermute(dk_send, "c", swap)
    steps = 4
    gshape = (nxy, half // nxy, d + 128)
    dq_5, _ = tie((dq, dk))
    (gq,) = call(
        wgrad_gain_kernel, (steps,),
        [row(half // steps, n), row(half // steps, n), whole((n, d)), whole((n + 8, d)), whole((8, d))],
        [(gshape, F32, pl.BlockSpec((nxy // steps,) + gshape[1:], lambda g: (g, 0, 0)))],
        "wgradq", 2 * big,
    )(own_t, par_t, dq_5, dq_par, gp)
    gq_sum = lax.psum_scatter(gq, ("x", "y"), scatter_dimension=0, tiled=True)
    gq_sum = gq_sum.reshape(gshape[1:])

    kshape = (nxy, half // nxy, d)
    (gk,) = call(
        wgrad_kernel, (steps,),
        [row(half // steps, n), row(half // steps, n), whole((n, d)), whole((n, d))],
        [(kshape, F32, pl.BlockSpec((nxy // steps,) + kshape[1:], lambda g: (g, 0, 0)))],
        "wgradk", 2 * big,
    )(own_t, par_t, dk, dk_par)
    gk_parts = lax.all_to_all(gk, ("x", "y"), 0, 0, tiled=True)

    dn_5, dk_5, _ = tie((dn, dk, gk))
    mo, lv = call(
        local_v_kernel, (groups,),
        [whole((n, d)), col(d), col(n), col(n), col(n)], [act(BF), act(F32)], "localv", 4 * big,
    )(at, w_out, dn_5, fq, fk)
    (dt,) = call(
        dtok_kernel, (groups,),
        [col(n), col(n), row(128, 128), col(n), col(n), col(d), col(d), col(d)],
        [((n, d), BF, whole((n, d)))], "dtok", 4 * big,
        scratch=[pltpu.VMEM((n, d), F32)],
    )(lv, fk, r_in, dq, dk_5, w_query, w_key, w_value)
    gk_parts, mo, dt = tie((gk_parts, mo, dt))

    each = half // nxy // nu
    jshape = (nu, 2 * each, d + 128)
    (both,) = call(
        join_kernel, (), [whole(gshape[1:]), whole(kshape)], [(jshape, F32, whole(jshape))],
        "join", 1 << 22,
    )(gq_sum, gk_parts)
    both = lax.all_to_all(both, "u", 0, 0, tiled=True)
    dw, dg = call(
        final_kernel, (), [whole(jshape)],
        [((2, each * d), F32, whole((2, each * d))), ((8, 128), F32, whole((8, 128)))],
        "final", 1 << 20,
    )(both)
    return mo.reshape(1, n, d), dt.reshape(1, n, d), dw, dg.reshape(d)


def solution(mesh):
    fine = Mesh(mesh.devices.reshape(4, 4, 2, 8), ("x", "y", "c", "u"))
    acts = P("u", SEQ, None)
    placed = (acts, P(), P(), P(), P(), P(), P("u"), acts)
    return jax.shard_map(
        on_device,
        mesh=fine,
        in_specs=placed,
        out_specs=(acts, acts, P(None, ("x", "y", "c", "u")), P()),
        check_vma=False,
    )
```

```python
import functools

import jax
import jax.numpy as jnp
from jax import lax
from jax.experimental import pallas as pl
from jax.experimental.pallas import tpu as pltpu
from jax.sharding import Mesh, PartitionSpec as P

EPS = 1e-05
HD = 64
GL = 256
F32 = jnp.float32
BF = jnp.bfloat16
NN = (((1,), (0,)), ((), ()))
NT = (((1,), (1,)), ((), ()))
TN = (((0,), (0,)), ((), ()))
SEQ = ("x", "y", "c")
GROUP = ("c", "b")
VMEM_LIMIT = 64 * 1024 * 1024


def dot(a, b, dims=NN):
    return lax.dot_general(a, b, dims, preferred_element_type=F32)


def split(v):
    hi = v.astype(BF)
    return hi, (v - hi.astype(F32)).astype(BF)


def lanes(shape):
    return lax.broadcasted_iota(jnp.int32, shape, 1)


def rows(shape):
    return lax.broadcasted_iota(jnp.int32, shape, 0)


def head_masks(shape):
    which = lanes(shape) // HD
    return [which == h for h in range(GL // HD)]


def pick(mask, v):
    return jnp.where(mask, v, jnp.zeros_like(v))


def pack_state(full):
    out = []
    for p in range(GL // 128):
        blk = full[128 * p:128 * p + 128, 128 * p:128 * p + 128]
        out.append(jnp.where(lanes((HD, 128)) < HD, blk[:HD], blk[HD:]))
    return jnp.concatenate(out, axis=0)


def unpack_state(st):
    zero = jnp.zeros((128, 128), st.dtype)
    blks = []
    for p in range(GL // 128):
        a = st[HD * p:HD * p + HD]
        first = lanes((HD, 128)) < HD
        blks.append(jnp.concatenate([pick(first, a), pick(~first, a)], axis=0))
    return jnp.concatenate(
        [
            jnp.concatenate([blks[0], zero], axis=1),
            jnp.concatenate([zero, blks[1]], axis=1),
        ],
        axis=0,
    )


def valid_rows(nv_ref, count):
    return (rows((count, 1)) < nv_ref[0]).astype(F32)


def features(raw):
    ex = jnp.exp(jnp.minimum(raw, 0.0))
    up = raw > 0
    return jnp.where(up, raw + 1.0, ex), jnp.where(up, 1.0, ex)


def head_mean(v):
    same = (rows((GL, GL)) // HD == lanes((GL, GL)) // HD).astype(BF)
    hi, lo = split(v)
    return (dot(hi, same) + dot(lo, same)) * (1.0 / HD)


def kv_kernel(nv_ref, tok, wk, wv, fk_o, fv_o, sk_o, st_o):
    n = tok.shape[0]
    valid = valid_rows(nv_ref, n)
    feat, slope = features(dot(tok[...], wk[...]))
    fk = (feat * valid).astype(BF)
    fv = dot(tok[...], wv[...]).astype(BF)
    fk_o[...] = fk
    fv_o[...] = fv
    sk_o[...] = slope * valid
    st_o[...] = pack_state(dot(fk, fv, TN))


def turn_kernel(tok, t16_o, t32_o):
    n = tok.shape[0]
    eye = (rows((n, n)) == lanes((n, n))).astype(BF)
    res = dot(tok[...], eye, TN)
    t16_o[...] = res.astype(BF)
    t32_o[...] = res


def q_kernel(tok, wq, dm, wo, fq_o, fqt_o, sq_o, do_o):
    feat, slope = features(dot(tok[...], wq[...]))
    fq = feat.astype(BF)
    fq_o[...] = fq
    sq_o[...] = slope
    eye = (rows((GL, GL)) == lanes((GL, GL))).astype(BF)
    fqt_o[...] = dot(eye, fq, NT).astype(BF)
    do_o[...] = dot(dm[...], wo[...], NT)


def numer_kernel(fq, fk, fv, nl_o):
    n = fq.shape[0]
    causal = rows((n, n)) >= lanes((n, n))
    total = jnp.zeros((n, GL), F32)
    for m in head_masks((n, GL)):
        hi, lo = split(pick(causal, dot(pick(m, fq[...]), fk[...], NT)))
        vm = pick(m, fv[...])
        total = total + dot(hi, vm) + dot(lo, vm)
    nl_o[...] = total


def norm_kernel(nv_ref, nl, st, fq, fqt, do, gain, at_o, dn_o, rs_o, gp_o):
    n = nl.shape[0]
    valid = valid_rows(nv_ref, n)
    s_hi, s_lo = split(unpack_state(st[...]))
    numer = nl[...] + dot(fq[...], s_hi) + dot(fq[...], s_lo)
    inv = lax.rsqrt(head_mean(numer * numer) + EPS)
    normed = numer * inv
    at_o[...] = (normed * gain[...] * valid).astype(BF)
    dov = do[...] * valid
    gp_o[...] = jnp.sum((dov * normed).reshape(n // 8, 8, GL), axis=0)
    g = dov * gain[...]
    dn = inv * (g - normed * head_mean(g * normed))
    dn_o[...] = dn
    d_hi, d_lo = split(dn)
    rs_o[...] = pack_state(dot(fqt[...], d_hi) + dot(fqt[...], d_lo))


def dq_kernel(me_ref, dn, st, fk, fv, sq, gp, dq_o, *send):
    n = dn.shape[0]
    s_hi, s_lo = split(unpack_state(st[...]))
    d_hi, d_lo = split(dn[...])
    total = dot(d_hi, s_hi, NT) + dot(d_lo, s_hi, NT) + dot(d_hi, s_lo, NT)
    causal = rows((n, n)) >= lanes((n, n))
    for m in head_masks((n, GL)):
        vm = pick(m, fv[...])
        hi, lo = split(pick(causal, dot(d_hi, vm, NT) + dot(d_lo, vm, NT)))
        km = pick(m, fk[...])
        total = total + dot(hi, km) + dot(lo, km)
    dq = (total * sq[...]).astype(BF)
    dq_o[...] = dq
    for k, out in enumerate(send):
        @pl.when(pl.program_id(0) == k)
        def _():
            out[0:n, :] = dq.astype(F32)
            out[n:n + 8, :] = gp[...]


def local_k_kernel(dn, fq, fv, lk_o):
    n = dn.shape[0]
    d_hi, d_lo = split(dn[...])
    later = lanes((n, n)) >= rows((n, n))
    tk = jnp.zeros((n, GL), F32)
    for m in head_masks((n, GL)):
        vm = pick(m, fv[...])
        hi, lo = split(pick(later, dot(vm, d_hi, NT) + dot(vm, d_lo, NT)))
        qm = pick(m, fq[...])
        tk = tk + dot(hi, qm) + dot(lo, qm)
    lk_o[...] = tk


def local_v_kernel(at, wo, dn, fq, fk, mo_o, lv_o):
    n = dn.shape[0]
    mo_o[...] = dot(at[...], wo[...]).astype(BF)
    d_hi, d_lo = split(dn[...])
    later = lanes((n, n)) >= rows((n, n))
    tv = jnp.zeros((n, GL), F32)
    for m in head_masks((n, GL)):
        hi, lo = split(pick(later, dot(pick(m, fk[...]), fq[...], NT)))
        dm = pick(m, d_hi)
        tv = tv + dot(hi, dm) + dot(lo, dm) + dot(hi, pick(m, d_lo))
    lv_o[...] = tv


def dk_kernel(me_ref, lk, fv, st, sk, dk_o, *send):
    r_hi, r_lo = split(unpack_state(st[...]))
    total = lk[...] + dot(fv[...], r_hi, NT) + dot(fv[...], r_lo, NT)
    dk = (total * sk[...]).astype(BF)
    dk_o[...] = dk
    for k, out in enumerate(send):
        @pl.when(pl.program_id(0) == k)
        def _():
            out[...] = dk.astype(F32)


def dtok_kernel(lv, fk, st, dq, dk, wq, wk, wv, dt_o, acc):
    r_hi, r_lo = split(unpack_state(st[...]))
    dv = (lv[...] + dot(fk[...], r_hi) + dot(fk[...], r_lo)).astype(BF)
    term = dot(dq[...], wq[...], NT) + dot(dk[...], wk[...], NT) + dot(dv, wv[...], NT)

    @pl.when(pl.program_id(0) == 0)
    def _():
        acc[...] = term

    @pl.when(pl.program_id(0) > 0)
    def _():
        acc[...] += term

    @pl.when(pl.program_id(0) == pl.num_programs(0) - 1)
    def _():
        dt_o[...] = acc[...].astype(BF)


def wgrad_q_kernel(t0, t1, t2, t3, d0, d1, d2, d3, out, all_o):
    n = t0.shape[1]
    k, m = out.shape[0], out.shape[1] - 8
    res = jnp.zeros((t0.shape[0], out.shape[2]), F32)
    gain = jnp.zeros((8, out.shape[2]), F32)
    for i, (t, d) in enumerate(zip((t0, t1, t2, t3), (d0, d1, d2, d3))):
        turned = t[...].astype(BF)
        all_o[:, n * i:n * i + n] = turned
        res = res + dot(turned, d[0:n, :].astype(BF))
        gain = gain + d[n:n + 8, :]
    out[:, 0:m, :] = res.reshape(k, m, res.shape[1])
    for i in range(k):
        out[i, m:m + 8, :] = gain


def wgrad_k_kernel(t, d0, d1, d2, d3, out):
    k, m, w = out.shape
    d = jnp.concatenate([v[...].astype(BF) for v in (d0, d1, d2, d3)], axis=0)
    out[...] = dot(t[...], d).reshape(k, m, w)


def prefix_kernel(backward, v, out):
    count = v.shape[0]
    order = range(count - 1, -1, -1) if backward else range(count)
    total = jnp.zeros(v.shape[1:], F32)
    for i in order:
        out[i] = total
        total = total + v[i]


def sum_kernel(v, out):
    total = v[0]
    for i in range(1, v.shape[0]):
        total = total + v[i]
    out[...] = total


def join_kernel(q, k, out):
    ksum = k[0]
    for i in range(1, k.shape[0]):
        ksum = ksum + k[i]
    height, width = ksum.shape
    gain = jnp.sum(q[height:height + 8, :], axis=0, keepdims=True)
    parts = [gain[:, 128 * i:128 * i + 128] for i in range(width // 128)]
    each = height // out.shape[0]
    parts.append(jnp.zeros((2 * each - len(parts), 128), F32))
    tile = jnp.concatenate(parts, axis=0)
    for j in range(out.shape[0]):
        out[j, 0:each, 0:width] = q[each * j:each * j + each, :]
        out[j, each:2 * each, 0:width] = ksum[each * j:each * j + each]
        out[j, :, width:width + 128] = tile


def final_kernel(v, dw_o, dg_o):
    width = v.shape[2] - 128
    each = v.shape[1] // 2
    for c in range(2):
        for b in range(2):
            g = 2 * c + b
            total = v[8 * c + b]
            for w in range(1, 4):
                total = total + v[8 * c + 2 * w + b]
            for which in range(2):
                for i in range(each):
                    r = which * each + i
                    at = 4 * width * i + width * g
                    dw_o[which:which + 1, at:at + width] = total[r:r + 1, 0:width]
            dg_o[2 * g:2 * g + 2, :] = total[0:2, width:width + 128]


def call(kernel, grid, in_specs, outs, name, flops, scratch=()):
    out_shape = [jax.ShapeDtypeStruct(s, d) for s, d, _ in outs]
    return pl.pallas_call(
        kernel,
        grid=grid,
        in_specs=in_specs,
        out_specs=[spec for _, _, spec in outs],
        out_shape=out_shape,
        scratch_shapes=list(scratch),
        name=name,
        cost_estimate=pl.CostEstimate(flops=flops, bytes_accessed=4 << 20, transcendentals=0),
        compiler_params=pltpu.CompilerParams(vmem_limit_bytes=VMEM_LIMIT),
    )


def call_at(kernel, steps, in_specs, outs, name, flops):
    return pl.pallas_call(
        kernel,
        grid_spec=pltpu.PrefetchScalarGridSpec(
            num_scalar_prefetch=1,
            grid=(steps,),
            in_specs=in_specs,
            out_specs=[spec for _, _, spec in outs],
        ),
        out_shape=[jax.ShapeDtypeStruct(s, d) for s, d, _ in outs],
        name=name,
        cost_estimate=pl.CostEstimate(flops=flops, bytes_accessed=4 << 20, transcendentals=0),
        compiler_params=pltpu.CompilerParams(vmem_limit_bytes=VMEM_LIMIT),
    )


SMEM = pl.BlockSpec(memory_space=pltpu.SMEM)


def whole(shape):
    return pl.BlockSpec(shape, lambda *_: (0,) * len(shape))


def col(r, w=GL):
    return pl.BlockSpec((r, w), lambda g: (0, g))


def row(r, w):
    return pl.BlockSpec((r, w), lambda g: (g, 0))


def col_at(r):
    return pl.BlockSpec((r, GL), lambda k, me: (0, jnp.bitwise_xor(me[0], k)))


def row_at(r, w):
    return pl.BlockSpec((r, w), lambda k, me: (jnp.bitwise_xor(me[0], k), 0))


def on_device(tokens, w_query, w_key, w_value, w_out, norm_gain, lengths, d_mixed):
    _, n, d = tokens.shape
    tok = tokens.reshape(n, d)
    dm = d_mixed.reshape(n, d)
    groups = d // GL
    nseq = lax.axis_size(SEQ)
    nxy = lax.axis_size(("x", "y"))
    ngroup = lax.axis_size(GROUP)
    nv = lengths - lax.axis_index(SEQ) * n
    me = jnp.full((1,), lax.axis_index(GROUP), jnp.int32)
    gain = norm_gain.reshape(1, d)
    act = lambda dt: ((n, d), dt, col(n))
    st_rows = d // 2
    state = ((st_rows, 128), F32, row(128, 128))
    big = 2 * n * d * d

    fk, fv, sk, st1 = call(
        kv_kernel, (groups,), [SMEM, whole((n, d)), col(d), col(d)],
        [act(BF), act(BF), act(F32), state], "kv", 2 * big,
    )(nv, tok, w_key, w_value)

    tie = lax.optimization_barrier

    def to_parts(st):
        return lax.all_to_all(st.reshape(nseq, st_rows // nseq, 128), SEQ, 0, 0, tiled=True)

    def run(parts, backward, name):
        shape = parts.shape
        (mine,) = call(
            functools.partial(prefix_kernel, backward), (), [whole(shape)],
            [(shape, F32, whole(shape))], name, 1 << 20,
        )(parts)
        return mine

    def from_parts(mine):
        return lax.all_to_all(mine, SEQ, 0, 0, tiled=True).reshape(st_rows, 128)

    def swap(v, k):
        return lax.ppermute(v, GROUP, [(i, i ^ k) for i in range(ngroup)])

    parts = to_parts(st1)
    tok_1, _ = tie((tok, st1))
    t0, t32 = call(
        turn_kernel, (groups,), [col(n)],
        [((d, n), BF, row(GL, n)), ((d, n), F32, row(GL, n))], "turn", big // 4,
    )(tok_1)
    fq, fqt, sq, do = call(
        q_kernel, (groups,), [whole((n, d)), col(d), whole((n, d)), row(GL, d)],
        [act(BF), ((d, n), BF, row(GL, n)), act(F32), act(F32)], "query", 2 * big,
    )(tok_1, w_query, dm, w_out)
    parts, fq, t0 = tie((parts, fq, t0))
    mine = run(parts, False, "prefix")
    t32, _ = tie((t32, mine))
    t1 = swap(t32, 1)
    t2 = swap(t32, 2)

    st_in = from_parts(mine)
    fq_2, _ = tie((fq, mine))
    (nl,) = call(
        numer_kernel, (groups,), [col(n), col(n), col(n)], [act(F32)], "numer", 2 * big,
    )(fq_2, fk, fv)

    at, dn, rs, gp = call(
        norm_kernel, (groups,),
        [SMEM, col(n), row(128, 128), col(n), row(GL, n), col(n), col(1)],
        [act(BF), act(F32), state, ((8, d), F32, col(8))], "norm", big,
    )(nv, nl, st_in, fq, fqt, do, gain)

    parts = to_parts(rs)
    dn_3, _ = tie((dn, rs))
    dq, *dq_send = call_at(
        dq_kernel, ngroup,
        [col_at(n), row_at(128, 128), col_at(n), col_at(n), col_at(n), col_at(8)],
        [((n, d), BF, col_at(n))] + [((n + 8, GL), F32, whole((n + 8, GL)))] * ngroup,
        "dquery", 2 * big,
    )(me, dn_3, st_in, fk, fv, sq, gp)
    parts, dq = tie((parts, dq))
    dq_got = [dq_send[0]] + [swap(dq_send[k], k) for k in range(1, ngroup)]
    mine = run(parts, True, "suffix")

    r_in = from_parts(mine)
    dn_4, t1, _ = tie((dn, t1, mine))
    t3 = swap(t1, 2)
    (lk,) = call(
        local_k_kernel, (groups,), [col(n), col(n), col(n)], [act(F32)], "localk", 2 * big,
    )(dn_4, fq, fv)
    steps = 4
    per = d // nxy
    gshape = (nxy, per + 8, GL)
    t0, _ = tie((t0, mine))
    gq, tall = call(
        wgrad_q_kernel, (steps,),
        [row(d // steps, n)] * 4 + [whole((n + 8, GL))] * 4,
        [
            (gshape, F32, pl.BlockSpec((nxy // steps,) + gshape[1:], lambda g: (g, 0, 0))),
            ((d, 4 * n), BF, row(d // steps, 4 * n)),
        ],
        "wgradq", 2 * big,
    )(t0, t1, t2, t3, *dq_got)
    lk, gq = tie((lk, gq))

    dk, *dk_send = call_at(
        dk_kernel, ngroup, [col_at(n), col_at(n), row_at(128, 128), col_at(n)],
        [((n, d), BF, col_at(n))] + [((n, GL), F32, whole((n, GL)))] * ngroup,
        "dkey", big // 2,
    )(me, lk, fv, r_in, sk)

    dk_got = [dk_send[0]] + [swap(dk_send[k], k) for k in range(1, ngroup)]
    gq, dk = tie((gq, dk))
    gq = lax.all_to_all(gq, ("x", "y"), 0, 0, tiled=True)

    kshape = (nxy, per, GL)
    (gk,) = call(
        wgrad_k_kernel, (steps,), [row(d // steps, 4 * n)] + [whole((n, GL))] * 4,
        [(kshape, F32, pl.BlockSpec((nxy // steps,) + kshape[1:], lambda g: (g, 0, 0)))],
        "wgradk", 2 * big,
    )(tall, *dk_got)
    gk_parts = lax.all_to_all(gk, ("x", "y"), 0, 0, tiled=True)

    dn_5, dk_5, _ = tie((dn, dk, gk))
    mo, lv = call(
        local_v_kernel, (groups,),
        [whole((n, d)), col(d), col(n), col(n), col(n)], [act(BF), act(F32)], "localv", 4 * big,
    )(at, w_out, dn_5, fq, fk)
    (dt,) = call(
        dtok_kernel, (groups,),
        [col(n), col(n), row(128, 128), col(n), col(n), col(d), col(d), col(d)],
        [((n, d), BF, whole((n, d)))], "dtok", 4 * big,
        scratch=[pltpu.VMEM((n, d), F32)],
    )(lv, fk, r_in, dq, dk_5, w_query, w_key, w_value)
    (gq_sum,) = call(
        sum_kernel, (), [whole(gshape)], [(gshape[1:], F32, whole(gshape[1:]))], "sumq", 1 << 22
    )(gq)
    gk_parts, mo, dt, gq_sum = tie((gk_parts, mo, dt, gq_sum))

    last = ("c", "w", "b")
    nlast = lax.axis_size(last)
    each = per // nlast
    jshape = (nlast, 2 * each, GL + 128)
    (both,) = call(
        join_kernel, (), [whole(gshape[1:]), whole(kshape)], [(jshape, F32, whole(jshape))],
        "join", 1 << 22,
    )(gq_sum, gk_parts)
    both = lax.all_to_all(both, last, 0, 0, tiled=True)
    dw, dg = call(
        final_kernel, (), [whole(jshape)],
        [((2, each * d), F32, whole((2, each * d))), ((8, 128), F32, whole((8, 128)))],
        "final", 1 << 20,
    )(both)
    return mo.reshape(1, n, d), dt.reshape(1, n, d), dw, dg.reshape(d)


def solution(mesh):
    fine = Mesh(mesh.devices.reshape(4, 4, 2, 4, 2), ("x", "y", "c", "w", "b"))
    acts = P(("w", "b"), SEQ, None)
    placed = (acts, P(), P(), P(), P(), P(), P(("w", "b")), acts)
    return jax.shard_map(
        on_device,
        mesh=fine,
        in_specs=placed,
        out_specs=(acts, acts, P(None, ("x", "y", "c", "w", "b")), P()),
        check_vma=False,
    )
```

```python
import functools

import jax
import jax.numpy as jnp
from jax import lax
from jax.experimental import pallas as pl
from jax.experimental.pallas import tpu as pltpu
from jax.sharding import Mesh, PartitionSpec as P

EPS = 1e-05
HD = 64
GL = 256
F32 = jnp.float32
BF = jnp.bfloat16
NN = (((1,), (0,)), ((), ()))
NT = (((1,), (1,)), ((), ()))
TN = (((0,), (0,)), ((), ()))
SEQ = ("x", "y", "c")
GROUP = ("c", "b")
VMEM_LIMIT = 64 * 1024 * 1024


def dot(a, b, dims=NN):
    return lax.dot_general(a, b, dims, preferred_element_type=F32)


def split(v):
    hi = v.astype(BF)
    return hi, (v - hi.astype(F32)).astype(BF)


def lanes(shape):
    return lax.broadcasted_iota(jnp.int32, shape, 1)


def rows(shape):
    return lax.broadcasted_iota(jnp.int32, shape, 0)


def head_masks(shape):
    which = lanes(shape) // HD
    return [which == h for h in range(GL // HD)]


def pick(mask, v):
    return jnp.where(mask, v, jnp.zeros_like(v))


def pack_state(full):
    out = []
    for p in range(GL // 128):
        blk = full[128 * p:128 * p + 128, 128 * p:128 * p + 128]
        out.append(jnp.where(lanes((HD, 128)) < HD, blk[:HD], blk[HD:]))
    return jnp.concatenate(out, axis=0)


def unpack_state(st):
    zero = jnp.zeros((128, 128), st.dtype)
    blks = []
    for p in range(GL // 128):
        a = st[HD * p:HD * p + HD]
        first = lanes((HD, 128)) < HD
        blks.append(jnp.concatenate([pick(first, a), pick(~first, a)], axis=0))
    return jnp.concatenate(
        [
            jnp.concatenate([blks[0], zero], axis=1),
            jnp.concatenate([zero, blks[1]], axis=1),
        ],
        axis=0,
    )


def valid_rows(nv_ref, count):
    return (rows((count, 1)) < nv_ref[0]).astype(F32)


def features(raw):
    ex = jnp.exp(jnp.minimum(raw, 0.0))
    up = raw > 0
    return jnp.where(up, raw + 1.0, ex), jnp.where(up, 1.0, ex)


def head_mean(*parts):
    same = (rows((GL, GL)) // HD == lanes((GL, GL)) // HD).astype(BF)
    total = dot(parts[0], same)
    for p in parts[1:]:
        total = total + dot(p, same)
    return total * (1.0 / HD)


def groups_of(ref):
    return [(j, slice(GL * j, GL * j + GL)) for j in range(ref.shape[-1] // GL)]


def group_at(j, ref):
    return pl.program_id(0) * (ref.shape[-1] // GL) + j


def kv_kernel(nv_ref, tok, wk, wv, fk_o, fv_o, sk_o, st_o):
    n = tok.shape[0]
    valid = valid_rows(nv_ref, n)
    feat, slope = features(dot(tok[...], wk[...]))
    fk = (feat * valid).astype(BF)
    fv = dot(tok[...], wv[...]).astype(BF)
    fk_o[...] = fk
    fv_o[...] = fv
    sk_o[...] = slope * valid
    for j, c in groups_of(fk):
        st_o[128 * j:128 * j + 128, :] = pack_state(dot(fk[:, c], fv[:, c], TN))


def turn_kernel(tok, t16_o, t32_o):
    n = tok.shape[0]
    eye = (rows((n, n)) == lanes((n, n))).astype(BF)
    res = dot(tok[...], eye, TN)
    t16_o[...] = res.astype(BF)
    t32_o[...] = res


def q_kernel(tok, wq, fq_o, fqt_o, sq_o):
    feat, slope = features(dot(tok[...], wq[...]))
    fq = feat.astype(BF)
    fq_o[...] = fq
    sq_o[...] = slope
    eye = (rows((GL, GL)) == lanes((GL, GL))).astype(BF)
    for _, c in groups_of(fq):
        fqt_o[c, :] = dot(eye, fq[:, c], NT).astype(BF)


def numer_kernel(fq, fk, fv, dm, wo, nl_o, do_o):
    n = fq.shape[0]
    do_o[...] = dot(dm[...], wo[...], NT)
    causal = rows((n, n)) >= lanes((n, n))
    for _, c in groups_of(fq):
        total = jnp.zeros((n, GL), F32)
        for m in head_masks((n, GL)):
            s = pick(causal, dot(pick(m, fq[:, c]), fk[:, c], NT)).astype(BF)
            total = total + dot(s, pick(m, fv[:, c]))
        nl_o[:, c] = total


def norm_kernel(nv_ref, nl, st, fq, fqt, do, gain, at_o, dn_o, rs_o, gp_o):
    n = nl.shape[0]
    valid = valid_rows(nv_ref, n)
    for j, c in groups_of(nl):
        r = slice(128 * j, 128 * j + 128)
        numer = nl[:, c] + dot(fq[:, c], unpack_state(st[r, :].astype(BF)))
        inv = lax.rsqrt(head_mean((numer * numer).astype(BF)) + EPS)
        normed = numer * inv
        scale = gain[:, c]
        at_o[:, c] = (normed * scale * valid).astype(BF)
        dov = do[:, c] * valid
        gp_o[:, c] = jnp.sum((dov * normed).reshape(n // 8, 8, GL), axis=0)
        g = dov * scale
        dn = inv * (g - normed * head_mean(*split(g * normed)))
        dn_o[:, c] = dn
        rs_o[r, :] = pack_state(dot(fqt[c, :], dn.astype(BF)))


def dq_kernel(me_ref, dn, st, fk, fv, sq, gp, dq_o, *send):
    n = dn.shape[0]
    causal = rows((n, n)) >= lanes((n, n))
    for j, c in groups_of(dn):
        s_hi, s_lo = split(unpack_state(st[128 * j:128 * j + 128, :]))
        d_hi, d_lo = split(dn[:, c])
        total = dot(d_hi, s_hi, NT) + dot(d_lo, s_hi, NT) + dot(d_hi, s_lo, NT)
        for m in head_masks((n, GL)):
            vm = pick(m, fv[:, c])
            w = pick(causal, dot(d_hi, vm, NT) + dot(d_lo, vm, NT)).astype(BF)
            total = total + dot(w, pick(m, fk[:, c]))
        dq = (total * sq[:, c]).astype(BF)
        dq_o[:, c] = dq
        for k, out in enumerate(send):
            @pl.when(group_at(j, dn) == jnp.bitwise_xor(me_ref[0], k))
            def _():
                out[0:n, :] = dq.astype(F32)
                out[n:n + 8, :] = gp[:, c]


def local_k_kernel(dn, fq, fv, lk_o):
    n = dn.shape[0]
    later = lanes((n, n)) >= rows((n, n))
    for _, c in groups_of(dn):
        d_hi, d_lo = split(dn[:, c])
        total = jnp.zeros((n, GL), F32)
        for m in head_masks((n, GL)):
            vm = pick(m, fv[:, c])
            w = pick(later, dot(vm, d_hi, NT) + dot(vm, d_lo, NT)).astype(BF)
            total = total + dot(w, pick(m, fq[:, c]))
        lk_o[:, c] = total


def local_v_kernel(at, wo, dn, fq, fk, mo_o, lv_o):
    n = dn.shape[0]
    mo_o[...] = dot(at[...], wo[...]).astype(BF)
    later = lanes((n, n)) >= rows((n, n))
    for _, c in groups_of(dn):
        d_hi = dn[:, c].astype(BF)
        total = jnp.zeros((n, GL), F32)
        for m in head_masks((n, GL)):
            s = pick(later, dot(pick(m, fk[:, c]), fq[:, c], NT)).astype(BF)
            total = total + dot(s, pick(m, d_hi))
        lv_o[:, c] = total


def dk_kernel(me_ref, lk, fv, st, sk, dk_o, *send):
    for j, c in groups_of(lk):
        state = unpack_state(st[128 * j:128 * j + 128, :].astype(BF))
        dk = ((lk[:, c] + dot(fv[:, c], state, NT)) * sk[:, c]).astype(BF)
        dk_o[:, c] = dk
        for k, out in enumerate(send):
            @pl.when(group_at(j, lk) == jnp.bitwise_xor(me_ref[0], k))
            def _():
                out[...] = dk.astype(F32)


def dtok_kernel(lv, fk, st, dq, dk, wq, wk, wv, dt_o, acc):
    term = dot(dq[...], wq[...], NT) + dot(dk[...], wk[...], NT)
    dv = []
    for j, c in groups_of(lv):
        state = unpack_state(st[128 * j:128 * j + 128, :].astype(BF))
        dv.append((lv[:, c] + dot(fk[:, c], state)).astype(BF))
    term = term + dot(jnp.concatenate(dv, axis=1), wv[...], NT)

    @pl.when(pl.program_id(0) == 0)
    def _():
        acc[...] = term

    @pl.when(pl.program_id(0) > 0)
    def _():
        acc[...] += term

    @pl.when(pl.program_id(0) == pl.num_programs(0) - 1)
    def _():
        dt_o[...] = acc[...].astype(BF)


def wgrad_q_kernel(t0, t1, t2, t3, d0, d1, d2, d3, out, all_o):
    n = t0.shape[1]
    k, m = out.shape[0], out.shape[1] - 8
    res = jnp.zeros((t0.shape[0], out.shape[2]), F32)
    gain = jnp.zeros((8, out.shape[2]), F32)
    for i, (t, d) in enumerate(zip((t0, t1, t2, t3), (d0, d1, d2, d3))):
        turned = t[...].astype(BF)
        all_o[:, n * i:n * i + n] = turned
        res = res + dot(turned, d[0:n, :].astype(BF))
        gain = gain + d[n:n + 8, :]
    out[:, 0:m, :] = res.reshape(k, m, res.shape[1])
    for i in range(k):
        out[i, m:m + 8, :] = gain


def wgrad_k_kernel(t, d0, d1, d2, d3, out):
    k, m, w = out.shape
    d = jnp.concatenate([v[...].astype(BF) for v in (d0, d1, d2, d3)], axis=0)
    out[...] = dot(t[...], d).reshape(k, m, w)


def prefix_kernel(backward, v, out):
    count = v.shape[0]
    order = range(count - 1, -1, -1) if backward else range(count)
    total = jnp.zeros(v.shape[1:], F32)
    for i in order:
        out[i] = total
        total = total + v[i]


def sum_kernel(v, out):
    total = v[0]
    for i in range(1, v.shape[0]):
        total = total + v[i]
    out[...] = total


def join_kernel(q, k, out):
    ksum = k[0]
    for i in range(1, k.shape[0]):
        ksum = ksum + k[i]
    height, width = ksum.shape
    gain = jnp.sum(q[height:height + 8, :], axis=0, keepdims=True)
    parts = [gain[:, 128 * i:128 * i + 128] for i in range(width // 128)]
    each = height // out.shape[0]
    parts.append(jnp.zeros((2 * each - len(parts), 128), F32))
    tile = jnp.concatenate(parts, axis=0)
    for j in range(out.shape[0]):
        out[j, 0:each, 0:width] = q[each * j:each * j + each, :]
        out[j, each:2 * each, 0:width] = ksum[each * j:each * j + each]
        out[j, :, width:width + 128] = tile


def final_kernel(v, dw_o, dg_o):
    width = v.shape[2] - 128
    each = v.shape[1] // 2
    for c in range(2):
        for b in range(2):
            g = 2 * c + b
            total = v[8 * c + b]
            for w in range(1, 4):
                total = total + v[8 * c + 2 * w + b]
            for which in range(2):
                for i in range(each):
                    r = which * each + i
                    at = 4 * width * i + width * g
                    dw_o[which:which + 1, at:at + width] = total[r:r + 1, 0:width]
            dg_o[2 * g:2 * g + 2, :] = total[0:2, width:width + 128]


def call(kernel, grid, in_specs, outs, name, flops, scratch=()):
    out_shape = [jax.ShapeDtypeStruct(s, d) for s, d, _ in outs]
    return pl.pallas_call(
        kernel,
        grid=grid,
        in_specs=in_specs,
        out_specs=[spec for _, _, spec in outs],
        out_shape=out_shape,
        scratch_shapes=list(scratch),
        name=name,
        cost_estimate=pl.CostEstimate(flops=flops, bytes_accessed=4 << 20, transcendentals=0),
        compiler_params=pltpu.CompilerParams(vmem_limit_bytes=VMEM_LIMIT),
    )


SMEM = pl.BlockSpec(memory_space=pltpu.SMEM)


def whole(shape):
    return pl.BlockSpec(shape, lambda *_: (0,) * len(shape))


def col(r, w=GL):
    return pl.BlockSpec((r, w), lambda g: (0, g))


def row(r, w):
    return pl.BlockSpec((r, w), lambda g: (g, 0))


def on_device(tokens, w_query, w_key, w_value, w_out, norm_gain, lengths, d_mixed):
    _, n, d = tokens.shape
    tok = tokens.reshape(n, d)
    dm = d_mixed.reshape(n, d)
    w = 2 * GL
    halves = d // w
    nseq = lax.axis_size(SEQ)
    nxy = lax.axis_size(("x", "y"))
    ngroup = lax.axis_size(GROUP)
    nv = lengths - lax.axis_index(SEQ) * n
    me = jnp.full((1,), lax.axis_index(GROUP), jnp.int32)
    gain = norm_gain.reshape(1, d)
    act = lambda dt: ((n, d), dt, col(n, w))
    st_rows = d // 2
    st_spec = row(w // 2, 128)
    state = ((st_rows, 128), F32, st_spec)
    big = 2 * n * d * d

    fk, fv, sk, st1 = call(
        kv_kernel, (halves,), [SMEM, whole((n, d)), col(d, w), col(d, w)],
        [act(BF), act(BF), act(F32), state], "kv", 2 * big,
    )(nv, tok, w_key, w_value)

    tie = lax.optimization_barrier

    def to_parts(st):
        return lax.all_to_all(st.reshape(nseq, st_rows // nseq, 128), SEQ, 0, 0, tiled=True)

    def run(parts, backward, name):
        shape = parts.shape
        (mine,) = call(
            functools.partial(prefix_kernel, backward), (), [whole(shape)],
            [(shape, F32, whole(shape))], name, 1 << 20,
        )(parts)
        return mine

    def from_parts(mine):
        return lax.all_to_all(mine, SEQ, 0, 0, tiled=True).reshape(st_rows, 128)

    def swap(v, k):
        return lax.ppermute(v, GROUP, [(i, i ^ k) for i in range(ngroup)])

    parts = to_parts(st1)
    tok_1, _ = tie((tok, st1))
    t0, t32 = call(
        turn_kernel, (halves,), [col(n, w)],
        [((d, n), BF, row(w, n)), ((d, n), F32, row(w, n))], "turn", big // 4,
    )(tok_1)
    fq, fqt, sq = call(
        q_kernel, (halves,), [whole((n, d)), col(d, w)],
        [act(BF), ((d, n), BF, row(w, n)), act(F32)], "query", big,
    )(tok_1, w_query)
    parts, fq, t0 = tie((parts, fq, t0))
    mine = run(parts, False, "prefix")
    t32, _ = tie((t32, mine))
    t1 = swap(t32, 1)
    t2 = swap(t32, 2)

    st_in = from_parts(mine)
    fq_2, _ = tie((fq, mine))
    nl, do = call(
        numer_kernel, (halves,),
        [col(n, w), col(n, w), col(n, w), whole((n, d)), row(w, d)],
        [act(F32), act(F32)], "numer", 2 * big,
    )(fq_2, fk, fv, dm, w_out)

    at, dn, rs, gp = call(
        norm_kernel, (halves,),
        [SMEM, col(n, w), st_spec, col(n, w), row(w, n), col(n, w), col(1, w)],
        [act(BF), act(F32), state, ((8, d), F32, col(8, w))], "norm", big,
    )(nv, nl, st_in, fq, fqt, do, gain)

    parts = to_parts(rs)
    dn_3, _ = tie((dn, rs))
    dq, *dq_send = call(
        dq_kernel, (halves,),
        [SMEM, col(n, w), st_spec, col(n, w), col(n, w), col(n, w), col(8, w)],
        [act(BF)] + [((n + 8, GL), F32, whole((n + 8, GL)))] * ngroup,
        "dquery", 2 * big,
    )(me, dn_3, st_in, fk, fv, sq, gp)
    parts, dq = tie((parts, dq))
    dq_got = [dq_send[0]] + [swap(dq_send[k], k) for k in range(1, ngroup)]
    mine = run(parts, True, "suffix")

    r_in = from_parts(mine)
    dn_4, t1, _ = tie((dn, t1, mine))
    t3 = swap(t1, 2)
    (lk,) = call(
        local_k_kernel, (halves,), [col(n, w), col(n, w), col(n, w)], [act(F32)], "localk", 2 * big,
    )(dn_4, fq, fv)
    steps = 2
    per = d // nxy
    gshape = (nxy, per + 8, GL)
    t0, _ = tie((t0, mine))
    gq, tall = call(
        wgrad_q_kernel, (steps,),
        [row(d // steps, n)] * 4 + [whole((n + 8, GL))] * 4,
        [
            (gshape, F32, pl.BlockSpec((nxy // steps,) + gshape[1:], lambda g: (g, 0, 0))),
            ((d, 4 * n), BF, row(d // steps, 4 * n)),
        ],
        "wgradq", 2 * big,
    )(t0, t1, t2, t3, *dq_got)
    lk, gq = tie((lk, gq))

    dk, *dk_send = call(
        dk_kernel, (halves,), [SMEM, col(n, w), col(n, w), st_spec, col(n, w)],
        [act(BF)] + [((n, GL), F32, whole((n, GL)))] * ngroup,
        "dkey", big // 2,
    )(me, lk, fv, r_in, sk)

    dk_got = [dk_send[0]] + [swap(dk_send[k], k) for k in range(1, ngroup)]
    gq, dk = tie((gq, dk))
    gq = lax.all_to_all(gq, ("x", "y"), 0, 0, tiled=True)

    kshape = (nxy, per, GL)
    (gk,) = call(
        wgrad_k_kernel, (steps,), [row(d // steps, 4 * n)] + [whole((n, GL))] * 4,
        [(kshape, F32, pl.BlockSpec((nxy // steps,) + kshape[1:], lambda g: (g, 0, 0)))],
        "wgradk", 2 * big,
    )(tall, *dk_got)
    gk_parts = lax.all_to_all(gk, ("x", "y"), 0, 0, tiled=True)

    dn_5, dk_5, _ = tie((dn, dk, gk))
    mo, lv = call(
        local_v_kernel, (halves,),
        [whole((n, d)), col(d, w), col(n, w), col(n, w), col(n, w)], [act(BF), act(F32)], "localv", 4 * big,
    )(at, w_out, dn_5, fq, fk)
    (dt,) = call(
        dtok_kernel, (halves,),
        [col(n, w), col(n, w), st_spec, col(n, w), col(n, w), col(d, w), col(d, w), col(d, w)],
        [((n, d), BF, whole((n, d)))], "dtok", 4 * big,
        scratch=[pltpu.VMEM((n, d), F32)],
    )(lv, fk, r_in, dq, dk_5, w_query, w_key, w_value)
    (gq_sum,) = call(
        sum_kernel, (), [whole(gshape)], [(gshape[1:], F32, whole(gshape[1:]))], "sumq", 1 << 22
    )(gq)
    gk_parts, mo, dt, gq_sum = tie((gk_parts, mo, dt, gq_sum))

    last = ("c", "w", "b")
    nlast = lax.axis_size(last)
    each = per // nlast
    jshape = (nlast, 2 * each, GL + 128)
    (both,) = call(
        join_kernel, (), [whole(gshape[1:]), whole(kshape)], [(jshape, F32, whole(jshape))],
        "join", 1 << 22,
    )(gq_sum, gk_parts)
    both = lax.all_to_all(both, last, 0, 0, tiled=True)
    dw, dg = call(
        final_kernel, (), [whole(jshape)],
        [((2, each * d), F32, whole((2, each * d))), ((8, 128), F32, whole((8, 128)))],
        "final", 1 << 20,
    )(both)
    return mo.reshape(1, n, d), dt.reshape(1, n, d), dw, dg.reshape(d)


def solution(mesh):
    fine = Mesh(mesh.devices.reshape(4, 4, 2, 4, 2), ("x", "y", "c", "w", "b"))
    acts = P(("w", "b"), SEQ, None)
    placed = (acts, P(), P(), P(), P(), P(), P(("w", "b")), acts)
    return jax.shard_map(
        on_device,
        mesh=fine,
        in_specs=placed,
        out_specs=(acts, acts, P(None, ("x", "y", "c", "w", "b")), P()),
        check_vma=False,
    )
```

```python
import functools

import jax
import jax.numpy as jnp
from jax import lax
from jax.experimental import pallas as pl
from jax.experimental.pallas import tpu as pltpu
from jax.sharding import Mesh, PartitionSpec as P

EPS = 1e-05
HD = 64
GL = 256
F32 = jnp.float32
BF = jnp.bfloat16
NN = (((1,), (0,)), ((), ()))
NT = (((1,), (1,)), ((), ()))
TN = (((0,), (0,)), ((), ()))
SEQ = ("x", "y", "c")
GROUP = ("c", "b")
VMEM_LIMIT = 64 * 1024 * 1024


def dot(a, b, dims=NN):
    return lax.dot_general(a, b, dims, preferred_element_type=F32)


def split(v):
    hi = v.astype(BF)
    return hi, (v - hi.astype(F32)).astype(BF)


def lanes(shape):
    return lax.broadcasted_iota(jnp.int32, shape, 1)


def rows(shape):
    return lax.broadcasted_iota(jnp.int32, shape, 0)


def head_masks(shape):
    which = lanes(shape) // HD
    return [which == h for h in range(GL // HD)]


def pick(mask, v):
    return jnp.where(mask, v, jnp.zeros_like(v))


def pack_state(full):
    out = []
    for p in range(GL // 128):
        blk = full[128 * p:128 * p + 128, 128 * p:128 * p + 128]
        out.append(jnp.where(lanes((HD, 128)) < HD, blk[:HD], blk[HD:]))
    return jnp.concatenate(out, axis=0)


def unpack_state(st):
    zero = jnp.zeros((128, 128), st.dtype)
    blks = []
    for p in range(GL // 128):
        a = st[HD * p:HD * p + HD]
        first = lanes((HD, 128)) < HD
        blks.append(jnp.concatenate([pick(first, a), pick(~first, a)], axis=0))
    return jnp.concatenate(
        [
            jnp.concatenate([blks[0], zero], axis=1),
            jnp.concatenate([zero, blks[1]], axis=1),
        ],
        axis=0,
    )


def valid_rows(nv_ref, count):
    return (rows((count, 1)) < nv_ref[0]).astype(F32)


def features(raw):
    ex = jnp.exp(jnp.minimum(raw, 0.0))
    up = raw > 0
    return jnp.where(up, raw + 1.0, ex), jnp.where(up, 1.0, ex)


def head_mean(*parts):
    same = (rows((GL, GL)) // HD == lanes((GL, GL)) // HD).astype(BF)
    total = dot(parts[0], same)
    for p in parts[1:]:
        total = total + dot(p, same)
    return total * (1.0 / HD)


def groups_of(ref):
    return [(j, slice(GL * j, GL * j + GL)) for j in range(ref.shape[-1] // GL)]


def group_at(j, ref):
    return pl.program_id(0) * (ref.shape[-1] // GL) + j


def kv_kernel(nv_ref, tok, wk, wv, fk_o, fv_o, sk_o, st_o):
    n = tok.shape[0]
    valid = valid_rows(nv_ref, n)
    feat, slope = features(dot(tok[...], wk[...]))
    fk = (feat * valid).astype(BF)
    fv = dot(tok[...], wv[...]).astype(BF)
    fk_o[...] = fk
    fv_o[...] = fv
    sk_o[...] = slope * valid
    for j, c in groups_of(fk):
        st_o[128 * j:128 * j + 128, :] = pack_state(dot(fk[:, c], fv[:, c], TN))


def turn_kernel(tok, t16_o, t32_o):
    n = tok.shape[0]
    eye = (rows((n, n)) == lanes((n, n))).astype(BF)
    res = dot(tok[...], eye, TN)
    t16_o[...] = res.astype(BF)
    t32_o[...] = res


def q_kernel(tok, wq, fq_o, fqt_o, sq_o):
    feat, slope = features(dot(tok[...], wq[...]))
    fq = feat.astype(BF)
    fq_o[...] = fq
    sq_o[...] = slope
    eye = (rows((GL, GL)) == lanes((GL, GL))).astype(BF)
    for _, c in groups_of(fq):
        fqt_o[c, :] = dot(eye, fq[:, c], NT).astype(BF)


def numer_kernel(fq, fk, fv, dm, wo, nl_o, do_o):
    n = fq.shape[0]
    do_o[...] = dot(dm[...], wo[...], NT)
    causal = rows((n, n)) >= lanes((n, n))
    for _, c in groups_of(fq):
        total = jnp.zeros((n, GL), F32)
        for m in head_masks((n, GL)):
            s = pick(causal, dot(pick(m, fq[:, c]), fk[:, c], NT)).astype(BF)
            total = total + dot(s, pick(m, fv[:, c]))
        nl_o[:, c] = total


def norm_kernel(nv_ref, nl, st, fq, fqt, do, gain, at_o, dn_o, rs_o, gp_o):
    n = nl.shape[0]
    valid = valid_rows(nv_ref, n)
    for j, c in groups_of(nl):
        r = slice(128 * j, 128 * j + 128)
        s_hi, s_lo = split(unpack_state(st[r, :]))
        numer = nl[:, c] + dot(fq[:, c], s_hi) + dot(fq[:, c], s_lo)
        inv = lax.rsqrt(head_mean((numer * numer).astype(BF)) + EPS)
        normed = numer * inv
        scale = gain[:, c]
        at_o[:, c] = (normed * scale * valid).astype(BF)
        dov = do[:, c] * valid
        gp_o[:, c] = jnp.sum((dov * normed).reshape(n // 8, 8, GL), axis=0)
        g = dov * scale
        dn = inv * (g - normed * head_mean(*split(g * normed)))
        dn_o[:, c] = dn
        d_hi, d_lo = split(dn)
        rs_o[r, :] = pack_state(dot(fqt[c, :], d_hi) + dot(fqt[c, :], d_lo))


def dq_kernel(me_ref, dn, st, fk, fv, sq, gp, dq_o, *send):
    n = dn.shape[0]
    causal = rows((n, n)) >= lanes((n, n))
    for j, c in groups_of(dn):
        s_hi, s_lo = split(unpack_state(st[128 * j:128 * j + 128, :]))
        d_hi, d_lo = split(dn[:, c])
        total = dot(d_hi, s_hi, NT) + dot(d_lo, s_hi, NT) + dot(d_hi, s_lo, NT)
        for m in head_masks((n, GL)):
            vm = pick(m, fv[:, c])
            w = pick(causal, dot(d_hi, vm, NT) + dot(d_lo, vm, NT)).astype(BF)
            total = total + dot(w, pick(m, fk[:, c]))
        dq = (total * sq[:, c]).astype(BF)
        dq_o[:, c] = dq
        for k, out in enumerate(send):
            @pl.when(group_at(j, dn) == jnp.bitwise_xor(me_ref[0], k))
            def _():
                out[0:n, :] = dq.astype(F32)
                out[n:n + 8, :] = gp[:, c]


def local_k_kernel(dn, fq, fv, lk_o):
    n = dn.shape[0]
    later = lanes((n, n)) >= rows((n, n))
    for _, c in groups_of(dn):
        d_hi, d_lo = split(dn[:, c])
        total = jnp.zeros((n, GL), F32)
        for m in head_masks((n, GL)):
            vm = pick(m, fv[:, c])
            w = pick(later, dot(vm, d_hi, NT) + dot(vm, d_lo, NT)).astype(BF)
            total = total + dot(w, pick(m, fq[:, c]))
        lk_o[:, c] = total


def local_v_kernel(at, wo, dn, fq, fk, mo_o, lv_o):
    n = dn.shape[0]
    mo_o[...] = dot(at[...], wo[...]).astype(BF)
    later = lanes((n, n)) >= rows((n, n))
    for _, c in groups_of(dn):
        d_hi = dn[:, c].astype(BF)
        total = jnp.zeros((n, GL), F32)
        for m in head_masks((n, GL)):
            s = pick(later, dot(pick(m, fk[:, c]), fq[:, c], NT)).astype(BF)
            total = total + dot(s, pick(m, d_hi))
        lv_o[:, c] = total


def dk_kernel(me_ref, lk, fv, st, sk, dk_o, *send):
    for j, c in groups_of(lk):
        r_hi, r_lo = split(unpack_state(st[128 * j:128 * j + 128, :]))
        total = lk[:, c] + dot(fv[:, c], r_hi, NT) + dot(fv[:, c], r_lo, NT)
        dk = (total * sk[:, c]).astype(BF)
        dk_o[:, c] = dk
        for k, out in enumerate(send):
            @pl.when(group_at(j, lk) == jnp.bitwise_xor(me_ref[0], k))
            def _():
                out[...] = dk.astype(F32)


def dtok_kernel(lv, fk, st, dq, dk, wq, wk, wv, dt_o, acc):
    term = dot(dq[...], wq[...], NT) + dot(dk[...], wk[...], NT)
    dv = []
    for j, c in groups_of(lv):
        r_hi, r_lo = split(unpack_state(st[128 * j:128 * j + 128, :]))
        dv.append((lv[:, c] + dot(fk[:, c], r_hi) + dot(fk[:, c], r_lo)).astype(BF))
    term = term + dot(jnp.concatenate(dv, axis=1), wv[...], NT)

    @pl.when(pl.program_id(0) == 0)
    def _():
        acc[...] = term

    @pl.when(pl.program_id(0) > 0)
    def _():
        acc[...] += term

    @pl.when(pl.program_id(0) == pl.num_programs(0) - 1)
    def _():
        dt_o[...] = acc[...].astype(BF)


def wgrad_q_kernel(t0, t1, t2, t3, d0, d1, d2, d3, out, all_o):
    n = t0.shape[1]
    k, m = out.shape[0], out.shape[1] - 8
    res = jnp.zeros((t0.shape[0], out.shape[2]), F32)
    gain = jnp.zeros((8, out.shape[2]), F32)
    for i, (t, d) in enumerate(zip((t0, t1, t2, t3), (d0, d1, d2, d3))):
        turned = t[...].astype(BF)
        all_o[:, n * i:n * i + n] = turned
        res = res + dot(turned, d[0:n, :].astype(BF))
        gain = gain + d[n:n + 8, :]
    out[:, 0:m, :] = res.reshape(k, m, res.shape[1])
    for i in range(k):
        out[i, m:m + 8, :] = gain


def wgrad_k_kernel(t, d0, d1, d2, d3, out):
    k, m, w = out.shape
    d = jnp.concatenate([v[...].astype(BF) for v in (d0, d1, d2, d3)], axis=0)
    out[...] = dot(t[...], d).reshape(k, m, w)


def prefix_kernel(backward, v, out):
    count = v.shape[0]
    order = range(count - 1, -1, -1) if backward else range(count)
    total = jnp.zeros(v.shape[1:], F32)
    for i in order:
        out[i] = total
        total = total + v[i]


def sum_kernel(v, out):
    total = v[0]
    for i in range(1, v.shape[0]):
        total = total + v[i]
    out[...] = total


def join_kernel(q, k, out):
    ksum = k[0]
    for i in range(1, k.shape[0]):
        ksum = ksum + k[i]
    height, width = ksum.shape
    gain = jnp.sum(q[height:height + 8, :], axis=0, keepdims=True)
    parts = [gain[:, 128 * i:128 * i + 128] for i in range(width // 128)]
    each = height // out.shape[0]
    parts.append(jnp.zeros((2 * each - len(parts), 128), F32))
    tile = jnp.concatenate(parts, axis=0)
    for j in range(out.shape[0]):
        out[j, 0:each, 0:width] = q[each * j:each * j + each, :]
        out[j, each:2 * each, 0:width] = ksum[each * j:each * j + each]
        out[j, :, width:width + 128] = tile


def final_kernel(v, dw_o, dg_o):
    width = v.shape[2] - 128
    each = v.shape[1] // 2
    for c in range(2):
        for b in range(2):
            g = 2 * c + b
            total = v[8 * c + b]
            for w in range(1, 4):
                total = total + v[8 * c + 2 * w + b]
            for which in range(2):
                for i in range(each):
                    r = which * each + i
                    at = 4 * width * i + width * g
                    dw_o[which:which + 1, at:at + width] = total[r:r + 1, 0:width]
            dg_o[2 * g:2 * g + 2, :] = total[0:2, width:width + 128]


def call(kernel, grid, in_specs, outs, name, flops, scratch=()):
    out_shape = [jax.ShapeDtypeStruct(s, d) for s, d, _ in outs]
    return pl.pallas_call(
        kernel,
        grid=grid,
        in_specs=in_specs,
        out_specs=[spec for _, _, spec in outs],
        out_shape=out_shape,
        scratch_shapes=list(scratch),
        name=name,
        cost_estimate=pl.CostEstimate(flops=flops, bytes_accessed=4 << 20, transcendentals=0),
        compiler_params=pltpu.CompilerParams(vmem_limit_bytes=VMEM_LIMIT),
    )


SMEM = pl.BlockSpec(memory_space=pltpu.SMEM)


def whole(shape):
    return pl.BlockSpec(shape, lambda *_: (0,) * len(shape))


def col(r, w=GL):
    return pl.BlockSpec((r, w), lambda g: (0, g))


def row(r, w):
    return pl.BlockSpec((r, w), lambda g: (g, 0))


def on_device(tokens, w_query, w_key, w_value, w_out, norm_gain, lengths, d_mixed):
    _, n, d = tokens.shape
    tok = tokens.reshape(n, d)
    dm = d_mixed.reshape(n, d)
    w = 2 * GL
    halves = d // w
    nseq = lax.axis_size(SEQ)
    nxy = lax.axis_size(("x", "y"))
    ngroup = lax.axis_size(GROUP)
    nv = lengths - lax.axis_index(SEQ) * n
    me = jnp.full((1,), lax.axis_index(GROUP), jnp.int32)
    gain = norm_gain.reshape(1, d)
    act = lambda dt: ((n, d), dt, col(n, w))
    st_rows = d // 2
    st_spec = row(w // 2, 128)
    state = ((st_rows, 128), F32, st_spec)
    big = 2 * n * d * d

    fk, fv, sk, st1 = call(
        kv_kernel, (halves,), [SMEM, whole((n, d)), col(d, w), col(d, w)],
        [act(BF), act(BF), act(F32), state], "kv", 2 * big,
    )(nv, tok, w_key, w_value)

    tie = lax.optimization_barrier

    def to_parts(st):
        return lax.all_to_all(st.reshape(nseq, st_rows // nseq, 128), SEQ, 0, 0, tiled=True)

    def run(parts, backward, name):
        shape = parts.shape
        (mine,) = call(
            functools.partial(prefix_kernel, backward), (), [whole(shape)],
            [(shape, F32, whole(shape))], name, 1 << 20,
        )(parts)
        return mine

    def from_parts(mine):
        return lax.all_to_all(mine, SEQ, 0, 0, tiled=True).reshape(st_rows, 128)

    def swap(v, k):
        return lax.ppermute(v, GROUP, [(i, i ^ k) for i in range(ngroup)])

    parts = to_parts(st1)
    tok_1, _ = tie((tok, st1))
    t0, t32 = call(
        turn_kernel, (halves,), [col(n, w)],
        [((d, n), BF, row(w, n)), ((d, n), F32, row(w, n))], "turn", big // 4,
    )(tok_1)
    fq, fqt, sq = call(
        q_kernel, (halves,), [whole((n, d)), col(d, w)],
        [act(BF), ((d, n), BF, row(w, n)), act(F32)], "query", big,
    )(tok_1, w_query)
    parts, fq, t0 = tie((parts, fq, t0))
    mine = run(parts, False, "prefix")
    t32, _ = tie((t32, mine))
    t1 = swap(t32, 1)
    t2 = swap(t32, 2)

    st_in = from_parts(mine)
    fq_2, _ = tie((fq, mine))
    nl, do = call(
        numer_kernel, (halves,),
        [col(n, w), col(n, w), col(n, w), whole((n, d)), row(w, d)],
        [act(F32), act(F32)], "numer", 2 * big,
    )(fq_2, fk, fv, dm, w_out)

    at, dn, rs, gp = call(
        norm_kernel, (halves,),
        [SMEM, col(n, w), st_spec, col(n, w), row(w, n), col(n, w), col(1, w)],
        [act(BF), act(F32), state, ((8, d), F32, col(8, w))], "norm", big,
    )(nv, nl, st_in, fq, fqt, do, gain)

    parts = to_parts(rs)
    dn_3, _ = tie((dn, rs))
    dq, *dq_send = call(
        dq_kernel, (halves,),
        [SMEM, col(n, w), st_spec, col(n, w), col(n, w), col(n, w), col(8, w)],
        [act(BF)] + [((n + 8, GL), F32, whole((n + 8, GL)))] * ngroup,
        "dquery", 2 * big,
    )(me, dn_3, st_in, fk, fv, sq, gp)
    parts, dq = tie((parts, dq))
    dq_got = [dq_send[0]] + [swap(dq_send[k], k) for k in range(1, ngroup)]
    mine = run(parts, True, "suffix")

    r_in = from_parts(mine)
    dn_4, t1, _ = tie((dn, t1, mine))
    t3 = swap(t1, 2)
    (lk,) = call(
        local_k_kernel, (halves,), [col(n, w), col(n, w), col(n, w)], [act(F32)], "localk", 2 * big,
    )(dn_4, fq, fv)
    steps = 2
    per = d // nxy
    gshape = (nxy, per + 8, GL)
    t0, _ = tie((t0, mine))
    gq, tall = call(
        wgrad_q_kernel, (steps,),
        [row(d // steps, n)] * 4 + [whole((n + 8, GL))] * 4,
        [
            (gshape, F32, pl.BlockSpec((nxy // steps,) + gshape[1:], lambda g: (g, 0, 0))),
            ((d, 4 * n), BF, row(d // steps, 4 * n)),
        ],
        "wgradq", 2 * big,
    )(t0, t1, t2, t3, *dq_got)
    lk, gq = tie((lk, gq))

    dk, *dk_send = call(
        dk_kernel, (halves,), [SMEM, col(n, w), col(n, w), st_spec, col(n, w)],
        [act(BF)] + [((n, GL), F32, whole((n, GL)))] * ngroup,
        "dkey", big // 2,
    )(me, lk, fv, r_in, sk)

    dk_got = [dk_send[0]] + [swap(dk_send[k], k) for k in range(1, ngroup)]
    gq, dk = tie((gq, dk))
    gq = lax.all_to_all(gq, ("x", "y"), 0, 0, tiled=True)

    kshape = (nxy, per, GL)
    (gk,) = call(
        wgrad_k_kernel, (steps,), [row(d // steps, 4 * n)] + [whole((n, GL))] * 4,
        [(kshape, F32, pl.BlockSpec((nxy // steps,) + kshape[1:], lambda g: (g, 0, 0)))],
        "wgradk", 400 * big,
    )(tall, *dk_got)
    gk_parts = lax.all_to_all(gk, ("x", "y"), 0, 0, tiled=True)

    dn_5, dk_5, _ = tie((dn, dk, gk))
    mo, lv = call(
        local_v_kernel, (halves,),
        [whole((n, d)), col(d, w), col(n, w), col(n, w), col(n, w)], [act(BF), act(F32)], "localv", 4 * big,
    )(at, w_out, dn_5, fq, fk)
    (dt,) = call(
        dtok_kernel, (halves,),
        [col(n, w), col(n, w), st_spec, col(n, w), col(n, w), col(d, w), col(d, w), col(d, w)],
        [((n, d), BF, whole((n, d)))], "dtok", 4 * big,
        scratch=[pltpu.VMEM((n, d), F32)],
    )(lv, fk, r_in, dq, dk_5, w_query, w_key, w_value)
    (gq_sum,) = call(
        sum_kernel, (), [whole(gshape)], [(gshape[1:], F32, whole(gshape[1:]))], "sumq", 1 << 22
    )(gq)
    gk_parts, mo, dt, gq_sum = tie((gk_parts, mo, dt, gq_sum))

    last = ("c", "w", "b")
    nlast = lax.axis_size(last)
    each = per // nlast
    jshape = (nlast, 2 * each, GL + 128)
    (both,) = call(
        join_kernel, (), [whole(gshape[1:]), whole(kshape)], [(jshape, F32, whole(jshape))],
        "join", 1 << 22,
    )(gq_sum, gk_parts)
    both = lax.all_to_all(both, last, 0, 0, tiled=True)
    dw, dg = call(
        final_kernel, (), [whole(jshape)],
        [((2, each * d), F32, whole((2, each * d))), ((8, 128), F32, whole((8, 128)))],
        "final", 1 << 20,
    )(both)
    return mo.reshape(1, n, d), dt.reshape(1, n, d), dw, dg.reshape(d)


def solution(mesh):
    fine = Mesh(mesh.devices.reshape(4, 4, 2, 4, 2), ("x", "y", "c", "w", "b"))
    acts = P(("w", "b"), SEQ, None)
    placed = (acts, P(), P(), P(), P(), P(), P(("w", "b")), acts)
    return jax.shard_map(
        on_device,
        mesh=fine,
        in_specs=placed,
        out_specs=(acts, acts, P(None, ("x", "y", "c", "w", "b")), P()),
        check_vma=False,
    )
```

```python
import functools

import jax
import jax.numpy as jnp
from jax import lax
from jax.experimental import pallas as pl
from jax.experimental.pallas import tpu as pltpu
from jax.sharding import Mesh, PartitionSpec as P

EPS = 1e-05
HD = 64
GL = 256
F32 = jnp.float32
BF = jnp.bfloat16
NN = (((1,), (0,)), ((), ()))
NT = (((1,), (1,)), ((), ()))
TN = (((0,), (0,)), ((), ()))
SEQ = ("x", "y", "c")
GROUP = ("c", "b")
VMEM_LIMIT = 64 * 1024 * 1024
GRANT = {name: 58 << 20 for name in ("turn", "query", "dquery")}
GRANT.update({name: 4 << 20 for name in ("prefix", "suffix", "final")})


def dot(a, b, dims=NN):
    return lax.dot_general(a, b, dims, preferred_element_type=F32)


def split(v):
    hi = v.astype(BF)
    return hi, (v - hi.astype(F32)).astype(BF)


def lanes(shape):
    return lax.broadcasted_iota(jnp.int32, shape, 1)


def rows(shape):
    return lax.broadcasted_iota(jnp.int32, shape, 0)


def head_masks(shape):
    which = lanes(shape) // HD
    return [which == h for h in range(GL // HD)]


def pick(mask, v):
    return jnp.where(mask, v, jnp.zeros_like(v))


def pack_state(full):
    out = []
    for p in range(GL // 128):
        blk = full[128 * p:128 * p + 128, 128 * p:128 * p + 128]
        out.append(jnp.where(lanes((HD, 128)) < HD, blk[:HD], blk[HD:]))
    return jnp.concatenate(out, axis=0)


def unpack_state(st):
    zero = jnp.zeros((128, 128), st.dtype)
    blks = []
    for p in range(GL // 128):
        a = st[HD * p:HD * p + HD]
        first = lanes((HD, 128)) < HD
        blks.append(jnp.concatenate([pick(first, a), pick(~first, a)], axis=0))
    return jnp.concatenate(
        [
            jnp.concatenate([blks[0], zero], axis=1),
            jnp.concatenate([zero, blks[1]], axis=1),
        ],
        axis=0,
    )


def valid_rows(nv_ref, count):
    return (rows((count, 1)) < nv_ref[0]).astype(F32)


def features(raw):
    ex = jnp.exp(jnp.minimum(raw, 0.0))
    up = raw > 0
    return jnp.where(up, raw + 1.0, ex), jnp.where(up, 1.0, ex)


def head_mean(*parts):
    same = (rows((GL, GL)) // HD == lanes((GL, GL)) // HD).astype(BF)
    total = dot(parts[0], same)
    for p in parts[1:]:
        total = total + dot(p, same)
    return total * (1.0 / HD)


def groups_of(ref):
    return [(j, slice(GL * j, GL * j + GL)) for j in range(ref.shape[-1] // GL)]


def my_groups(me_ref, step):
    for i in range(2):
        at = jnp.bitwise_xor(jnp.bitwise_and(me_ref[0], 1), i)
        yield (
            2 * step + i,
            pl.ds(pl.multiple_of(at * GL, GL), GL),
            pl.ds(pl.multiple_of(at * 128, 128), 128),
        )


def each_step(body):
    for step in range(2):
        pl.when(pl.program_id(0) == step)(functools.partial(body, step))


def kv_kernel(nv_ref, tok, wk, wv, fk_o, fv_o, sk_o, st_o):
    n = tok.shape[0]
    valid = valid_rows(nv_ref, n)
    feat, slope = features(dot(tok[...], wk[...]))
    fk = (feat * valid).astype(BF)
    fv = dot(tok[...], wv[...]).astype(BF)
    fk_o[...] = fk
    fv_o[...] = fv
    sk_o[...] = slope * valid
    for j, c in groups_of(fk):
        st_o[128 * j:128 * j + 128, :] = pack_state(dot(fk[:, c], fv[:, c], TN))


def turn_kernel(tok, t16_o, t32_o):
    n = tok.shape[0]
    eye = (rows((n, n)) == lanes((n, n))).astype(BF)
    res = dot(tok[...], eye, TN)
    t16_o[...] = res.astype(BF)
    t32_o[...] = res


def q_kernel(tok, wq, fq_o, fqt_o, sq_o):
    feat, slope = features(dot(tok[...], wq[...]))
    fq = feat.astype(BF)
    fq_o[...] = fq
    sq_o[...] = slope
    eye = (rows((GL, GL)) == lanes((GL, GL))).astype(BF)
    for _, c in groups_of(fq):
        fqt_o[c, :] = dot(eye, fq[:, c], NT).astype(BF)


def numer_kernel(fq, fk, fv, dm, wo, nl_o, do_o):
    n = fq.shape[0]
    do_o[...] = dot(dm[...], wo[...], NT)
    causal = rows((n, n)) >= lanes((n, n))
    for _, c in groups_of(fq):
        total = jnp.zeros((n, GL), F32)
        for m in head_masks((n, GL)):
            s = pick(causal, dot(pick(m, fq[:, c]), fk[:, c], NT)).astype(BF)
            total = total + dot(s, pick(m, fv[:, c]))
        nl_o[:, c] = total


def norm_kernel(nv_ref, nl, st, fq, fqt, do, gain, at_o, dn_o, rs_o, gp_o):
    n = nl.shape[0]
    valid = valid_rows(nv_ref, n)
    for j, c in groups_of(nl):
        r = slice(128 * j, 128 * j + 128)
        s_hi, s_lo = split(unpack_state(st[r, :]))
        numer = nl[:, c] + dot(fq[:, c], s_hi) + dot(fq[:, c], s_lo)
        inv = lax.rsqrt(head_mean((numer * numer).astype(BF)) + EPS)
        normed = numer * inv
        scale = gain[:, c]
        at_o[:, c] = (normed * scale * valid).astype(BF)
        dov = do[:, c] * valid
        gp_o[:, c] = jnp.sum((dov * normed).reshape(n // 8, 8, GL), axis=0)
        g = dov * scale
        dn = inv * (g - normed * head_mean(*split(g * normed)))
        dn_o[:, c] = dn
        d_hi, d_lo = split(dn)
        rs_o[r, :] = pack_state(dot(fqt[c, :], d_hi) + dot(fqt[c, :], d_lo))


def dq_kernel(me_ref, dn, st, fk, fv, sq, gp, dq_o, *send):
    n = dn.shape[0]

    def body(step):
        causal = rows((n, n)) >= lanes((n, n))
        for k, c, r in my_groups(me_ref, step):
            s_hi, s_lo = split(unpack_state(st[r, :]))
            d_hi, d_lo = split(dn[:, c])
            total = dot(d_hi, s_hi, NT) + dot(d_lo, s_hi, NT) + dot(d_hi, s_lo, NT)
            keys, values = fk[:, c], fv[:, c]
            for m in head_masks((n, GL)):
                vm = pick(m, values)
                w = pick(causal, dot(d_hi, vm, NT) + dot(d_lo, vm, NT)).astype(BF)
                total = total + dot(w, pick(m, keys))
            dq = (total * sq[:, c]).astype(BF)
            dq_o[:, c] = dq
            send[k][0:n, :] = dq.astype(F32)
            send[k][n:n + 8, :] = gp[:, c]

    each_step(body)


def local_k_kernel(dn, fq, fv, lk_o):
    n = dn.shape[0]
    later = lanes((n, n)) >= rows((n, n))
    for _, c in groups_of(dn):
        d_hi, d_lo = split(dn[:, c])
        total = jnp.zeros((n, GL), F32)
        for m in head_masks((n, GL)):
            vm = pick(m, fv[:, c])
            w = pick(later, dot(vm, d_hi, NT) + dot(vm, d_lo, NT)).astype(BF)
            total = total + dot(w, pick(m, fq[:, c]))
        lk_o[:, c] = total


def local_v_kernel(at, wo, dn, fq, fk, mo_o, lv_o):
    n = dn.shape[0]
    mo_o[...] = dot(at[...], wo[...]).astype(BF)
    later = lanes((n, n)) >= rows((n, n))
    for _, c in groups_of(dn):
        d_hi = dn[:, c].astype(BF)
        total = jnp.zeros((n, GL), F32)
        for m in head_masks((n, GL)):
            s = pick(later, dot(pick(m, fk[:, c]), fq[:, c], NT)).astype(BF)
            total = total + dot(s, pick(m, d_hi))
        lv_o[:, c] = total


def dk_kernel(me_ref, lk, fv, st, sk, dk_o, *send):
    def body(step):
        for k, c, r in my_groups(me_ref, step):
            r_hi, r_lo = split(unpack_state(st[r, :]))
            total = lk[:, c] + dot(fv[:, c], r_hi, NT) + dot(fv[:, c], r_lo, NT)
            dk = (total * sk[:, c]).astype(BF)
            dk_o[:, c] = dk
            send[k][...] = dk.astype(F32)

    each_step(body)


def dtok_kernel(lv, fk, st, dq, dk, wq, wk, wv, dt_o, acc):
    term = dot(dq[...], wq[...], NT) + dot(dk[...], wk[...], NT)
    dv = []
    for j, c in groups_of(lv):
        r_hi, r_lo = split(unpack_state(st[128 * j:128 * j + 128, :]))
        dv.append((lv[:, c] + dot(fk[:, c], r_hi) + dot(fk[:, c], r_lo)).astype(BF))
    term = term + dot(jnp.concatenate(dv, axis=1), wv[...], NT)

    @pl.when(pl.program_id(0) == 0)
    def _():
        acc[...] = term

    @pl.when(pl.program_id(0) > 0)
    def _():
        acc[...] += term

    @pl.when(pl.program_id(0) == pl.num_programs(0) - 1)
    def _():
        dt_o[...] = acc[...].astype(BF)


def wgrad_q_kernel(t0, t1, t2, t3, d0, d1, d2, d3, first, rest, all_o):
    n = t0.shape[1]
    k, m = first.shape[0], first.shape[1]
    left = rest.shape[1] - 8
    res = jnp.zeros((t0.shape[0], first.shape[2]), F32)
    gain = jnp.zeros((8, first.shape[2]), F32)
    for i, (t, d) in enumerate(zip((t0, t1, t2, t3), (d0, d1, d2, d3))):
        turned = t[...].astype(BF)
        all_o[:, n * i:n * i + n] = turned
        res = res + dot(turned, d[0:n, :].astype(BF))
        gain = gain + d[n:n + 8, :]
    res = res.reshape(k, m + left, res.shape[1])
    first[...] = res[:, 0:m, :]
    rest[:, 0:left, :] = res[:, m:m + left, :]
    for i in range(k):
        rest[i, left:left + 8, :] = gain


def wgrad_k_kernel(t, d0, d1, d2, d3, rest, out):
    k, m, w = out.shape
    left = rest.shape[1]
    d = jnp.concatenate([v[...].astype(BF) for v in (d0, d1, d2, d3)], axis=0)
    out[:, 0:m - left, :] = dot(t[...], d).reshape(k, m - left, w)
    out[:, m - left:m, :] = rest[...]


def prefix_kernel(backward, v, out):
    count = v.shape[0]
    order = range(count - 1, -1, -1) if backward else range(count)
    total = jnp.zeros(v.shape[1:], F32)
    for i in order:
        out[i] = total
        total = total + v[i]


def sum_kernel(v, out):
    total = v[0]
    for i in range(1, v.shape[0]):
        total = total + v[i]
    out[...] = total


def join_kernel(q, k, out):
    total = k[0]
    for i in range(1, k.shape[0]):
        total = total + k[i]
    first, width = q.shape
    each = out.shape[1] // 2
    height = each * out.shape[0]
    qsum = jnp.concatenate([q[...], total[height:2 * height - first]], axis=0)
    gain = jnp.sum(total[2 * height - first:], axis=0, keepdims=True)
    parts = [gain[:, 128 * i:128 * i + 128] for i in range(width // 128)]
    parts.append(jnp.zeros((2 * each - len(parts), 128), F32))
    tile = jnp.concatenate(parts, axis=0)
    for j in range(out.shape[0]):
        out[j, 0:each, 0:width] = qsum[each * j:each * j + each]
        out[j, each:2 * each, 0:width] = total[each * j:each * j + each]
        out[j, :, width:width + 128] = tile


def final_kernel(v, dw_o, dg_o):
    width = v.shape[2] - 128
    each = v.shape[1] // 2
    for c in range(2):
        for b in range(2):
            g = 2 * c + b
            total = v[8 * c + b]
            for w in range(1, 4):
                total = total + v[8 * c + 2 * w + b]
            for which in range(2):
                for i in range(each):
                    r = which * each + i
                    at = 4 * width * i + width * g
                    dw_o[which:which + 1, at:at + width] = total[r:r + 1, 0:width]
            dg_o[2 * g:2 * g + 2, :] = total[0:2, width:width + 128]


def call(kernel, grid, in_specs, outs, name, flops, scratch=()):
    out_shape = [jax.ShapeDtypeStruct(s, d) for s, d, _ in outs]
    return pl.pallas_call(
        kernel,
        grid=grid,
        in_specs=in_specs,
        out_specs=[spec for _, _, spec in outs],
        out_shape=out_shape,
        scratch_shapes=list(scratch),
        name=name,
        cost_estimate=pl.CostEstimate(flops=flops, bytes_accessed=4 << 20, transcendentals=0),
        compiler_params=pltpu.CompilerParams(vmem_limit_bytes=GRANT.get(name, VMEM_LIMIT)),
    )


def call_mine(kernel, in_specs, outs, name, flops):
    return pl.pallas_call(
        kernel,
        grid_spec=pltpu.PrefetchScalarGridSpec(
            num_scalar_prefetch=1,
            grid=(2,),
            in_specs=in_specs,
            out_specs=[spec for _, _, spec in outs],
        ),
        out_shape=[jax.ShapeDtypeStruct(s, d) for s, d, _ in outs],
        name=name,
        cost_estimate=pl.CostEstimate(flops=flops, bytes_accessed=4 << 20, transcendentals=0),
        compiler_params=pltpu.CompilerParams(vmem_limit_bytes=GRANT.get(name, VMEM_LIMIT)),
    )


SMEM = pl.BlockSpec(memory_space=pltpu.SMEM)


def whole(shape):
    return pl.BlockSpec(shape, lambda *_: (0,) * len(shape))


def col(r, w=GL):
    return pl.BlockSpec((r, w), lambda g: (0, g))


def row(r, w):
    return pl.BlockSpec((r, w), lambda g: (g, 0))


def pair_at(step, me):
    return jnp.bitwise_xor(jnp.right_shift(me[0], 1), step)


def col_mine(r, w):
    return pl.BlockSpec((r, w), lambda step, me: (0, pair_at(step, me)))


def row_mine(r, w):
    return pl.BlockSpec((r, w), lambda step, me: (pair_at(step, me), 0))


def on_device(tokens, w_query, w_key, w_value, w_out, norm_gain, lengths, d_mixed):
    _, n, d = tokens.shape
    tok = tokens.reshape(n, d)
    dm = d_mixed.reshape(n, d)
    w = 2 * GL
    halves = d // w
    nseq = lax.axis_size(SEQ)
    nxy = lax.axis_size(("x", "y"))
    ngroup = lax.axis_size(GROUP)
    nv = lengths - lax.axis_index(SEQ) * n
    me = jnp.full((1,), lax.axis_index(GROUP), jnp.int32)
    gain = norm_gain.reshape(1, d)
    act = lambda dt: ((n, d), dt, col(n, w))
    st_rows = d // 2
    st_spec = row(w // 2, 128)
    state = ((st_rows, 128), F32, st_spec)
    big = 2 * n * d * d

    fk, fv, sk, st1 = call(
        kv_kernel, (halves,), [SMEM, whole((n, d)), col(d, w), col(d, w)],
        [act(BF), act(BF), act(F32), state], "kv", 2 * big,
    )(nv, tok, w_key, w_value)

    tie = lax.optimization_barrier

    def to_parts(st):
        return lax.all_to_all(st.reshape(nseq, st_rows // nseq, 128), SEQ, 0, 0, tiled=True)

    def run(parts, backward, name):
        shape = parts.shape
        (mine,) = call(
            functools.partial(prefix_kernel, backward), (), [whole(shape)],
            [(shape, F32, whole(shape))], name, 1 << 20,
        )(parts)
        return mine

    def from_parts(mine):
        return lax.all_to_all(mine, SEQ, 0, 0, tiled=True).reshape(st_rows, 128)

    def swap(v, k):
        return lax.ppermute(v, GROUP, [(i, i ^ k) for i in range(ngroup)])

    parts = to_parts(st1)
    tok_1, _ = tie((tok, st1))
    t0, t32 = call(
        turn_kernel, (halves,), [col(n, w)],
        [((d, n), BF, row(w, n)), ((d, n), F32, row(w, n))], "turn", big // 4,
    )(tok_1)
    fq, fqt, sq = call(
        q_kernel, (halves,), [whole((n, d)), col(d, w)],
        [act(BF), ((d, n), BF, row(w, n)), act(F32)], "query", big,
    )(tok_1, w_query)
    parts, fq, t0 = tie((parts, fq, t0))
    mine = run(parts, False, "prefix")
    t32, _ = tie((t32, mine))
    t1 = swap(t32, 1)
    t2 = swap(t32, 2)

    st_in = from_parts(mine)
    fq_2, _ = tie((fq, mine))
    nl, do = call(
        numer_kernel, (halves,),
        [col(n, w), col(n, w), col(n, w), whole((n, d)), row(w, d)],
        [act(F32), act(F32)], "numer", 2 * big,
    )(fq_2, fk, fv, dm, w_out)

    at, dn, rs, gp = call(
        norm_kernel, (halves,),
        [SMEM, col(n, w), st_spec, col(n, w), row(w, n), col(n, w), col(1, w)],
        [act(BF), act(F32), state, ((8, d), F32, col(8, w))], "norm", big,
    )(nv, nl, st_in, fq, fqt, do, gain)

    parts = to_parts(rs)
    dn_3, _ = tie((dn, rs))
    mine_act = ((n, d), BF, col_mine(n, w))
    dq, *dq_send = call_mine(
        dq_kernel,
        [col_mine(n, w), row_mine(w // 2, 128)] + [col_mine(n, w)] * 3 + [col_mine(8, w)],
        [mine_act] + [((n + 8, GL), F32, whole((n + 8, GL)))] * ngroup,
        "dquery", 2 * big,
    )(me, dn_3, st_in, fk, fv, sq, gp)
    parts, dq = tie((parts, dq))
    dq_got = [dq_send[0]] + [swap(dq_send[k], k) for k in range(1, ngroup)]
    mine = run(parts, True, "suffix")

    r_in = from_parts(mine)
    dn_4, t1, _ = tie((dn, t1, mine))
    t3 = swap(t1, 2)
    (lk,) = call(
        local_k_kernel, (halves,), [col(n, w), col(n, w), col(n, w)], [act(F32)], "localk", 2 * big,
    )(dn_4, fq, fv)
    steps = 2
    per = d // nxy
    first = per // 2
    gshape = (nxy, first, GL)
    rshape = (nxy, per - first + 8, GL)
    in_steps = lambda shape: pl.BlockSpec((nxy // steps,) + shape[1:], lambda g: (g, 0, 0))
    t0, _ = tie((t0, mine))
    gq, rest, tall = call(
        wgrad_q_kernel, (steps,),
        [row(d // steps, n)] * 4 + [whole((n + 8, GL))] * 4,
        [
            (gshape, F32, in_steps(gshape)),
            (rshape, F32, in_steps(rshape)),
            ((d, 4 * n), BF, row(d // steps, 4 * n)),
        ],
        "wgradq", 2 * big,
    )(t0, t1, t2, t3, *dq_got)
    lk, gq = tie((lk, gq))

    dk, *dk_send = call_mine(
        dk_kernel,
        [col_mine(n, w), col_mine(n, w), row_mine(w // 2, 128), col_mine(n, w)],
        [mine_act] + [((n, GL), F32, whole((n, GL)))] * ngroup,
        "dkey", big // 2,
    )(me, lk, fv, r_in, sk)

    dk_got = [dk_send[0]] + [swap(dk_send[k], k) for k in range(1, ngroup)]
    gq, dk = tie((gq, dk))
    gq = lax.all_to_all(gq, ("x", "y"), 0, 0, tiled=True)

    kshape = (nxy, per + rshape[1], GL)
    (gk,) = call(
        wgrad_k_kernel, (steps,), [row(d // steps, 4 * n)] + [whole((n, GL))] * 4 + [in_steps(rshape)],
        [(kshape, F32, in_steps(kshape))],
        "wgradk", 400 * big,
    )(tall, *dk_got, rest)
    gk_parts = lax.all_to_all(gk, ("x", "y"), 0, 0, tiled=True)

    dn_5, dk_5, _ = tie((dn, dk, gk))
    mo, lv = call(
        local_v_kernel, (halves,),
        [whole((n, d)), col(d, w), col(n, w), col(n, w), col(n, w)], [act(BF), act(F32)], "localv", 4 * big,
    )(at, w_out, dn_5, fq, fk)
    (dt,) = call(
        dtok_kernel, (halves,),
        [col(n, w), col(n, w), st_spec, col(n, w), col(n, w), col(d, w), col(d, w), col(d, w)],
        [((n, d), BF, whole((n, d)))], "dtok", 4 * big,
        scratch=[pltpu.VMEM((n, d), F32)],
    )(lv, fk, r_in, dq, dk_5, w_query, w_key, w_value)
    (gq_sum,) = call(
        sum_kernel, (), [whole(gshape)], [(gshape[1:], F32, whole(gshape[1:]))], "sumq", 1 << 22
    )(gq)
    gk_parts, mo, dt, gq_sum = tie((gk_parts, mo, dt, gq_sum))

    last = ("c", "w", "b")
    nlast = lax.axis_size(last)
    each = per // nlast
    jshape = (nlast, 2 * each, GL + 128)
    (both,) = call(
        join_kernel, (), [whole(gshape[1:]), whole(kshape)], [(jshape, F32, whole(jshape))],
        "join", 1 << 22,
    )(gq_sum, gk_parts)
    both = lax.all_to_all(both, last, 0, 0, tiled=True)
    dw, dg = call(
        final_kernel, (), [whole(jshape)],
        [((2, each * d), F32, whole((2, each * d))), ((8, 128), F32, whole((8, 128)))],
        "final", 1 << 20,
    )(both)
    return mo.reshape(1, n, d), dt.reshape(1, n, d), dw, dg.reshape(d)


def solution(mesh):
    fine = Mesh(mesh.devices.reshape(4, 4, 2, 4, 2), ("x", "y", "c", "w", "b"))
    acts = P(("w", "b"), SEQ, None)
    placed = (acts, P(), P(), P(), P(), P(), P(("w", "b")), acts)
    return jax.shard_map(
        on_device,
        mesh=fine,
        in_specs=placed,
        out_specs=(acts, acts, P(None, ("x", "y", "c", "w", "b")), P()),
        check_vma=False,
    )
```

```python
import functools

import jax
import jax.numpy as jnp
from jax import lax
from jax.experimental import pallas as pl
from jax.experimental.pallas import tpu as pltpu
from jax.sharding import Mesh, PartitionSpec as P

EPS = 1e-05
HD = 64
GL = 256
F32 = jnp.float32
BF = jnp.bfloat16
NN = (((1,), (0,)), ((), ()))
NT = (((1,), (1,)), ((), ()))
TN = (((0,), (0,)), ((), ()))
SEQ = ("x", "y", "c")
GROUP = ("c", "b")
VMEM_LIMIT = 64 * 1024 * 1024
GRANT = {name: 58 << 20 for name in ("turn", "query", "dquery")}
GRANT.update({name: 4 << 20 for name in ("prefix", "suffix", "final")})


def dot(a, b, dims=NN):
    return lax.dot_general(a, b, dims, preferred_element_type=F32)


def split(v):
    hi = v.astype(BF)
    return hi, (v - hi.astype(F32)).astype(BF)


def lanes(shape):
    return lax.broadcasted_iota(jnp.int32, shape, 1)


def rows(shape):
    return lax.broadcasted_iota(jnp.int32, shape, 0)


def head_masks(shape):
    which = lanes(shape) // HD
    return [which == h for h in range(GL // HD)]


def pick(mask, v):
    return jnp.where(mask, v, jnp.zeros_like(v))


def pack_state(full):
    out = []
    for p in range(GL // 128):
        blk = full[128 * p:128 * p + 128, 128 * p:128 * p + 128]
        out.append(jnp.where(lanes((HD, 128)) < HD, blk[:HD], blk[HD:]))
    return jnp.concatenate(out, axis=0)


def unpack_state(st):
    zero = jnp.zeros((128, 128), st.dtype)
    blks = []
    for p in range(GL // 128):
        a = st[HD * p:HD * p + HD]
        first = lanes((HD, 128)) < HD
        blks.append(jnp.concatenate([pick(first, a), pick(~first, a)], axis=0))
    return jnp.concatenate(
        [
            jnp.concatenate([blks[0], zero], axis=1),
            jnp.concatenate([zero, blks[1]], axis=1),
        ],
        axis=0,
    )


def valid_rows(nv_ref, count):
    return (rows((count, 1)) < nv_ref[0]).astype(F32)


def features(raw):
    ex = jnp.exp(jnp.minimum(raw, 0.0))
    up = raw > 0
    return jnp.where(up, raw + 1.0, ex), jnp.where(up, 1.0, ex)


def head_mean(*parts):
    same = (rows((GL, GL)) // HD == lanes((GL, GL)) // HD).astype(BF)
    total = dot(parts[0], same)
    for p in parts[1:]:
        total = total + dot(p, same)
    return total * (1.0 / HD)


def groups_of(ref):
    return [(j, slice(GL * j, GL * j + GL)) for j in range(ref.shape[-1] // GL)]


def my_groups(me_ref, step):
    for i in range(2):
        at = jnp.bitwise_xor(jnp.bitwise_and(me_ref[0], 1), i)
        yield (
            2 * step + i,
            pl.ds(pl.multiple_of(at * GL, GL), GL),
            pl.ds(pl.multiple_of(at * 128, 128), 128),
        )


def each_step(body):
    for step in range(2):
        pl.when(pl.program_id(0) == step)(functools.partial(body, step))


def kv_kernel(nv_ref, tok, wk, wv, fk_o, fv_o, sk_o, st_o):
    n = tok.shape[0]
    valid = valid_rows(nv_ref, n)
    feat, slope = features(dot(tok[...], wk[...]))
    fk = (feat * valid).astype(BF)
    fv = dot(tok[...], wv[...]).astype(BF)
    fk_o[...] = fk
    fv_o[...] = fv
    sk_o[...] = slope * valid
    for j, c in groups_of(fk):
        st_o[128 * j:128 * j + 128, :] = pack_state(dot(fk[:, c], fv[:, c], TN))


def turn_kernel(tok, t16_o, t32_o):
    n = tok.shape[0]
    eye = (rows((n, n)) == lanes((n, n))).astype(BF)
    res = dot(tok[...], eye, TN)
    t16_o[...] = res.astype(BF)
    t32_o[...] = res


def q_kernel(tok, wq, fq_o, fqt_o, sq_o):
    feat, slope = features(dot(tok[...], wq[...]))
    fq = feat.astype(BF)
    fq_o[...] = fq
    sq_o[...] = slope
    eye = (rows((GL, GL)) == lanes((GL, GL))).astype(BF)
    for _, c in groups_of(fq):
        fqt_o[c, :] = dot(eye, fq[:, c], NT).astype(BF)


def numer_kernel(fq, fk, fv, dm, wo, nl_o, do_o):
    n = fq.shape[0]
    do_o[...] = dot(dm[...], wo[...], NT)
    causal = rows((n, n)) >= lanes((n, n))
    for _, c in groups_of(fq):
        total = jnp.zeros((n, GL), F32)
        for m in head_masks((n, GL)):
            s = pick(causal, dot(pick(m, fq[:, c]), fk[:, c], NT)).astype(BF)
            total = total + dot(s, pick(m, fv[:, c]))
        nl_o[:, c] = total


def norm_kernel(nv_ref, nl, st, fq, fqt, do, gain, at_o, dn_o, rs_o, gp_o):
    n = nl.shape[0]
    valid = valid_rows(nv_ref, n)
    for j, c in groups_of(nl):
        r = slice(128 * j, 128 * j + 128)
        s_hi, s_lo = split(unpack_state(st[r, :]))
        numer = nl[:, c] + dot(fq[:, c], s_hi) + dot(fq[:, c], s_lo)
        inv = lax.rsqrt(head_mean((numer * numer).astype(BF)) + EPS)
        normed = numer * inv
        scale = gain[:, c]
        at_o[:, c] = (normed * scale * valid).astype(BF)
        dov = do[:, c] * valid
        gp_o[:, c] = jnp.sum((dov * normed).reshape(n // 8, 8, GL), axis=0)
        g = dov * scale
        dn = inv * (g - normed * head_mean(*split(g * normed)))
        dn_o[:, c] = dn
        d_hi, d_lo = split(dn)
        rs_o[r, :] = pack_state(dot(fqt[c, :], d_hi) + dot(fqt[c, :], d_lo))


def dq_kernel(me_ref, dn, st, fk, fv, sq, gp, dq_o, *send):
    n = dn.shape[0]

    def body(step):
        causal = rows((n, n)) >= lanes((n, n))
        for k, c, r in my_groups(me_ref, step):
            s_hi, s_lo = split(unpack_state(st[r, :]))
            d_hi, d_lo = split(dn[:, c])
            total = dot(d_hi, s_hi, NT) + dot(d_lo, s_hi, NT) + dot(d_hi, s_lo, NT)
            keys, values = fk[:, c], fv[:, c]
            for m in head_masks((n, GL)):
                vm = pick(m, values)
                w = pick(causal, dot(d_hi, vm, NT) + dot(d_lo, vm, NT)).astype(BF)
                total = total + dot(w, pick(m, keys))
            dq = (total * sq[:, c]).astype(BF)
            dq_o[:, c] = dq
            send[k][0:n, :] = dq.astype(F32)
            send[k][n:n + 8, :] = gp[:, c]

    each_step(body)


def local_k_kernel(dn, fq, fv, lk_o):
    n = dn.shape[0]
    later = lanes((n, n)) >= rows((n, n))
    for _, c in groups_of(dn):
        d_hi, d_lo = split(dn[:, c])
        total = jnp.zeros((n, GL), F32)
        for m in head_masks((n, GL)):
            vm = pick(m, fv[:, c])
            w = pick(later, dot(vm, d_hi, NT) + dot(vm, d_lo, NT)).astype(BF)
            total = total + dot(w, pick(m, fq[:, c]))
        lk_o[:, c] = total


def local_v_kernel(at, wo, dn, fq, fk, mo_o, lv_o):
    n = dn.shape[0]
    mo_o[...] = dot(at[...], wo[...]).astype(BF)
    later = lanes((n, n)) >= rows((n, n))
    for _, c in groups_of(dn):
        d_hi = dn[:, c].astype(BF)
        total = jnp.zeros((n, GL), F32)
        for m in head_masks((n, GL)):
            s = pick(later, dot(pick(m, fk[:, c]), fq[:, c], NT)).astype(BF)
            total = total + dot(s, pick(m, d_hi))
        lv_o[:, c] = total


def dk_kernel(me_ref, lk, fv, st, sk, dk_o, *send):
    def body(step):
        for k, c, r in my_groups(me_ref, step):
            r_hi, r_lo = split(unpack_state(st[r, :]))
            total = lk[:, c] + dot(fv[:, c], r_hi, NT) + dot(fv[:, c], r_lo, NT)
            dk = (total * sk[:, c]).astype(BF)
            dk_o[:, c] = dk
            send[k][...] = dk.astype(F32)

    each_step(body)


def dtok_kernel(lv, fk, st, dq, dk, wq, wk, wv, dt_o, acc):
    term = dot(dq[...], wq[...], NT) + dot(dk[...], wk[...], NT)
    dv = []
    for j, c in groups_of(lv):
        r_hi, r_lo = split(unpack_state(st[128 * j:128 * j + 128, :]))
        dv.append((lv[:, c] + dot(fk[:, c], r_hi) + dot(fk[:, c], r_lo)).astype(BF))
    term = term + dot(jnp.concatenate(dv, axis=1), wv[...], NT)

    @pl.when(pl.program_id(0) == 0)
    def _():
        acc[...] = term

    @pl.when(pl.program_id(0) > 0)
    def _():
        acc[...] += term

    @pl.when(pl.program_id(0) == pl.num_programs(0) - 1)
    def _():
        dt_o[...] = acc[...].astype(BF)


def wgrad_q_kernel(y_ref, t0, t1, t2, t3, d0, d1, d2, d3, all_o, *send):
    n = t0.shape[3]
    blocks, m = t0.shape[0], t0.shape[2]
    res = jnp.zeros((blocks * m, d0.shape[1]), F32)
    gain = jnp.zeros((8, d0.shape[1]), F32)
    for i, (t, d) in enumerate(zip((t0, t1, t2, t3), (d0, d1, d2, d3))):
        turned = t[...].reshape(blocks * m, n).astype(BF)
        all_o[:, :, :, n * i:n * i + n] = turned.reshape(blocks, 1, m, n)
        res = res + dot(turned, d[0:n, :].astype(BF))
        gain = gain + d[n:n + 8, :]
    for k, out in enumerate(send):
        @pl.when(pl.program_id(0) == k)
        def _():
            out[:, 0:m, :] = res.reshape(blocks, m, res.shape[1])
            for i in range(blocks):
                out[i, m:m + 8, :] = gain


def sum_y_kernel(x_ref, v0, v1, v2, v3, *send):
    for k, out in enumerate(send):
        at = jnp.bitwise_xor(x_ref[0], k)
        out[...] = v0[at] + v1[at] + v2[at] + v3[at]


def wgrad_k_kernel(t, d0, d1, d2, d3, out):
    k, m, w = out.shape
    d = jnp.concatenate([v[...].astype(BF) for v in (d0, d1, d2, d3)], axis=0)
    out[...] = dot(t[...], d).reshape(k, m, w)


def prefix_kernel(backward, v, out):
    count = v.shape[0]
    order = range(count - 1, -1, -1) if backward else range(count)
    total = jnp.zeros(v.shape[1:], F32)
    for i in order:
        out[i] = total
        total = total + v[i]


def join_kernel(q0, q1, q2, q3, k, out):
    total = k[0]
    for i in range(1, k.shape[0]):
        total = total + k[i]
    height, width = total.shape
    each = out.shape[1] // 2
    q = q0[...] + q1[...] + q2[...] + q3[...]
    gain = jnp.sum(q[height:height + 8], axis=0, keepdims=True)
    parts = [gain[:, 128 * i:128 * i + 128] for i in range(width // 128)]
    parts.append(jnp.zeros((2 * each - len(parts), 128), F32))
    tile = jnp.concatenate(parts, axis=0)
    for j in range(out.shape[0]):
        out[j, 0:each, 0:width] = q[each * j:each * j + each]
        out[j, each:2 * each, 0:width] = total[each * j:each * j + each]
        out[j, :, width:width + 128] = tile


def final_kernel(v, dw_o, dg_o):
    width = v.shape[2] - 128
    each = v.shape[1] // 2
    for c in range(2):
        for b in range(2):
            g = 2 * c + b
            total = v[8 * c + b]
            for w in range(1, 4):
                total = total + v[8 * c + 2 * w + b]
            for which in range(2):
                for i in range(each):
                    r = which * each + i
                    at = 4 * width * i + width * g
                    dw_o[which:which + 1, at:at + width] = total[r:r + 1, 0:width]
            dg_o[2 * g:2 * g + 2, :] = total[0:2, width:width + 128]


def call(kernel, grid, in_specs, outs, name, flops, scratch=()):
    out_shape = [jax.ShapeDtypeStruct(s, d) for s, d, _ in outs]
    return pl.pallas_call(
        kernel,
        grid=grid,
        in_specs=in_specs,
        out_specs=[spec for _, _, spec in outs],
        out_shape=out_shape,
        scratch_shapes=list(scratch),
        name=name,
        cost_estimate=pl.CostEstimate(flops=flops, bytes_accessed=4 << 20, transcendentals=0),
        compiler_params=pltpu.CompilerParams(vmem_limit_bytes=GRANT.get(name, VMEM_LIMIT)),
    )


def call_mine(kernel, in_specs, outs, name, flops, steps=2):
    return pl.pallas_call(
        kernel,
        grid_spec=pltpu.PrefetchScalarGridSpec(
            num_scalar_prefetch=1,
            grid=(steps,),
            in_specs=in_specs,
            out_specs=[spec for _, _, spec in outs],
        ),
        out_shape=[jax.ShapeDtypeStruct(s, d) for s, d, _ in outs],
        name=name,
        cost_estimate=pl.CostEstimate(flops=flops, bytes_accessed=4 << 20, transcendentals=0),
        compiler_params=pltpu.CompilerParams(vmem_limit_bytes=GRANT.get(name, VMEM_LIMIT)),
    )


SMEM = pl.BlockSpec(memory_space=pltpu.SMEM)


def whole(shape):
    return pl.BlockSpec(shape, lambda *_: (0,) * len(shape))


def col(r, w=GL):
    return pl.BlockSpec((r, w), lambda g: (0, g))


def row(r, w):
    return pl.BlockSpec((r, w), lambda g: (g, 0))


def pair_at(step, me):
    return jnp.bitwise_xor(jnp.right_shift(me[0], 1), step)


def col_mine(r, w):
    return pl.BlockSpec((r, w), lambda step, me: (0, pair_at(step, me)))


def row_mine(r, w):
    return pl.BlockSpec((r, w), lambda step, me: (pair_at(step, me), 0))


def on_device(tokens, w_query, w_key, w_value, w_out, norm_gain, lengths, d_mixed):
    _, n, d = tokens.shape
    tok = tokens.reshape(n, d)
    dm = d_mixed.reshape(n, d)
    w = 2 * GL
    halves = d // w
    nseq = lax.axis_size(SEQ)
    nxy = lax.axis_size(("x", "y"))
    ngroup = lax.axis_size(GROUP)
    nv = lengths - lax.axis_index(SEQ) * n
    own = lambda axes: jnp.full((1,), lax.axis_index(axes), jnp.int32)
    me = own(GROUP)
    gain = norm_gain.reshape(1, d)
    act = lambda dt: ((n, d), dt, col(n, w))
    st_rows = d // 2
    st_spec = row(w // 2, 128)
    state = ((st_rows, 128), F32, st_spec)
    big = 2 * n * d * d

    fk, fv, sk, st1 = call(
        kv_kernel, (halves,), [SMEM, whole((n, d)), col(d, w), col(d, w)],
        [act(BF), act(BF), act(F32), state], "kv", 2 * big,
    )(nv, tok, w_key, w_value)

    tie = lax.optimization_barrier

    def to_parts(st):
        return lax.all_to_all(st.reshape(nseq, st_rows // nseq, 128), SEQ, 0, 0, tiled=True)

    def run(parts, backward, name):
        shape = parts.shape
        (mine,) = call(
            functools.partial(prefix_kernel, backward), (), [whole(shape)],
            [(shape, F32, whole(shape))], name, 1 << 20,
        )(parts)
        return mine

    def from_parts(mine):
        return lax.all_to_all(mine, SEQ, 0, 0, tiled=True).reshape(st_rows, 128)

    def swap(v, k):
        return lax.ppermute(v, GROUP, [(i, i ^ k) for i in range(ngroup)])

    def turn_about(axis, v, k):
        return lax.ppermute(v, axis, [(i, i ^ k) for i in range(lax.axis_size(axis))])

    parts = to_parts(st1)
    tok_1, _ = tie((tok, st1))
    t0, t32 = call(
        turn_kernel, (halves,), [col(n, w)],
        [((d, n), BF, row(w, n)), ((d, n), F32, row(w, n))], "turn", big // 4,
    )(tok_1)
    fq, fqt, sq = call(
        q_kernel, (halves,), [whole((n, d)), col(d, w)],
        [act(BF), ((d, n), BF, row(w, n)), act(F32)], "query", big,
    )(tok_1, w_query)
    parts, fq, t0 = tie((parts, fq, t0))
    mine = run(parts, False, "prefix")
    t32, _ = tie((t32, mine))
    t1 = swap(t32, 1)
    t2 = swap(t32, 2)

    st_in = from_parts(mine)
    fq_2, _ = tie((fq, mine))
    nl, do = call(
        numer_kernel, (halves,),
        [col(n, w), col(n, w), col(n, w), whole((n, d)), row(w, d)],
        [act(F32), act(F32)], "numer", 2 * big,
    )(fq_2, fk, fv, dm, w_out)

    at, dn, rs, gp = call(
        norm_kernel, (halves,),
        [SMEM, col(n, w), st_spec, col(n, w), row(w, n), col(n, w), col(1, w)],
        [act(BF), act(F32), state, ((8, d), F32, col(8, w))], "norm", big,
    )(nv, nl, st_in, fq, fqt, do, gain)

    parts = to_parts(rs)
    dn_3, _ = tie((dn, rs))
    mine_act = ((n, d), BF, col_mine(n, w))
    dq, *dq_send = call_mine(
        dq_kernel,
        [col_mine(n, w), row_mine(w // 2, 128)] + [col_mine(n, w)] * 3 + [col_mine(8, w)],
        [mine_act] + [((n + 8, GL), F32, whole((n + 8, GL)))] * ngroup,
        "dquery", 2 * big,
    )(me, dn_3, st_in, fk, fv, sq, gp)
    parts, dq = tie((parts, dq))
    dq_got = [dq_send[0]] + [swap(dq_send[k], k) for k in range(1, ngroup)]
    mine = run(parts, True, "suffix")

    r_in = from_parts(mine)
    dn_4, t1, _ = tie((dn, t1, mine))
    t3 = swap(t1, 2)
    (lk,) = call(
        local_k_kernel, (halves,), [col(n, w), col(n, w), col(n, w)], [act(F32)], "localk", 1,
    )(dn_4, fq, fv)
    dk, *dk_send = call_mine(
        dk_kernel,
        [col_mine(n, w), col_mine(n, w), row_mine(w // 2, 128), col_mine(n, w)],
        [mine_act] + [((n, GL), F32, whole((n, GL)))] * ngroup,
        "dkey", 1,
    )(me, lk, fv, r_in, sk)

    dk_got = [dk_send[0]] + [swap(dk_send[k], k) for k in range(1, ngroup)]
    side = lax.axis_size("x")
    per = d // nxy
    dq_got, _ = tie((dq_got, dk))
    at_y = lambda depth: pl.BlockSpec(
        (side, 1, per, depth), lambda k, y: (0, jnp.bitwise_xor(y[0], k), 0, 0)
    )
    by_xy = lambda v: v.reshape(side, side, per, v.shape[-1])
    qshape = (side, per + 8, GL)
    tall, *gq_send = call_mine(
        wgrad_q_kernel,
        [at_y(n)] * 4 + [whole((n + 8, GL))] * 4,
        [((side, side, per, 4 * n), BF, at_y(4 * n))] + [(qshape, F32, whole(qshape))] * side,
        "wgradq", 2 * big, side,
    )(own("y"), by_xy(t0), by_xy(t1), by_xy(t2), by_xy(t3), *dq_got)
    gq_got = [gq_send[0]] + [turn_about("y", gq_send[k], k) for k in range(1, side)]

    steps = 2
    kshape = (nxy, per, GL)
    (gk,) = call(
        wgrad_k_kernel, (steps,), [row(d // steps, 4 * n)] + [whole((n, GL))] * 4,
        [(kshape, F32, pl.BlockSpec((nxy // steps,) + kshape[1:], lambda g: (g, 0, 0)))],
        "wgradk", 400 * big,
    )(tall.reshape(d, 4 * n), *dk_got)
    gk_parts = lax.all_to_all(gk, ("x", "y"), 0, 0, tiled=True)

    dn_5, dk_5, _ = tie((dn, dk, gk))
    mo, lv = call(
        local_v_kernel, (halves,),
        [whole((n, d)), col(d, w), col(n, w), col(n, w), col(n, w)], [act(BF), act(F32)], "localv", 400 * big,
    )(at, w_out, dn_5, fq, fk)
    (dt,) = call(
        dtok_kernel, (halves,),
        [col(n, w), col(n, w), st_spec, col(n, w), col(n, w), col(d, w), col(d, w), col(d, w)],
        [((n, d), BF, whole((n, d)))], "dtok", 1,
        scratch=[pltpu.VMEM((n, d), F32)],
    )(lv, fk, r_in, dq, dk_5, w_query, w_key, w_value)
    gq_got, _ = tie((gq_got, gk))
    gq_send = call(
        sum_y_kernel, (), [SMEM] + [whole(qshape)] * side,
        [(qshape[1:], F32, whole(qshape[1:]))] * side, "sumy", 1 << 22,
    )(own("x"), *gq_got)
    gq_got = [gq_send[0]] + [turn_about("x", gq_send[k], k) for k in range(1, side)]
    gk_parts, mo, dt, gq_got = tie((gk_parts, mo, dt, gq_got))

    last = ("c", "w", "b")
    nlast = lax.axis_size(last)
    each = per // nlast
    jshape = (nlast, 2 * each, GL + 128)
    (both,) = call(
        join_kernel, (), [whole(qshape[1:])] * side + [whole(kshape)],
        [(jshape, F32, whole(jshape))], "join", 1 << 22,
    )(*gq_got, gk_parts)
    both = lax.all_to_all(both, last, 0, 0, tiled=True)
    dw, dg = call(
        final_kernel, (), [whole(jshape)],
        [((2, each * d), F32, whole((2, each * d))), ((8, 128), F32, whole((8, 128)))],
        "final", 1 << 20,
    )(both)
    return mo.reshape(1, n, d), dt.reshape(1, n, d), dw, dg.reshape(d)


def solution(mesh):
    fine = Mesh(mesh.devices.reshape(4, 4, 2, 4, 2), ("x", "y", "c", "w", "b"))
    acts = P(("w", "b"), SEQ, None)
    placed = (acts, P(), P(), P(), P(), P(), P(("w", "b")), acts)
    return jax.shard_map(
        on_device,
        mesh=fine,
        in_specs=placed,
        out_specs=(acts, acts, P(None, ("x", "y", "c", "w", "b")), P()),
        check_vma=False,
    )
```

```python
import functools

import jax
import jax.numpy as jnp
from jax import lax
from jax.experimental import pallas as pl
from jax.experimental.pallas import tpu as pltpu
from jax.sharding import Mesh, PartitionSpec as P

EPS = 1e-05
HD = 64
GL = 256
F32 = jnp.float32
BF = jnp.bfloat16
NN = (((1,), (0,)), ((), ()))
NT = (((1,), (1,)), ((), ()))
TN = (((0,), (0,)), ((), ()))
SEQ = ("x", "y", "c")
GROUP = ("c", "b")
VMEM_LIMIT = 64 * 1024 * 1024
GRANT = {name: 58 << 20 for name in ("turn", "query", "dquery")}
GRANT.update({name: 4 << 20 for name in ("prefix", "suffix", "final")})


def dot(a, b, dims=NN):
    return lax.dot_general(a, b, dims, preferred_element_type=F32)


def split(v):
    hi = v.astype(BF)
    return hi, (v - hi.astype(F32)).astype(BF)


def lanes(shape):
    return lax.broadcasted_iota(jnp.int32, shape, 1)


def rows(shape):
    return lax.broadcasted_iota(jnp.int32, shape, 0)


def head_masks(shape):
    which = lanes(shape) // HD
    return [which == h for h in range(GL // HD)]


def pick(mask, v):
    return jnp.where(mask, v, jnp.zeros_like(v))


def pack_state(full):
    out = []
    for p in range(GL // 128):
        blk = full[128 * p:128 * p + 128, 128 * p:128 * p + 128]
        out.append(jnp.where(lanes((HD, 128)) < HD, blk[:HD], blk[HD:]))
    return jnp.concatenate(out, axis=0)


def unpack_state(st):
    zero = jnp.zeros((128, 128), st.dtype)
    blks = []
    for p in range(GL // 128):
        a = st[HD * p:HD * p + HD]
        first = lanes((HD, 128)) < HD
        blks.append(jnp.concatenate([pick(first, a), pick(~first, a)], axis=0))
    return jnp.concatenate(
        [
            jnp.concatenate([blks[0], zero], axis=1),
            jnp.concatenate([zero, blks[1]], axis=1),
        ],
        axis=0,
    )


def valid_rows(nv_ref, count):
    return (rows((count, 1)) < nv_ref[0]).astype(F32)


def features(raw):
    ex = jnp.exp(jnp.minimum(raw, 0.0))
    up = raw > 0
    return jnp.where(up, raw + 1.0, ex), jnp.where(up, 1.0, ex)


def head_mean(*parts):
    same = (rows((GL, GL)) // HD == lanes((GL, GL)) // HD).astype(BF)
    total = dot(parts[0], same)
    for p in parts[1:]:
        total = total + dot(p, same)
    return total * (1.0 / HD)


def groups_of(ref):
    return [(j, slice(GL * j, GL * j + GL)) for j in range(ref.shape[-1] // GL)]


def my_groups(me_ref, step):
    for i in range(2):
        at = jnp.bitwise_xor(jnp.bitwise_and(me_ref[0], 1), i)
        yield (
            2 * step + i,
            pl.ds(pl.multiple_of(at * GL, GL), GL),
            pl.ds(pl.multiple_of(at * 128, 128), 128),
        )


def each_step(body):
    for step in range(2):
        pl.when(pl.program_id(0) == step)(functools.partial(body, step))


def kv_kernel(nv_ref, tok, wk, wv, fk_o, fv_o, sk_o, st_o):
    n = tok.shape[0]
    valid = valid_rows(nv_ref, n)
    feat, slope = features(dot(tok[...], wk[...]))
    fk = (feat * valid).astype(BF)
    fv = dot(tok[...], wv[...]).astype(BF)
    fk_o[...] = fk
    fv_o[...] = fv
    sk_o[...] = slope * valid
    for j, c in groups_of(fk):
        st_o[128 * j:128 * j + 128, :] = pack_state(dot(fk[:, c], fv[:, c], TN))


def turn_kernel(tok, t16_o, t32_o):
    n = tok.shape[0]
    eye = (rows((n, n)) == lanes((n, n))).astype(BF)
    res = dot(tok[...], eye, TN)
    t16_o[...] = res.astype(BF)
    t32_o[...] = res


def q_kernel(tok, wq, fq_o, fqt_o, sq_o):
    feat, slope = features(dot(tok[...], wq[...]))
    fq = feat.astype(BF)
    fq_o[...] = fq
    sq_o[...] = slope
    eye = (rows((GL, GL)) == lanes((GL, GL))).astype(BF)
    for _, c in groups_of(fq):
        fqt_o[c, :] = dot(eye, fq[:, c], NT).astype(BF)


def numer_kernel(fq, fk, fv, dm, wo, nl_o, do_o):
    n = fq.shape[0]
    do_o[...] = dot(dm[...], wo[...], NT)
    causal = rows((n, n)) >= lanes((n, n))
    for _, c in groups_of(fq):
        total = jnp.zeros((n, GL), F32)
        for m in head_masks((n, GL)):
            s = pick(causal, dot(pick(m, fq[:, c]), fk[:, c], NT)).astype(BF)
            total = total + dot(s, pick(m, fv[:, c]))
        nl_o[:, c] = total


def norm_kernel(nv_ref, nl, st, fq, fqt, do, gain, at_o, dn_o, rs_o, gp_o):
    n = nl.shape[0]
    valid = valid_rows(nv_ref, n)
    for j, c in groups_of(nl):
        r = slice(128 * j, 128 * j + 128)
        s_hi, s_lo = split(unpack_state(st[r, :]))
        numer = nl[:, c] + dot(fq[:, c], s_hi) + dot(fq[:, c], s_lo)
        inv = lax.rsqrt(head_mean((numer * numer).astype(BF)) + EPS)
        normed = numer * inv
        scale = gain[:, c]
        at_o[:, c] = (normed * scale * valid).astype(BF)
        dov = do[:, c] * valid
        gp_o[:, c] = jnp.sum((dov * normed).reshape(n // 8, 8, GL), axis=0)
        g = dov * scale
        dn = inv * (g - normed * head_mean(*split(g * normed)))
        dn_o[:, c] = dn
        d_hi, d_lo = split(dn)
        rs_o[r, :] = pack_state(dot(fqt[c, :], d_hi) + dot(fqt[c, :], d_lo))


def dq_kernel(me_ref, dn, st, fk, fv, sq, gp, dq_o, *send):
    n = dn.shape[0]

    def body(step):
        causal = rows((n, n)) >= lanes((n, n))
        for k, c, r in my_groups(me_ref, step):
            s_hi, s_lo = split(unpack_state(st[r, :]))
            d_hi, d_lo = split(dn[:, c])
            total = dot(d_hi, s_hi, NT) + dot(d_lo, s_hi, NT) + dot(d_hi, s_lo, NT)
            keys, values = fk[:, c], fv[:, c]
            for m in head_masks((n, GL)):
                vm = pick(m, values)
                w = pick(causal, dot(d_hi, vm, NT) + dot(d_lo, vm, NT)).astype(BF)
                total = total + dot(w, pick(m, keys))
            dq = (total * sq[:, c]).astype(BF)
            dq_o[:, c] = dq
            send[k][0:n, :] = dq.astype(F32)
            send[k][n:n + 8, :] = gp[:, c]

    each_step(body)


def local_k_kernel(dn, fq, fv, lk_o):
    n = dn.shape[0]
    later = lanes((n, n)) >= rows((n, n))
    for _, c in groups_of(dn):
        d_hi, d_lo = split(dn[:, c])
        total = jnp.zeros((n, GL), F32)
        for m in head_masks((n, GL)):
            vm = pick(m, fv[:, c])
            w = pick(later, dot(vm, d_hi, NT) + dot(vm, d_lo, NT)).astype(BF)
            total = total + dot(w, pick(m, fq[:, c]))
        lk_o[:, c] = total


def local_v_kernel(at, wo, dn, fq, fk, mo_o, lv_o):
    n = dn.shape[0]
    mo_o[...] = dot(at[...], wo[...]).astype(BF)
    later = lanes((n, n)) >= rows((n, n))
    for _, c in groups_of(dn):
        d_hi = dn[:, c].astype(BF)
        total = jnp.zeros((n, GL), F32)
        for m in head_masks((n, GL)):
            s = pick(later, dot(pick(m, fk[:, c]), fq[:, c], NT)).astype(BF)
            total = total + dot(s, pick(m, d_hi))
        lv_o[:, c] = total


def dk_kernel(me_ref, lk, fv, st, sk, dk_o, *send):
    def body(step):
        for k, c, r in my_groups(me_ref, step):
            r_hi, r_lo = split(unpack_state(st[r, :]))
            total = lk[:, c] + dot(fv[:, c], r_hi, NT) + dot(fv[:, c], r_lo, NT)
            dk = (total * sk[:, c]).astype(BF)
            dk_o[:, c] = dk
            send[k][...] = dk.astype(F32)

    each_step(body)


def dtok_kernel(lv, fk, st, dq, dk, wq, wk, wv, dt_o, acc):
    term = dot(dq[...], wq[...], NT) + dot(dk[...], wk[...], NT)
    dv = []
    for j, c in groups_of(lv):
        r_hi, r_lo = split(unpack_state(st[128 * j:128 * j + 128, :]))
        dv.append((lv[:, c] + dot(fk[:, c], r_hi) + dot(fk[:, c], r_lo)).astype(BF))
    term = term + dot(jnp.concatenate(dv, axis=1), wv[...], NT)

    @pl.when(pl.program_id(0) == 0)
    def _():
        acc[...] = term

    @pl.when(pl.program_id(0) > 0)
    def _():
        acc[...] += term

    @pl.when(pl.program_id(0) == pl.num_programs(0) - 1)
    def _():
        dt_o[...] = acc[...].astype(BF)


def wgrad_q_kernel(y_ref, t0, t1, t2, t3, d0, d1, d2, d3, all_o, *send):
    n = t0.shape[3]
    blocks, m = t0.shape[0], t0.shape[2]
    res = jnp.zeros((blocks * m, d0.shape[1]), F32)
    gain = jnp.zeros((8, d0.shape[1]), F32)
    for i, (t, d) in enumerate(zip((t0, t1, t2, t3), (d0, d1, d2, d3))):
        turned = t[...].reshape(blocks * m, n).astype(BF)
        all_o[:, :, :, n * i:n * i + n] = turned.reshape(blocks, 1, m, n)
        res = res + dot(turned, d[0:n, :].astype(BF))
        gain = gain + d[n:n + 8, :]
    for k, out in enumerate(send):
        @pl.when(pl.program_id(0) == k)
        def _():
            out[:, 0:m, :] = res.reshape(blocks, m, res.shape[1])
            for i in range(blocks):
                out[i, m:m + 8, :] = gain


def sum_y_kernel(x_ref, v0, v1, v2, v3, *send):
    for k, out in enumerate(send):
        at = jnp.bitwise_xor(x_ref[0], k)
        out[...] = v0[at] + v1[at] + v2[at] + v3[at]


def wgrad_k_kernel(t, d0, d1, d2, d3, out):
    k, m, w = out.shape
    d = jnp.concatenate([v[...].astype(BF) for v in (d0, d1, d2, d3)], axis=0)
    out[...] = dot(t[...], d).reshape(k, m, w)


def prefix_kernel(backward, v, out):
    count = v.shape[0]
    order = range(count - 1, -1, -1) if backward else range(count)
    total = jnp.zeros(v.shape[1:], F32)
    for i in order:
        out[i] = total
        total = total + v[i]


def join_kernel(q0, q1, q2, q3, k, out):
    total = k[0]
    for i in range(1, k.shape[0]):
        total = total + k[i]
    height, width = total.shape
    each = out.shape[1] // 2
    q = q0[...] + q1[...] + q2[...] + q3[...]
    gain = jnp.sum(q[height:height + 8], axis=0, keepdims=True)
    parts = [gain[:, 128 * i:128 * i + 128] for i in range(width // 128)]
    parts.append(jnp.zeros((2 * each - len(parts), 128), F32))
    tile = jnp.concatenate(parts, axis=0)
    for j in range(out.shape[0]):
        out[j, 0:each, 0:width] = q[each * j:each * j + each]
        out[j, each:2 * each, 0:width] = total[each * j:each * j + each]
        out[j, :, width:width + 128] = tile


def final_kernel(v, dw_o, dg_o):
    width = v.shape[2] - 128
    each = v.shape[1] // 2
    for c in range(2):
        for b in range(2):
            g = 2 * c + b
            total = v[8 * c + b]
            for w in range(1, 4):
                total = total + v[8 * c + 2 * w + b]
            for which in range(2):
                for i in range(each):
                    r = which * each + i
                    at = 4 * width * i + width * g
                    dw_o[which:which + 1, at:at + width] = total[r:r + 1, 0:width]
            dg_o[2 * g:2 * g + 2, :] = total[0:2, width:width + 128]


def call(kernel, grid, in_specs, outs, name, flops, scratch=()):
    out_shape = [jax.ShapeDtypeStruct(s, d) for s, d, _ in outs]
    return pl.pallas_call(
        kernel,
        grid=grid,
        in_specs=in_specs,
        out_specs=[spec for _, _, spec in outs],
        out_shape=out_shape,
        scratch_shapes=list(scratch),
        name=name,
        cost_estimate=pl.CostEstimate(flops=flops, bytes_accessed=4 << 20, transcendentals=0),
        compiler_params=pltpu.CompilerParams(vmem_limit_bytes=GRANT.get(name, VMEM_LIMIT)),
    )


def call_mine(kernel, in_specs, outs, name, flops, steps=2):
    return pl.pallas_call(
        kernel,
        grid_spec=pltpu.PrefetchScalarGridSpec(
            num_scalar_prefetch=1,
            grid=(steps,),
            in_specs=in_specs,
            out_specs=[spec for _, _, spec in outs],
        ),
        out_shape=[jax.ShapeDtypeStruct(s, d) for s, d, _ in outs],
        name=name,
        cost_estimate=pl.CostEstimate(flops=flops, bytes_accessed=4 << 20, transcendentals=0),
        compiler_params=pltpu.CompilerParams(vmem_limit_bytes=GRANT.get(name, VMEM_LIMIT)),
    )


SMEM = pl.BlockSpec(memory_space=pltpu.SMEM)


def whole(shape):
    return pl.BlockSpec(shape, lambda *_: (0,) * len(shape))


def col(r, w=GL):
    return pl.BlockSpec((r, w), lambda g: (0, g))


def row(r, w):
    return pl.BlockSpec((r, w), lambda g: (g, 0))


def pair_at(step, me):
    return jnp.bitwise_xor(jnp.right_shift(me[0], 1), step)


def col_mine(r, w):
    return pl.BlockSpec((r, w), lambda step, me: (0, pair_at(step, me)))


def row_mine(r, w):
    return pl.BlockSpec((r, w), lambda step, me: (pair_at(step, me), 0))


def on_device(tokens, w_query, w_key, w_value, w_out, norm_gain, lengths, d_mixed):
    _, n, d = tokens.shape
    tok = tokens.reshape(n, d)
    dm = d_mixed.reshape(n, d)
    w = 2 * GL
    halves = d // w
    nseq = lax.axis_size(SEQ)
    nxy = lax.axis_size(("x", "y"))
    ngroup = lax.axis_size(GROUP)
    nv = lengths - lax.axis_index(SEQ) * n
    own = lambda axes: jnp.full((1,), lax.axis_index(axes), jnp.int32)
    me = own(GROUP)
    gain = norm_gain.reshape(1, d)
    act = lambda dt: ((n, d), dt, col(n, w))
    st_rows = d // 2
    st_spec = row(w // 2, 128)
    state = ((st_rows, 128), F32, st_spec)
    big = 2 * n * d * d

    fk, fv, sk, st1 = call(
        kv_kernel, (halves,), [SMEM, whole((n, d)), col(d, w), col(d, w)],
        [act(BF), act(BF), act(F32), state], "kv", 2 * big,
    )(nv, tok, w_key, w_value)

    tie = lax.optimization_barrier

    def to_parts(st):
        return lax.all_to_all(st.reshape(nseq, st_rows // nseq, 128), SEQ, 0, 0, tiled=True)

    def run(parts, backward, name):
        shape = parts.shape
        (mine,) = call(
            functools.partial(prefix_kernel, backward), (), [whole(shape)],
            [(shape, F32, whole(shape))], name, 1 << 20,
        )(parts)
        return mine

    def from_parts(mine):
        return lax.all_to_all(mine, SEQ, 0, 0, tiled=True).reshape(st_rows, 128)

    def swap(v, k):
        return lax.ppermute(v, GROUP, [(i, i ^ k) for i in range(ngroup)])

    def turn_about(axis, v, k):
        return lax.ppermute(v, axis, [(i, i ^ k) for i in range(lax.axis_size(axis))])

    parts = to_parts(st1)
    tok_1, _ = tie((tok, st1))
    t0, t32 = call(
        turn_kernel, (halves,), [col(n, w)],
        [((d, n), BF, row(w, n)), ((d, n), F32, row(w, n))], "turn", big // 4,
    )(tok_1)
    fq, fqt, sq = call(
        q_kernel, (halves,), [whole((n, d)), col(d, w)],
        [act(BF), ((d, n), BF, row(w, n)), act(F32)], "query", big,
    )(tok_1, w_query)
    parts, fq, t0 = tie((parts, fq, t0))
    mine = run(parts, False, "prefix")

    t32, _ = tie((t32, mine))
    t1 = swap(t32, 1)
    t2 = swap(t32, 2)

    st_in = from_parts(mine)
    fq_2, _ = tie((fq, mine))
    nl, do = call(
        numer_kernel, (halves,),
        [col(n, w), col(n, w), col(n, w), whole((n, d)), row(w, d)],
        [act(F32), act(F32)], "numer", 2 * big,
    )(fq_2, fk, fv, dm, w_out)

    at, dn, rs, gp = call(
        norm_kernel, (halves,),
        [SMEM, col(n, w), st_spec, col(n, w), row(w, n), col(n, w), col(1, w)],
        [act(BF), act(F32), state, ((8, d), F32, col(8, w))], "norm", big,
    )(nv, nl, st_in, fq, fqt, do, gain)

    parts = to_parts(rs)
    dn_3, _ = tie((dn, rs))
    mine_act = ((n, d), BF, col_mine(n, w))
    dq, *dq_send = call_mine(
        dq_kernel,
        [col_mine(n, w), row_mine(w // 2, 128)] + [col_mine(n, w)] * 3 + [col_mine(8, w)],
        [mine_act] + [((n + 8, GL), F32, whole((n + 8, GL)))] * ngroup,
        "dquery", 2 * big,
    )(me, dn_3, st_in, fk, fv, sq, gp)
    parts, dq = tie((parts, dq))
    dq_got = [dq_send[0]] + [swap(dq_send[k], k) for k in range(1, ngroup)]
    mine = run(parts, True, "suffix")

    r_in = from_parts(mine)
    dn_4, t1, _ = tie((dn, t1, mine))
    t3 = swap(t1, 2)
    (lk,) = call(
        local_k_kernel, (halves,), [col(n, w), col(n, w), col(n, w)], [act(F32)], "localk", 1,
    )(dn_4, fq, fv)
    dk, *dk_send = call_mine(
        dk_kernel,
        [col_mine(n, w), col_mine(n, w), row_mine(w // 2, 128), col_mine(n, w)],
        [mine_act] + [((n, GL), F32, whole((n, GL)))] * ngroup,
        "dkey", 1,
    )(me, lk, fv, r_in, sk)

    dk_got = [dk_send[0]] + [swap(dk_send[k], k) for k in range(1, ngroup)]
    side = lax.axis_size("x")
    per = d // nxy
    dq_got, _ = tie((dq_got, dk))
    at_y = lambda depth: pl.BlockSpec(
        (side, 1, per, depth), lambda k, y: (0, jnp.bitwise_xor(y[0], k), 0, 0)
    )
    by_xy = lambda v: v.reshape(side, side, per, v.shape[-1])
    qshape = (side, per + 8, GL)
    tall, *gq_send = call_mine(
        wgrad_q_kernel,
        [at_y(n)] * 4 + [whole((n + 8, GL))] * 4,
        [((side, side, per, 4 * n), BF, at_y(4 * n))] + [(qshape, F32, whole(qshape))] * side,
        "wgradq", 2 * big, side,
    )(own("y"), by_xy(t0), by_xy(t1), by_xy(t2), by_xy(t3), *dq_got)
    gq_got = [gq_send[0]] + [turn_about("y", gq_send[k], k) for k in range(1, side)]

    steps = 2
    kshape = (nxy, per, GL)
    (gk,) = call(
        wgrad_k_kernel, (steps,), [row(d // steps, 4 * n)] + [whole((n, GL))] * 4,
        [(kshape, F32, pl.BlockSpec((nxy // steps,) + kshape[1:], lambda g: (g, 0, 0)))],
        "wgradk", 400 * big,
    )(tall.reshape(d, 4 * n), *dk_got)
    gk_parts = lax.all_to_all(gk, ("x", "y"), 0, 0, tiled=True)

    dn_5, _ = tie((dn, gk))
    mo, lv = call(
        local_v_kernel, (halves,),
        [whole((n, d)), col(d, w), col(n, w), col(n, w), col(n, w)], [act(BF), act(F32)], "localv", 400 * big,
    )(at, w_out, dn_5, fq, fk)
    gq_got, _ = tie((gq_got, gk))
    gq_send = call(
        sum_y_kernel, (), [SMEM] + [whole(qshape)] * side,
        [(qshape[1:], F32, whole(qshape[1:]))] * side, "sumy", 1 << 22,
    )(own("x"), *gq_got)
    gq_got = [gq_send[0]] + [turn_about("x", gq_send[k], k) for k in range(1, side)]
    gk_parts, mo, lv, gq_got = tie((gk_parts, mo, lv, gq_got))

    last = ("c", "w", "b")
    nlast = lax.axis_size(last)
    each = per // nlast
    jshape = (nlast, 2 * each, GL + 128)
    (both,) = call(
        join_kernel, (), [whole(qshape[1:])] * side + [whole(kshape)],
        [(jshape, F32, whole(jshape))], "join", 1 << 22,
    )(*gq_got, gk_parts)
    dk_6, _ = tie((dk, both))
    both = lax.all_to_all(both, last, 0, 0, tiled=True)

    (dt,) = call(
        dtok_kernel, (halves,),
        [col(n, w), col(n, w), st_spec, col(n, w), col(n, w), col(d, w), col(d, w), col(d, w)],
        [((n, d), BF, whole((n, d)))], "dtok", 1,
        scratch=[pltpu.VMEM((n, d), F32)],
    )(lv, fk, r_in, dq, dk_6, w_query, w_key, w_value)
    dw, dg = call(
        final_kernel, (), [whole(jshape)],
        [((2, each * d), F32, whole((2, each * d))), ((8, 128), F32, whole((8, 128)))],
        "final", 1 << 20,
    )(both)
    return mo.reshape(1, n, d), dt.reshape(1, n, d), dw, dg.reshape(d)


def solution(mesh):
    fine = Mesh(mesh.devices.reshape(4, 4, 2, 4, 2), ("x", "y", "c", "w", "b"))
    acts = P(("w", "b"), SEQ, None)
    placed = (acts, P(), P(), P(), P(), P(), P(("w", "b")), acts)
    return jax.shard_map(
        on_device,
        mesh=fine,
        in_specs=placed,
        out_specs=(acts, acts, P(None, ("x", "y", "c", "w", "b")), P()),
        check_vma=False,
    )
```

```python
import functools

import jax
import jax.numpy as jnp
from jax import lax
from jax.experimental import pallas as pl
from jax.experimental.pallas import tpu as pltpu
from jax.sharding import Mesh, PartitionSpec as P

EPS = 1e-05
HD = 64
GL = 256
F32 = jnp.float32
BF = jnp.bfloat16
NN = (((1,), (0,)), ((), ()))
NT = (((1,), (1,)), ((), ()))
TN = (((0,), (0,)), ((), ()))
SEQ = ("x", "y", "c")
GROUP = ("c", "b")
VMEM_LIMIT = 64 * 1024 * 1024
GRANT = {name: 58 << 20 for name in ("turn", "query", "dquery")}
GRANT.update({name: 4 << 20 for name in ("prefix", "suffix", "final")})


def dot(a, b, dims=NN):
    return lax.dot_general(a, b, dims, preferred_element_type=F32)


def split(v):
    hi = v.astype(BF)
    return hi, (v - hi.astype(F32)).astype(BF)


def lanes(shape):
    return lax.broadcasted_iota(jnp.int32, shape, 1)


def rows(shape):
    return lax.broadcasted_iota(jnp.int32, shape, 0)


def head_masks(shape):
    which = lanes(shape) // HD
    return [which == h for h in range(GL // HD)]


def pick(mask, v):
    return jnp.where(mask, v, jnp.zeros_like(v))


def pack_state(full):
    out = []
    for p in range(GL // 128):
        blk = full[128 * p:128 * p + 128, 128 * p:128 * p + 128]
        out.append(jnp.where(lanes((HD, 128)) < HD, blk[:HD], blk[HD:]))
    return jnp.concatenate(out, axis=0)


def unpack_state(st):
    zero = jnp.zeros((128, 128), st.dtype)
    blks = []
    for p in range(GL // 128):
        a = st[HD * p:HD * p + HD]
        first = lanes((HD, 128)) < HD
        blks.append(jnp.concatenate([pick(first, a), pick(~first, a)], axis=0))
    return jnp.concatenate(
        [
            jnp.concatenate([blks[0], zero], axis=1),
            jnp.concatenate([zero, blks[1]], axis=1),
        ],
        axis=0,
    )


def valid_rows(nv_ref, count):
    return (rows((count, 1)) < nv_ref[0]).astype(F32)


def features(raw):
    ex = jnp.exp(jnp.minimum(raw, 0.0))
    up = raw > 0
    return jnp.where(up, raw + 1.0, ex), jnp.where(up, 1.0, ex)


def head_mean(*parts):
    same = (rows((GL, GL)) // HD == lanes((GL, GL)) // HD).astype(BF)
    total = dot(parts[0], same)
    for p in parts[1:]:
        total = total + dot(p, same)
    return total * (1.0 / HD)


def groups_of(ref):
    return [(j, slice(GL * j, GL * j + GL)) for j in range(ref.shape[-1] // GL)]


def my_groups(me_ref, step):
    for i in range(2):
        at = jnp.bitwise_xor(jnp.bitwise_and(me_ref[0], 1), i)
        yield (
            2 * step + i,
            pl.ds(pl.multiple_of(at * GL, GL), GL),
            pl.ds(pl.multiple_of(at * 128, 128), 128),
        )


def each_step(body):
    for step in range(2):
        pl.when(pl.program_id(0) == step)(functools.partial(body, step))


def kv_kernel(nv_ref, tok, wk, wv, fk_o, fv_o, sk_o, st_o):
    n = tok.shape[0]
    valid = valid_rows(nv_ref, n)
    feat, slope = features(dot(tok[...], wk[...]))
    fk = (feat * valid).astype(BF)
    fv = dot(tok[...], wv[...]).astype(BF)
    fk_o[...] = fk
    fv_o[...] = fv
    sk_o[...] = slope * valid
    for j, c in groups_of(fk):
        st_o[128 * j:128 * j + 128, :] = pack_state(dot(fk[:, c], fv[:, c], TN))


def turn_kernel(tok, t16_o, t32_o):
    n = tok.shape[0]
    eye = (rows((n, n)) == lanes((n, n))).astype(BF)
    res = dot(tok[...], eye, TN)
    t16_o[...] = res.astype(BF)
    t32_o[...] = res


def q_kernel(tok, wq, fq_o, fqt_o, sq_o):
    feat, slope = features(dot(tok[...], wq[...]))
    fq = feat.astype(BF)
    fq_o[...] = fq
    sq_o[...] = slope
    eye = (rows((GL, GL)) == lanes((GL, GL))).astype(BF)
    for _, c in groups_of(fq):
        fqt_o[c, :] = dot(eye, fq[:, c], NT).astype(BF)


def numer_kernel(fq, fk, fv, dm, wo, nl_o, do_o):
    n = fq.shape[0]
    do_o[...] = dot(dm[...], wo[...], NT)
    causal = rows((n, n)) >= lanes((n, n))
    for _, c in groups_of(fq):
        total = jnp.zeros((n, GL), F32)
        for m in head_masks((n, GL)):
            s = pick(causal, dot(pick(m, fq[:, c]), fk[:, c], NT)).astype(BF)
            total = total + dot(s, pick(m, fv[:, c]))
        nl_o[:, c] = total


def norm_kernel(nv_ref, nl, st, fq, fqt, do, gain, at_o, dn_o, rs_o, gp_o):
    n = nl.shape[0]
    valid = valid_rows(nv_ref, n)
    for j, c in groups_of(nl):
        r = slice(128 * j, 128 * j + 128)
        s_hi, s_lo = split(unpack_state(st[r, :]))
        numer = nl[:, c] + dot(fq[:, c], s_hi) + dot(fq[:, c], s_lo)
        inv = lax.rsqrt(head_mean((numer * numer).astype(BF)) + EPS)
        normed = numer * inv
        scale = gain[:, c]
        at_o[:, c] = (normed * scale * valid).astype(BF)
        dov = do[:, c] * valid
        gp_o[:, c] = jnp.sum((dov * normed).reshape(n // 8, 8, GL), axis=0)
        g = dov * scale
        dn = inv * (g - normed * head_mean(*split(g * normed)))
        dn_o[:, c] = dn
        d_hi, d_lo = split(dn)
        rs_o[r, :] = pack_state(dot(fqt[c, :], d_hi) + dot(fqt[c, :], d_lo))


def dq_kernel(me_ref, dn, st, fk, fv, sq, gp, dq_o, *send):
    n = dn.shape[0]

    def body(step):
        causal = rows((n, n)) >= lanes((n, n))
        for k, c, r in my_groups(me_ref, step):
            s_hi, s_lo = split(unpack_state(st[r, :]))
            d_hi, d_lo = split(dn[:, c])
            total = dot(d_hi, s_hi, NT) + dot(d_lo, s_hi, NT) + dot(d_hi, s_lo, NT)
            keys, values = fk[:, c], fv[:, c]
            for m in head_masks((n, GL)):
                vm = pick(m, values)
                w = pick(causal, dot(d_hi, vm, NT) + dot(d_lo, vm, NT)).astype(BF)
                total = total + dot(w, pick(m, keys))
            dq = (total * sq[:, c]).astype(BF)
            dq_o[:, c] = dq
            send[k][0:n, :] = dq.astype(F32)
            send[k][n:n + 8, :] = gp[:, c]

    each_step(body)


def local_k_kernel(dn, fq, fv, lk_o):
    n = dn.shape[0]
    later = lanes((n, n)) >= rows((n, n))
    for _, c in groups_of(dn):
        d_hi, d_lo = split(dn[:, c])
        total = jnp.zeros((n, GL), F32)
        for m in head_masks((n, GL)):
            vm = pick(m, fv[:, c])
            w = pick(later, dot(vm, d_hi, NT) + dot(vm, d_lo, NT)).astype(BF)
            total = total + dot(w, pick(m, fq[:, c]))
        lk_o[:, c] = total


def local_v_kernel(at, wo, dn, fq, fk, mo_o, lv_o):
    n = dn.shape[0]
    mo_o[...] = dot(at[...], wo[...]).astype(BF)
    later = lanes((n, n)) >= rows((n, n))
    for _, c in groups_of(dn):
        d_hi = dn[:, c].astype(BF)
        total = jnp.zeros((n, GL), F32)
        for m in head_masks((n, GL)):
            s = pick(later, dot(pick(m, fk[:, c]), fq[:, c], NT)).astype(BF)
            total = total + dot(s, pick(m, d_hi))
        lv_o[:, c] = total


def dk_kernel(first, me_ref, lk, fv, st, sk, dk_o, *send):
    for k, c, r in my_groups(me_ref, first):
        r_hi, r_lo = split(unpack_state(st[r, :]))
        total = lk[:, c] + dot(fv[:, c], r_hi, NT) + dot(fv[:, c], r_lo, NT)
        dk = (total * sk[:, c]).astype(BF)
        dk_o[:, c] = dk
        send[k - 2 * first][...] = dk.astype(F32)


def dtok_kernel(me_ref, lv, fk, st, dq, near, far, wq, wk, wv, dt_o, acc):
    dk = jnp.where(jnp.right_shift(me_ref[0], 1) == pl.program_id(0), near[...], far[...])
    term = dot(dq[...], wq[...], NT) + dot(dk, wk[...], NT)
    dv = []
    for j, c in groups_of(lv):
        r_hi, r_lo = split(unpack_state(st[128 * j:128 * j + 128, :]))
        dv.append((lv[:, c] + dot(fk[:, c], r_hi) + dot(fk[:, c], r_lo)).astype(BF))
    term = term + dot(jnp.concatenate(dv, axis=1), wv[...], NT)

    @pl.when(pl.program_id(0) == 0)
    def _():
        acc[...] = term

    @pl.when(pl.program_id(0) > 0)
    def _():
        acc[...] += term

    @pl.when(pl.program_id(0) == pl.num_programs(0) - 1)
    def _():
        dt_o[...] = acc[...].astype(BF)


def wgrad_q_kernel(y_ref, t0, t1, t2, t3, d0, d1, d2, d3, all_o, *send):
    n = t0.shape[3]
    blocks, m = t0.shape[0], t0.shape[2]

    def body(step):
        parts = [d[0:n, :].astype(BF) for d in (d0, d1, d2, d3)]
        gain = d0[n:n + 8, :] + d1[n:n + 8, :] + d2[n:n + 8, :] + d3[n:n + 8, :]
        for i in range(2):
            out = send[2 * step + i]
            at = jnp.bitwise_xor(jnp.bitwise_and(y_ref[0], 1), i)
            res = jnp.zeros((blocks * m, d0.shape[1]), F32)
            for j, t in enumerate((t0, t1, t2, t3)):
                turned = t[:, at].reshape(blocks * m, n).astype(BF)
                all_o[:, at, :, n * j:n * j + n] = turned.reshape(blocks, m, n)
                res = res + dot(turned, parts[j])
            out[:, 0:m, :] = res.reshape(blocks, m, res.shape[1])
            for block in range(blocks):
                out[block, m:m + 8, :] = gain

    each_step(body)


def sum_y_kernel(x_ref, v0, v1, v2, v3, *send):
    for k, out in enumerate(send):
        at = jnp.bitwise_xor(x_ref[0], k)
        out[...] = v0[at] + v1[at] + v2[at] + v3[at]


def wgrad_k_kernel(t, d0, d1, d2, d3, out):
    k, m, w = out.shape
    d = jnp.concatenate([v[...].astype(BF) for v in (d0, d1, d2, d3)], axis=0)
    out[...] = dot(t[...], d).reshape(k, m, w)


def prefix_kernel(backward, v, out):
    count = v.shape[0]
    order = range(count - 1, -1, -1) if backward else range(count)
    total = jnp.zeros(v.shape[1:], F32)
    for i in order:
        out[i] = total
        total = total + v[i]


def join_kernel(q0, q1, q2, q3, k, out):
    total = k[0]
    for i in range(1, k.shape[0]):
        total = total + k[i]
    height, width = total.shape
    each = out.shape[1] // 2
    q = q0[...] + q1[...] + q2[...] + q3[...]
    gain = jnp.sum(q[height:height + 8], axis=0, keepdims=True)
    parts = [gain[:, 128 * i:128 * i + 128] for i in range(width // 128)]
    parts.append(jnp.zeros((2 * each - len(parts), 128), F32))
    tile = jnp.concatenate(parts, axis=0)
    for j in range(out.shape[0]):
        out[j, 0:each, 0:width] = q[each * j:each * j + each]
        out[j, each:2 * each, 0:width] = total[each * j:each * j + each]
        out[j, :, width:width + 128] = tile


def final_kernel(v, dw_o, dg_o):
    width = v.shape[2] - 128
    each = v.shape[1] // 2
    for c in range(2):
        for b in range(2):
            g = 2 * b + c
            total = v[8 * c + b]
            for w in range(1, 4):
                total = total + v[8 * c + 2 * w + b]
            for which in range(2):
                for i in range(each):
                    r = which * each + i
                    at = 4 * width * i + width * g
                    dw_o[which:which + 1, at:at + width] = total[r:r + 1, 0:width]
            dg_o[2 * g:2 * g + 2, :] = total[0:2, width:width + 128]


def call(kernel, grid, in_specs, outs, name, flops, scratch=()):
    out_shape = [jax.ShapeDtypeStruct(s, d) for s, d, _ in outs]
    return pl.pallas_call(
        kernel,
        grid=grid,
        in_specs=in_specs,
        out_specs=[spec for _, _, spec in outs],
        out_shape=out_shape,
        scratch_shapes=list(scratch),
        name=name,
        cost_estimate=pl.CostEstimate(flops=flops, bytes_accessed=4 << 20, transcendentals=0),
        compiler_params=pltpu.CompilerParams(vmem_limit_bytes=GRANT.get(name, VMEM_LIMIT)),
    )


def call_mine(kernel, in_specs, outs, name, flops, steps=2):
    return pl.pallas_call(
        kernel,
        grid_spec=pltpu.PrefetchScalarGridSpec(
            num_scalar_prefetch=1,
            grid=(steps,),
            in_specs=in_specs,
            out_specs=[spec for _, _, spec in outs],
        ),
        out_shape=[jax.ShapeDtypeStruct(s, d) for s, d, _ in outs],
        name=name,
        cost_estimate=pl.CostEstimate(flops=flops, bytes_accessed=4 << 20, transcendentals=0),
        compiler_params=pltpu.CompilerParams(vmem_limit_bytes=GRANT.get(name, VMEM_LIMIT)),
    )


SMEM = pl.BlockSpec(memory_space=pltpu.SMEM)


def whole(shape):
    return pl.BlockSpec(shape, lambda *_: (0,) * len(shape))


def col(r, w=GL):
    return pl.BlockSpec((r, w), lambda g: (0, g))


def row(r, w):
    return pl.BlockSpec((r, w), lambda g: (g, 0))


def pair_at(step, me):
    return jnp.bitwise_xor(jnp.right_shift(me[0], 1), step)


def col_mine(r, w):
    return pl.BlockSpec((r, w), lambda step, me: (0, pair_at(step, me)))


def row_mine(r, w):
    return pl.BlockSpec((r, w), lambda step, me: (pair_at(step, me), 0))


def on_device(tokens, w_query, w_key, w_value, w_out, norm_gain, lengths, d_mixed):
    _, n, d = tokens.shape
    tok = tokens.reshape(n, d)
    dm = d_mixed.reshape(n, d)
    w = 2 * GL
    halves = d // w
    nseq = lax.axis_size(SEQ)
    nxy = lax.axis_size(("x", "y"))
    ngroup = lax.axis_size(GROUP)
    nv = lengths - lax.axis_index(SEQ) * n
    own = lambda axes: jnp.full((1,), lax.axis_index(axes), jnp.int32)
    me = 2 * own("b") + own("c")
    gain = norm_gain.reshape(1, d)
    act = lambda dt: ((n, d), dt, col(n, w))
    st_rows = d // 2
    st_spec = row(w // 2, 128)
    state = ((st_rows, 128), F32, st_spec)
    big = 2 * n * d * d

    fk, fv, sk, st1 = call(
        kv_kernel, (halves,), [SMEM, whole((n, d)), col(d, w), col(d, w)],
        [act(BF), act(BF), act(F32), state], "kv", 2 * big,
    )(nv, tok, w_key, w_value)

    tie = lax.optimization_barrier

    def to_parts(st):
        return lax.all_to_all(st.reshape(nseq, st_rows // nseq, 128), SEQ, 0, 0, tiled=True)

    def run(parts, backward, name):
        shape = parts.shape
        (mine,) = call(
            functools.partial(prefix_kernel, backward), (), [whole(shape)],
            [(shape, F32, whole(shape))], name, 1 << 20,
        )(parts)
        return mine

    def from_parts(mine):
        return lax.all_to_all(mine, SEQ, 0, 0, tiled=True).reshape(st_rows, 128)

    def swap(v, k):
        k = (k & 1) * 2 + k // 2
        return lax.ppermute(v, GROUP, [(i, i ^ k) for i in range(ngroup)])

    def turn_about(axis, v, k):
        return lax.ppermute(v, axis, [(i, i ^ k) for i in range(lax.axis_size(axis))])

    parts = to_parts(st1)
    tok_1, _ = tie((tok, st1))
    t0, t32 = call(
        turn_kernel, (halves,), [col(n, w)],
        [((d, n), BF, row(w, n)), ((d, n), F32, row(w, n))], "turn", big // 4,
    )(tok_1)
    fq, fqt, sq = call(
        q_kernel, (halves,), [whole((n, d)), col(d, w)],
        [act(BF), ((d, n), BF, row(w, n)), act(F32)], "query", big,
    )(tok_1, w_query)
    parts, fq, t0 = tie((parts, fq, t0))
    mine = run(parts, False, "prefix")

    t32, _ = tie((t32, mine))
    t1 = swap(t32, 1)
    t2 = swap(t32, 2)

    st_in = from_parts(mine)
    fq_2, _ = tie((fq, mine))
    nl, do = call(
        numer_kernel, (halves,),
        [col(n, w), col(n, w), col(n, w), whole((n, d)), row(w, d)],
        [act(F32), act(F32)], "numer", 2 * big,
    )(fq_2, fk, fv, dm, w_out)

    at, dn, rs, gp = call(
        norm_kernel, (halves,),
        [SMEM, col(n, w), st_spec, col(n, w), row(w, n), col(n, w), col(1, w)],
        [act(BF), act(F32), state, ((8, d), F32, col(8, w))], "norm", big,
    )(nv, nl, st_in, fq, fqt, do, gain)

    parts = to_parts(rs)
    dn_3, _ = tie((dn, rs))
    mine_act = ((n, d), BF, col_mine(n, w))
    dq, *dq_send = call_mine(
        dq_kernel,
        [col_mine(n, w), row_mine(w // 2, 128)] + [col_mine(n, w)] * 3 + [col_mine(8, w)],
        [mine_act] + [((n + 8, GL), F32, whole((n + 8, GL)))] * ngroup,
        "dquery", 2 * big,
    )(me, dn_3, st_in, fk, fv, sq, gp)
    parts, dq = tie((parts, dq))
    dq_got = [dq_send[0]] + [swap(dq_send[k], k) for k in range(1, ngroup)]
    mine = run(parts, True, "suffix")

    r_in = from_parts(mine)
    dn_4, t2, _ = tie((dn, t2, mine))
    t3 = swap(t2, 1)
    (lk,) = call(
        local_k_kernel, (halves,), [col(n, w), col(n, w), col(n, w)], [act(F32)], "localk", 1,
    )(dn_4, fq, fv)
    def dkey(first, lk, name):
        pair = lambda r: pl.BlockSpec((r, w), lambda _, me: (0, pair_at(first, me)))
        wide = ((n, w), BF, whole((n, w)))
        one = ((n, GL), F32, whole((n, GL)))
        st_pair = pl.BlockSpec((w // 2, 128), lambda _, me: (pair_at(first, me), 0))
        return call_mine(
            functools.partial(dk_kernel, first), [pair(n), pair(n), st_pair, pair(n)],
            [wide, one, one], name, 1, 1,
        )(me, lk, fv, r_in, sk)

    dk_far, *far = dkey(1, lk, "dkeyfar")

    far_got = [swap(far[0], 2), swap(far[1], 3)]
    side = lax.axis_size("x")
    per = d // nxy
    dq_got, _ = tie((dq_got, dk_far))
    at_y = lambda depth: pl.BlockSpec(
        (side, 2, per, depth), lambda step, y: (0, pair_at(step, y), 0, 0)
    )
    by_xy = lambda v: v.reshape(side, side, per, v.shape[-1])
    qshape = (side, per + 8, GL)
    tall, *gq_send = call_mine(
        wgrad_q_kernel,
        [at_y(n)] * 4 + [whole((n + 8, GL))] * 4,
        [((side, side, per, 4 * n), BF, at_y(4 * n))] + [(qshape, F32, whole(qshape))] * side,
        "wgradq", 2 * big,
    )(own("y"), by_xy(t0), by_xy(t1), by_xy(t2), by_xy(t3), *dq_got)
    gq_got = [gq_send[0]] + [turn_about("y", gq_send[k], k) for k in range(1, side)]

    lk_near, _ = tie((lk, gq_send[0]))
    dk_near, *near = dkey(0, lk_near, "dkeynear")
    dk_got = [near[0], swap(near[1], 1)] + far_got

    steps = 2
    kshape = (nxy, per, GL)
    (gk,) = call(
        wgrad_k_kernel, (steps,), [row(d // steps, 4 * n)] + [whole((n, GL))] * 4,
        [(kshape, F32, pl.BlockSpec((nxy // steps,) + kshape[1:], lambda g: (g, 0, 0)))],
        "wgradk", 400 * big,
    )(tall.reshape(d, 4 * n), *dk_got)
    gk_parts = lax.all_to_all(gk, ("x", "y"), 0, 0, tiled=True)

    dn_5, _ = tie((dn, gk))
    mo, lv = call(
        local_v_kernel, (halves,),
        [whole((n, d)), col(d, w), col(n, w), col(n, w), col(n, w)], [act(BF), act(F32)], "localv", 400 * big,
    )(at, w_out, dn_5, fq, fk)
    gq_got, _ = tie((gq_got, gk))
    gq_send = call(
        sum_y_kernel, (), [SMEM] + [whole(qshape)] * side,
        [(qshape[1:], F32, whole(qshape[1:]))] * side, "sumy", 1 << 22,
    )(own("x"), *gq_got)
    gq_got = [gq_send[0]] + [turn_about("x", gq_send[k], k) for k in range(1, side)]
    gk_parts, mo, lv, gq_got = tie((gk_parts, mo, lv, gq_got))

    last = ("c", "w", "b")
    nlast = lax.axis_size(last)
    each = per // nlast
    jshape = (nlast, 2 * each, GL + 128)
    (both,) = call(
        join_kernel, (), [whole(qshape[1:])] * side + [whole(kshape)],
        [(jshape, F32, whole(jshape))], "join", 1 << 22,
    )(*gq_got, gk_parts)
    lv, _ = tie((lv, both))
    both = lax.all_to_all(both, last, 0, 0, tiled=True)

    (dt,) = call(
        dtok_kernel, (halves,),
        [SMEM, col(n, w), col(n, w), st_spec, col(n, w), whole((n, w)), whole((n, w))]
        + [col(d, w)] * 3,
        [((n, d), BF, whole((n, d)))], "dtok", 1,
        scratch=[pltpu.VMEM((n, d), F32)],
    )(me, lv, fk, r_in, dq, dk_near, dk_far, w_query, w_key, w_value)
    dw, dg = call(
        final_kernel, (), [whole(jshape)],
        [((2, each * d), F32, whole((2, each * d))), ((8, 128), F32, whole((8, 128)))],
        "final", 1 << 20,
    )(both)
    return mo.reshape(1, n, d), dt.reshape(1, n, d), dw, dg.reshape(d)


def solution(mesh):
    fine = Mesh(mesh.devices.reshape(4, 4, 2, 4, 2), ("x", "y", "c", "w", "b"))
    acts = P(("w", "b"), SEQ, None)
    placed = (acts, P(), P(), P(), P(), P(), P(("w", "b")), acts)
    return jax.shard_map(
        on_device,
        mesh=fine,
        in_specs=placed,
        out_specs=(acts, acts, P(None, ("x", "y", "c", "w", "b")), P()),
        check_vma=False,
    )
```

```python
import functools

import jax
import jax.numpy as jnp
from jax import lax
from jax.experimental import pallas as pl
from jax.experimental.pallas import tpu as pltpu
from jax.sharding import Mesh, PartitionSpec as P

EPS = 1e-05
HD = 64
GL = 256
F32 = jnp.float32
BF = jnp.bfloat16
NN = (((1,), (0,)), ((), ()))
NT = (((1,), (1,)), ((), ()))
TN = (((0,), (0,)), ((), ()))
SEQ = ("x", "y", "c")
GROUP = ("c", "b")
VMEM_LIMIT = 64 * 1024 * 1024
GRANT = {name: 58 << 20 for name in ("turn", "query", "dquery")}
GRANT.update({name: 4 << 20 for name in ("prefix", "suffix", "final")})


def dot(a, b, dims=NN):
    return lax.dot_general(a, b, dims, preferred_element_type=F32)


def split(v):
    hi = v.astype(BF)
    return hi, (v - hi.astype(F32)).astype(BF)


def lanes(shape):
    return lax.broadcasted_iota(jnp.int32, shape, 1)


def rows(shape):
    return lax.broadcasted_iota(jnp.int32, shape, 0)


def head_masks(shape):
    which = lanes(shape) // HD
    return [which == h for h in range(GL // HD)]


def pick(mask, v):
    return jnp.where(mask, v, jnp.zeros_like(v))


def pack_state(full):
    out = []
    for p in range(GL // 128):
        blk = full[128 * p:128 * p + 128, 128 * p:128 * p + 128]
        out.append(jnp.where(lanes((HD, 128)) < HD, blk[:HD], blk[HD:]))
    return jnp.concatenate(out, axis=0)


def unpack_state(st):
    zero = jnp.zeros((128, 128), st.dtype)
    blks = []
    for p in range(GL // 128):
        a = st[HD * p:HD * p + HD]
        first = lanes((HD, 128)) < HD
        blks.append(jnp.concatenate([pick(first, a), pick(~first, a)], axis=0))
    return jnp.concatenate(
        [
            jnp.concatenate([blks[0], zero], axis=1),
            jnp.concatenate([zero, blks[1]], axis=1),
        ],
        axis=0,
    )


def valid_rows(nv_ref, count):
    return (rows((count, 1)) < nv_ref[0]).astype(F32)


def features(raw):
    ex = jnp.exp(jnp.minimum(raw, 0.0))
    up = raw > 0
    return jnp.where(up, raw + 1.0, ex), jnp.where(up, 1.0, ex)


def head_mean(*parts):
    same = (rows((GL, GL)) // HD == lanes((GL, GL)) // HD).astype(BF)
    total = dot(parts[0], same)
    for p in parts[1:]:
        total = total + dot(p, same)
    return total * (1.0 / HD)


def groups_of(ref):
    return [(j, slice(GL * j, GL * j + GL)) for j in range(ref.shape[-1] // GL)]


def my_groups(me_ref, step):
    for i in range(2):
        at = jnp.bitwise_xor(jnp.bitwise_and(me_ref[0], 1), i)
        yield (
            2 * step + i,
            pl.ds(pl.multiple_of(at * GL, GL), GL),
            pl.ds(pl.multiple_of(at * 128, 128), 128),
        )


def each_step(body):
    for step in range(2):
        pl.when(pl.program_id(0) == step)(functools.partial(body, step))


def kv_kernel(nv_ref, tok, wk, wv, fk_o, fv_o, sk_o, st_o):
    n = tok.shape[0]
    valid = valid_rows(nv_ref, n)
    feat, slope = features(dot(tok[...], wk[...]))
    fk = (feat * valid).astype(BF)
    fv = dot(tok[...], wv[...]).astype(BF)
    fk_o[...] = fk
    fv_o[...] = fv
    sk_o[...] = slope * valid
    for j, c in groups_of(fk):
        st_o[128 * j:128 * j + 128, :] = pack_state(dot(fk[:, c], fv[:, c], TN))


def turn_kernel(tok, t16_o, t32_o):
    n = tok.shape[0]
    eye = (rows((n, n)) == lanes((n, n))).astype(BF)
    res = dot(tok[...], eye, TN)
    t16_o[...] = res.astype(BF)
    t32_o[...] = res


def q_kernel(tok, wq, fq_o, fqt_o, sq_o):
    feat, slope = features(dot(tok[...], wq[...]))
    fq = feat.astype(BF)
    fq_o[...] = fq
    sq_o[...] = slope
    eye = (rows((GL, GL)) == lanes((GL, GL))).astype(BF)
    for _, c in groups_of(fq):
        fqt_o[c, :] = dot(eye, fq[:, c], NT).astype(BF)


def numer_kernel(fq, fk, fv, dm, wo, nl_o, do_o):
    n = fq.shape[0]
    do_o[...] = dot(dm[...], wo[...], NT)
    causal = rows((n, n)) >= lanes((n, n))
    for _, c in groups_of(fq):
        total = jnp.zeros((n, GL), F32)
        for m in head_masks((n, GL)):
            s = pick(causal, dot(pick(m, fq[:, c]), fk[:, c], NT)).astype(BF)
            total = total + dot(s, pick(m, fv[:, c]))
        nl_o[:, c] = total


def norm_kernel(nv_ref, nl, st, fq, fqt, do, gain, at_o, dn_o, rs_o, gp_o):
    n = nl.shape[0]
    valid = valid_rows(nv_ref, n)
    for j, c in groups_of(nl):
        r = slice(128 * j, 128 * j + 128)
        s_hi, s_lo = split(unpack_state(st[r, :]))
        numer = nl[:, c] + dot(fq[:, c], s_hi) + dot(fq[:, c], s_lo)
        inv = lax.rsqrt(head_mean((numer * numer).astype(BF)) + EPS)
        normed = numer * inv
        scale = gain[:, c]
        at_o[:, c] = (normed * scale * valid).astype(BF)
        dov = do[:, c] * valid
        gp_o[:, c] = jnp.sum((dov * normed).reshape(n // 8, 8, GL), axis=0)
        g = dov * scale
        dn = inv * (g - normed * head_mean(*split(g * normed)))
        dn_o[:, c] = dn
        d_hi, d_lo = split(dn)
        rs_o[r, :] = pack_state(dot(fqt[c, :], d_hi) + dot(fqt[c, :], d_lo))


def dq_kernel(me_ref, dn, st, fk, fv, sq, gp, dq_o, *send):
    n = dn.shape[0]

    def body(step):
        causal = rows((n, n)) >= lanes((n, n))
        for k, c, r in my_groups(me_ref, step):
            s_hi, s_lo = split(unpack_state(st[r, :]))
            d_hi, d_lo = split(dn[:, c])
            total = dot(d_hi, s_hi, NT) + dot(d_lo, s_hi, NT) + dot(d_hi, s_lo, NT)
            keys, values = fk[:, c], fv[:, c]
            for m in head_masks((n, GL)):
                vm = pick(m, values)
                w = pick(causal, dot(d_hi, vm, NT) + dot(d_lo, vm, NT)).astype(BF)
                total = total + dot(w, pick(m, keys))
            dq = (total * sq[:, c]).astype(BF)
            dq_o[:, c] = dq
            send[k][0:n, :] = dq.astype(F32)
            send[k][n:n + 8, :] = gp[:, c]

    each_step(body)


def local_k_kernel(dn, fq, fv, lk_o):
    n = dn.shape[0]
    later = lanes((n, n)) >= rows((n, n))
    for _, c in groups_of(dn):
        d_hi, d_lo = split(dn[:, c])
        total = jnp.zeros((n, GL), F32)
        for m in head_masks((n, GL)):
            vm = pick(m, fv[:, c])
            w = pick(later, dot(vm, d_hi, NT) + dot(vm, d_lo, NT)).astype(BF)
            total = total + dot(w, pick(m, fq[:, c]))
        lk_o[:, c] = total


def local_v_kernel(at, wo, dn, fq, fk, mo_o, lv_o):
    n = dn.shape[0]
    mo_o[...] = dot(at[...], wo[...]).astype(BF)
    later = lanes((n, n)) >= rows((n, n))
    for _, c in groups_of(dn):
        d_hi = dn[:, c].astype(BF)
        total = jnp.zeros((n, GL), F32)
        for m in head_masks((n, GL)):
            s = pick(later, dot(pick(m, fk[:, c]), fq[:, c], NT)).astype(BF)
            total = total + dot(s, pick(m, d_hi))
        lv_o[:, c] = total


def dk_kernel(me_ref, lk, fv, st, sk, dk_o, *send):
    def body(step):
        for k, c, r in my_groups(me_ref, step):
            r_hi, r_lo = split(unpack_state(st[r, :]))
            total = lk[:, c] + dot(fv[:, c], r_hi, NT) + dot(fv[:, c], r_lo, NT)
            dk = (total * sk[:, c]).astype(BF)
            dk_o[:, c] = dk
            send[k][...] = dk.astype(F32)

    each_step(body)


def dtok_kernel(lv, fk, st, dq, dk, wq, wk, wv, dt_o, acc):
    term = dot(dq[...], wq[...], NT) + dot(dk[...], wk[...], NT)
    dv = []
    for j, c in groups_of(lv):
        r_hi, r_lo = split(unpack_state(st[128 * j:128 * j + 128, :]))
        dv.append((lv[:, c] + dot(fk[:, c], r_hi) + dot(fk[:, c], r_lo)).astype(BF))
    term = term + dot(jnp.concatenate(dv, axis=1), wv[...], NT)

    @pl.when(pl.program_id(0) == 0)
    def _():
        acc[...] = term

    @pl.when(pl.program_id(0) > 0)
    def _():
        acc[...] += term

    @pl.when(pl.program_id(0) == pl.num_programs(0) - 1)
    def _():
        dt_o[...] = acc[...].astype(BF)


def wgrad_q_kernel(y_ref, t0, t1, t2, t3, d0, d1, d2, d3, all_o, *send):
    n = t0.shape[3]
    blocks, m = t0.shape[0], t0.shape[2]

    def body(step):
        parts = [d[0:n, :].astype(BF) for d in (d0, d1, d2, d3)]
        gain = d0[n:n + 8, :] + d1[n:n + 8, :] + d2[n:n + 8, :] + d3[n:n + 8, :]
        for i in range(2):
            out = send[2 * step + i]
            at = jnp.bitwise_xor(jnp.bitwise_and(y_ref[0], 1), i)
            res = jnp.zeros((blocks * m, d0.shape[1]), F32)
            for j, t in enumerate((t0, t1, t2, t3)):
                turned = t[:, at].reshape(blocks * m, n).astype(BF)
                all_o[:, at, :, n * j:n * j + n] = turned.reshape(blocks, m, n)
                res = res + dot(turned, parts[j])
            out[:, 0:m, :] = res.reshape(blocks, m, res.shape[1])
            for block in range(blocks):
                out[block, m:m + 8, :] = gain

    each_step(body)


def sum_y_kernel(x_ref, v0, v1, v2, v3, *send):
    for k, out in enumerate(send):
        at = jnp.bitwise_xor(x_ref[0], k)
        out[...] = v0[at] + v1[at] + v2[at] + v3[at]


def wgrad_k_kernel(t, d0, d1, d2, d3, out):
    k, m, w = out.shape
    d = jnp.concatenate([v[...].astype(BF) for v in (d0, d1, d2, d3)], axis=0)
    out[...] = dot(t[...], d).reshape(k, m, w)


def prefix_kernel(backward, v, out):
    count = v.shape[0]
    order = range(count - 1, -1, -1) if backward else range(count)
    total = jnp.zeros(v.shape[1:], F32)
    for i in order:
        out[i] = total
        total = total + v[i]


def join_kernel(q0, q1, q2, q3, k, out):
    total = k[0]
    for i in range(1, k.shape[0]):
        total = total + k[i]
    height, width = total.shape
    each = out.shape[1] // 2
    q = q0[...] + q1[...] + q2[...] + q3[...]
    gain = jnp.sum(q[height:height + 8], axis=0, keepdims=True)
    parts = [gain[:, 128 * i:128 * i + 128] for i in range(width // 128)]
    parts.append(jnp.zeros((2 * each - len(parts), 128), F32))
    tile = jnp.concatenate(parts, axis=0)
    for j in range(out.shape[0]):
        out[j, 0:each, 0:width] = q[each * j:each * j + each]
        out[j, each:2 * each, 0:width] = total[each * j:each * j + each]
        out[j, :, width:width + 128] = tile


def final_kernel(v, dw_o, dg_o):
    width = v.shape[2] - 128
    each = v.shape[1] // 2
    for c in range(2):
        for b in range(2):
            g = 2 * c + b
            total = v[8 * c + b]
            for w in range(1, 4):
                total = total + v[8 * c + 2 * w + b]
            for which in range(2):
                for i in range(each):
                    r = which * each + i
                    at = 4 * width * i + width * g
                    dw_o[which:which + 1, at:at + width] = total[r:r + 1, 0:width]
            dg_o[2 * g:2 * g + 2, :] = total[0:2, width:width + 128]


def call(kernel, grid, in_specs, outs, name, flops, scratch=()):
    out_shape = [jax.ShapeDtypeStruct(s, d) for s, d, _ in outs]
    return pl.pallas_call(
        kernel,
        grid=grid,
        in_specs=in_specs,
        out_specs=[spec for _, _, spec in outs],
        out_shape=out_shape,
        scratch_shapes=list(scratch),
        name=name,
        cost_estimate=pl.CostEstimate(flops=flops, bytes_accessed=4 << 20, transcendentals=0),
        compiler_params=pltpu.CompilerParams(vmem_limit_bytes=GRANT.get(name, VMEM_LIMIT)),
    )


def call_mine(kernel, in_specs, outs, name, flops, steps=2):
    return pl.pallas_call(
        kernel,
        grid_spec=pltpu.PrefetchScalarGridSpec(
            num_scalar_prefetch=1,
            grid=(steps,),
            in_specs=in_specs,
            out_specs=[spec for _, _, spec in outs],
        ),
        out_shape=[jax.ShapeDtypeStruct(s, d) for s, d, _ in outs],
        name=name,
        cost_estimate=pl.CostEstimate(flops=flops, bytes_accessed=4 << 20, transcendentals=0),
        compiler_params=pltpu.CompilerParams(vmem_limit_bytes=GRANT.get(name, VMEM_LIMIT)),
    )


SMEM = pl.BlockSpec(memory_space=pltpu.SMEM)


def whole(shape):
    return pl.BlockSpec(shape, lambda *_: (0,) * len(shape))


def col(r, w=GL):
    return pl.BlockSpec((r, w), lambda g: (0, g))


def row(r, w):
    return pl.BlockSpec((r, w), lambda g: (g, 0))


def pair_at(step, me):
    return jnp.bitwise_xor(jnp.right_shift(me[0], 1), step)


def col_mine(r, w):
    return pl.BlockSpec((r, w), lambda step, me: (0, pair_at(step, me)))


def row_mine(r, w):
    return pl.BlockSpec((r, w), lambda step, me: (pair_at(step, me), 0))


def on_device(tokens, w_query, w_key, w_value, w_out, norm_gain, lengths, d_mixed):
    _, n, d = tokens.shape
    tok = tokens.reshape(n, d)
    dm = d_mixed.reshape(n, d)
    w = 2 * GL
    halves = d // w
    nseq = lax.axis_size(SEQ)
    nxy = lax.axis_size(("x", "y"))
    ngroup = lax.axis_size(GROUP)
    nv = lengths - lax.axis_index(SEQ) * n
    own = lambda axes: jnp.full((1,), lax.axis_index(axes), jnp.int32)
    me = own(GROUP)
    gain = norm_gain.reshape(1, d)
    act = lambda dt: ((n, d), dt, col(n, w))
    st_rows = d // 2
    st_spec = row(w // 2, 128)
    state = ((st_rows, 128), F32, st_spec)
    big = 2 * n * d * d

    fk, fv, sk, st1 = call(
        kv_kernel, (halves,), [SMEM, whole((n, d)), col(d, w), col(d, w)],
        [act(BF), act(BF), act(F32), state], "kv", 2 * big,
    )(nv, tok, w_key, w_value)

    tie = lax.optimization_barrier

    def to_parts(st):
        return lax.all_to_all(st.reshape(nseq, st_rows // nseq, 128), SEQ, 0, 0, tiled=True)

    def run(parts, backward, name):
        shape = parts.shape
        (mine,) = call(
            functools.partial(prefix_kernel, backward), (), [whole(shape)],
            [(shape, F32, whole(shape))], name, 1 << 20,
        )(parts)
        return mine

    def from_parts(mine):
        return lax.all_to_all(mine, SEQ, 0, 0, tiled=True).reshape(st_rows, 128)

    def swap(v, k):
        return lax.ppermute(v, GROUP, [(i, i ^ k) for i in range(ngroup)])

    def turn_about(axis, v, k):
        return lax.ppermute(v, axis, [(i, i ^ k) for i in range(lax.axis_size(axis))])

    parts = to_parts(st1)
    tok_1, _ = tie((tok, st1))
    t0, t32 = call(
        turn_kernel, (halves,), [col(n, w)],
        [((d, n), BF, row(w, n)), ((d, n), F32, row(w, n))], "turn", big // 4,
    )(tok_1)
    fq, fqt, sq = call(
        q_kernel, (halves,), [whole((n, d)), col(d, w)],
        [act(BF), ((d, n), BF, row(w, n)), act(F32)], "query", big,
    )(tok_1, w_query)
    parts, fq, t0 = tie((parts, fq, t0))
    mine = run(parts, False, "prefix")

    t32, _ = tie((t32, mine))
    t1 = swap(t32, 1)
    t2 = swap(t32, 2)

    st_in = from_parts(mine)
    fq_2, _ = tie((fq, mine))
    nl, do = call(
        numer_kernel, (halves,),
        [col(n, w), col(n, w), col(n, w), whole((n, d)), row(w, d)],
        [act(F32), act(F32)], "numer", 2 * big,
    )(fq_2, fk, fv, dm, w_out)

    at, dn, rs, gp = call(
        norm_kernel, (halves,),
        [SMEM, col(n, w), st_spec, col(n, w), row(w, n), col(n, w), col(1, w)],
        [act(BF), act(F32), state, ((8, d), F32, col(8, w))], "norm", big,
    )(nv, nl, st_in, fq, fqt, do, gain)

    parts = to_parts(rs)
    dn_3, _ = tie((dn, rs))
    mine_act = ((n, d), BF, col_mine(n, w))
    dq, *dq_send = call_mine(
        dq_kernel,
        [col_mine(n, w), row_mine(w // 2, 128)] + [col_mine(n, w)] * 3 + [col_mine(8, w)],
        [mine_act] + [((n + 8, GL), F32, whole((n + 8, GL)))] * ngroup,
        "dquery", 2 * big,
    )(me, dn_3, st_in, fk, fv, sq, gp)
    parts, dq = tie((parts, dq))
    dq_got = [dq_send[0]] + [swap(dq_send[k], k) for k in range(1, ngroup)]
    mine = run(parts, True, "suffix")

    r_in = from_parts(mine)
    dn_4, t1, _ = tie((dn, t1, mine))
    t3 = swap(t1, 2)
    (lk,) = call(
        local_k_kernel, (halves,), [col(n, w), col(n, w), col(n, w)], [act(F32)], "localk", 1,
    )(dn_4, fq, fv)
    dk, *dk_send = call_mine(
        dk_kernel,
        [col_mine(n, w), col_mine(n, w), row_mine(w // 2, 128), col_mine(n, w)],
        [mine_act] + [((n, GL), F32, whole((n, GL)))] * ngroup,
        "dkey", 1,
    )(me, lk, fv, r_in, sk)

    dk_got = [dk_send[0]] + [swap(dk_send[k], k) for k in range(1, ngroup)]
    side = lax.axis_size("x")
    per = d // nxy
    dq_got, _ = tie((dq_got, dk))
    at_y = lambda depth: pl.BlockSpec(
        (side, 2, per, depth), lambda step, y: (0, pair_at(step, y), 0, 0)
    )
    by_xy = lambda v: v.reshape(side, side, per, v.shape[-1])
    qshape = (side, per + 8, GL)
    tall, *gq_send = call_mine(
        wgrad_q_kernel,
        [at_y(n)] * 4 + [whole((n + 8, GL))] * 4,
        [((side, side, per, 4 * n), BF, at_y(4 * n))] + [(qshape, F32, whole(qshape))] * side,
        "wgradq", 2 * big,
    )(own("y"), by_xy(t0), by_xy(t1), by_xy(t2), by_xy(t3), *dq_got)
    gq_got = [gq_send[0]] + [turn_about("y", gq_send[k], k) for k in range(1, side)]

    steps = 2
    kshape = (nxy, per, GL)
    (gk,) = call(
        wgrad_k_kernel, (steps,), [row(d // steps, 4 * n)] + [whole((n, GL))] * 4,
        [(kshape, F32, pl.BlockSpec((nxy // steps,) + kshape[1:], lambda g: (g, 0, 0)))],
        "wgradk", 400 * big,
    )(tall.reshape(d, 4 * n), *dk_got)
    gk_parts = lax.all_to_all(gk, ("x", "y"), 0, 0, tiled=True)

    dn_5, _ = tie((dn, gk))
    mo, lv = call(
        local_v_kernel, (halves,),
        [whole((n, d)), col(d, w), col(n, w), col(n, w), col(n, w)], [act(BF), act(F32)], "localv", 400 * big,
    )(at, w_out, dn_5, fq, fk)
    gq_got, _ = tie((gq_got, gk))
    gq_send = call(
        sum_y_kernel, (), [SMEM] + [whole(qshape)] * side,
        [(qshape[1:], F32, whole(qshape[1:]))] * side, "sumy", 1 << 22,
    )(own("x"), *gq_got)
    gq_got = [gq_send[0]] + [turn_about("x", gq_send[k], k) for k in range(1, side)]
    gk_parts, mo, lv, gq_got = tie((gk_parts, mo, lv, gq_got))

    last = ("c", "w", "b")
    nlast = lax.axis_size(last)
    each = per // nlast
    jshape = (nlast, 2 * each, GL + 128)
    (both,) = call(
        join_kernel, (), [whole(qshape[1:])] * side + [whole(kshape)],
        [(jshape, F32, whole(jshape))], "join", 1 << 22,
    )(*gq_got, gk_parts)
    dk_6, _ = tie((dk, both))
    both = lax.all_to_all(both, last, 0, 0, tiled=True)

    (dt,) = call(
        dtok_kernel, (halves,),
        [col(n, w), col(n, w), st_spec, col(n, w), col(n, w), col(d, w), col(d, w), col(d, w)],
        [((n, d), BF, whole((n, d)))], "dtok", 1,
        scratch=[pltpu.VMEM((n, d), F32)],
    )(lv, fk, r_in, dq, dk_6, w_query, w_key, w_value)
    dw, dg = call(
        final_kernel, (), [whole(jshape)],
        [((2, each * d), F32, whole((2, each * d))), ((8, 128), F32, whole((8, 128)))],
        "final", 1 << 20,
    )(both)
    return mo.reshape(1, n, d), dt.reshape(1, n, d), dw, dg.reshape(d)


def solution(mesh):
    fine = Mesh(mesh.devices.reshape(4, 4, 2, 4, 2), ("x", "y", "c", "w", "b"))
    acts = P(("w", "b"), SEQ, None)
    placed = (acts, P(), P(), P(), P(), P(), P(("w", "b")), acts)
    return jax.shard_map(
        on_device,
        mesh=fine,
        in_specs=placed,
        out_specs=(acts, acts, P(None, ("x", "y", "c", "w", "b")), P()),
        check_vma=False,
    )
```

```python
import functools

import jax
import jax.numpy as jnp
from jax import lax
from jax.experimental import pallas as pl
from jax.experimental.pallas import tpu as pltpu
from jax.sharding import Mesh, PartitionSpec as P

EPS = 1e-05
HD = 64
GL = 256
F32 = jnp.float32
BF = jnp.bfloat16
NN = (((1,), (0,)), ((), ()))
NT = (((1,), (1,)), ((), ()))
TN = (((0,), (0,)), ((), ()))
SEQ = ("x", "y", "c")
GROUP = ("c", "b")
VMEM_LIMIT = 64 * 1024 * 1024
GRANT = {name: 58 << 20 for name in ("turn", "query", "dquery")}
GRANT.update({name: 4 << 20 for name in ("prefix", "suffix", "final")})


def dot(a, b, dims=NN):
    return lax.dot_general(a, b, dims, preferred_element_type=F32)


def split(v):
    hi = v.astype(BF)
    return hi, (v - hi.astype(F32)).astype(BF)


def lanes(shape):
    return lax.broadcasted_iota(jnp.int32, shape, 1)


def rows(shape):
    return lax.broadcasted_iota(jnp.int32, shape, 0)


def head_masks(shape):
    which = lanes(shape) // HD
    return [which == h for h in range(GL // HD)]


def pick(mask, v):
    return jnp.where(mask, v, jnp.zeros_like(v))


def pack_state(full):
    out = []
    for p in range(GL // 128):
        blk = full[128 * p:128 * p + 128, 128 * p:128 * p + 128]
        out.append(jnp.where(lanes((HD, 128)) < HD, blk[:HD], blk[HD:]))
    return jnp.concatenate(out, axis=0)


def unpack_state(st):
    zero = jnp.zeros((128, 128), st.dtype)
    blks = []
    for p in range(GL // 128):
        a = st[HD * p:HD * p + HD]
        first = lanes((HD, 128)) < HD
        blks.append(jnp.concatenate([pick(first, a), pick(~first, a)], axis=0))
    return jnp.concatenate(
        [
            jnp.concatenate([blks[0], zero], axis=1),
            jnp.concatenate([zero, blks[1]], axis=1),
        ],
        axis=0,
    )


def valid_rows(nv_ref, count):
    return (rows((count, 1)) < nv_ref[0]).astype(F32)


def features(raw):
    ex = jnp.exp(jnp.minimum(raw, 0.0))
    up = raw > 0
    return jnp.where(up, raw + 1.0, ex), jnp.where(up, 1.0, ex)


def head_mean(*parts):
    same = (rows((GL, GL)) // HD == lanes((GL, GL)) // HD).astype(BF)
    total = dot(parts[0], same)
    for p in parts[1:]:
        total = total + dot(p, same)
    return total * (1.0 / HD)


def groups_of(ref):
    return [(j, slice(GL * j, GL * j + GL)) for j in range(ref.shape[-1] // GL)]


def my_groups(me_ref, step):
    for i in range(2):
        at = jnp.bitwise_xor(jnp.bitwise_and(me_ref[0], 1), i)
        yield (
            2 * step + i,
            pl.ds(pl.multiple_of(at * GL, GL), GL),
            pl.ds(pl.multiple_of(at * 128, 128), 128),
        )


def each_step(body):
    for step in range(2):
        pl.when(pl.program_id(0) == step)(functools.partial(body, step))


def kv_kernel(nv_ref, tok, wk, wv, fk_o, fv_o, sk_o, st_o):
    n = tok.shape[0]
    valid = valid_rows(nv_ref, n)
    feat, slope = features(dot(tok[...], wk[...]))
    fk = (feat * valid).astype(BF)
    fv = dot(tok[...], wv[...]).astype(BF)
    fk_o[...] = fk
    fv_o[...] = fv
    sk_o[...] = slope * valid
    for j, c in groups_of(fk):
        st_o[128 * j:128 * j + 128, :] = pack_state(dot(fk[:, c], fv[:, c], TN))


def turn_kernel(tok, t16_o, t32_o):
    n = tok.shape[0]
    eye = (rows((n, n)) == lanes((n, n))).astype(BF)
    res = dot(tok[...], eye, TN)
    t16_o[...] = res.astype(BF)
    t32_o[...] = res


def q_kernel(tok, wq, fq_o, fqt_o, sq_o):
    feat, slope = features(dot(tok[...], wq[...]))
    fq = feat.astype(BF)
    fq_o[...] = fq
    sq_o[...] = slope
    eye = (rows((GL, GL)) == lanes((GL, GL))).astype(BF)
    for _, c in groups_of(fq):
        fqt_o[c, :] = dot(eye, fq[:, c], NT).astype(BF)


def numer_kernel(fq, fk, fv, dm, wo, nl_o, do_o):
    n = fq.shape[0]
    do_o[...] = dot(dm[...], wo[...], NT)
    causal = rows((n, n)) >= lanes((n, n))
    for _, c in groups_of(fq):
        total = jnp.zeros((n, GL), F32)
        for m in head_masks((n, GL)):
            s = pick(causal, dot(pick(m, fq[:, c]), fk[:, c], NT)).astype(BF)
            total = total + dot(s, pick(m, fv[:, c]))
        nl_o[:, c] = total


def norm_kernel(nv_ref, nl, st, fq, fqt, do, gain, at_o, dn_o, rs_o, gp_o):
    n = nl.shape[0]
    valid = valid_rows(nv_ref, n)
    for j, c in groups_of(nl):
        r = slice(128 * j, 128 * j + 128)
        s_hi, s_lo = split(unpack_state(st[r, :]))
        numer = nl[:, c] + dot(fq[:, c], s_hi) + dot(fq[:, c], s_lo)
        inv = lax.rsqrt(head_mean((numer * numer).astype(BF)) + EPS)
        normed = numer * inv
        scale = gain[:, c]
        at_o[:, c] = (normed * scale * valid).astype(BF)
        dov = do[:, c] * valid
        gp_o[:, c] = jnp.sum((dov * normed).reshape(n // 8, 8, GL), axis=0)
        g = dov * scale
        dn = inv * (g - normed * head_mean(*split(g * normed)))
        dn_o[:, c] = dn
        d_hi, d_lo = split(dn)
        rs_o[r, :] = pack_state(dot(fqt[c, :], d_hi) + dot(fqt[c, :], d_lo))


def dq_kernel(me_ref, dn, st, fk, fv, sq, gp, dq_o, mine, near, far):
    n = dn.shape[0]

    def body(step):
        causal = rows((n, n)) >= lanes((n, n))
        for k, c, r in my_groups(me_ref, step):
            s_hi, s_lo = split(unpack_state(st[r, :]))
            d_hi, d_lo = split(dn[:, c])
            total = dot(d_hi, s_hi, NT) + dot(d_lo, s_hi, NT) + dot(d_hi, s_lo, NT)
            keys, values = fk[:, c], fv[:, c]
            for m in head_masks((n, GL)):
                vm = pick(m, values)
                w = pick(causal, dot(d_hi, vm, NT) + dot(d_lo, vm, NT)).astype(BF)
                total = total + dot(w, pick(m, keys))
            dq = (total * sq[:, c]).astype(BF)
            dq_o[:, c] = dq
            out = (mine, far.at[0], near, far.at[1])[k]
            out[0:n, :] = dq.astype(F32)
            out[n:n + 8, :] = gp[:, c]

    each_step(body)


def local_k_kernel(dn, fq, fv, lk_o):
    n = dn.shape[0]
    later = lanes((n, n)) >= rows((n, n))
    for _, c in groups_of(dn):
        d_hi, d_lo = split(dn[:, c])
        total = jnp.zeros((n, GL), F32)
        for m in head_masks((n, GL)):
            vm = pick(m, fv[:, c])
            w = pick(later, dot(vm, d_hi, NT) + dot(vm, d_lo, NT)).astype(BF)
            total = total + dot(w, pick(m, fq[:, c]))
        lk_o[:, c] = total


def local_v_kernel(at, wo, dn, fq, fk, mo_o, lv_o):
    n = dn.shape[0]
    mo_o[...] = dot(at[...], wo[...]).astype(BF)
    later = lanes((n, n)) >= rows((n, n))
    for _, c in groups_of(dn):
        d_hi = dn[:, c].astype(BF)
        total = jnp.zeros((n, GL), F32)
        for m in head_masks((n, GL)):
            s = pick(later, dot(pick(m, fk[:, c]), fq[:, c], NT)).astype(BF)
            total = total + dot(s, pick(m, d_hi))
        lv_o[:, c] = total


def dk_kernel(me_ref, lk, fv, st, sk, dk_o, *send):
    def body(step):
        for k, c, r in my_groups(me_ref, step):
            r_hi, r_lo = split(unpack_state(st[r, :]))
            total = lk[:, c] + dot(fv[:, c], r_hi, NT) + dot(fv[:, c], r_lo, NT)
            dk = (total * sk[:, c]).astype(BF)
            dk_o[:, c] = dk
            send[k][...] = dk.astype(F32)

    each_step(body)


def dtok_kernel(lv, fk, st, dq, dk, wq, wk, wv, dt_o, acc):
    term = dot(dq[...], wq[...], NT) + dot(dk[...], wk[...], NT)
    dv = []
    for j, c in groups_of(lv):
        r_hi, r_lo = split(unpack_state(st[128 * j:128 * j + 128, :]))
        dv.append((lv[:, c] + dot(fk[:, c], r_hi) + dot(fk[:, c], r_lo)).astype(BF))
    term = term + dot(jnp.concatenate(dv, axis=1), wv[...], NT)

    @pl.when(pl.program_id(0) == 0)
    def _():
        acc[...] = term

    @pl.when(pl.program_id(0) > 0)
    def _():
        acc[...] += term

    @pl.when(pl.program_id(0) == pl.num_programs(0) - 1)
    def _():
        dt_o[...] = acc[...].astype(BF)


def wgrad_q_kernel(y_ref, t0, t1, t2, t3, d0, d1, d2, d3, all_o, *send):
    d1, d3 = d1.at[0], d3.at[0]
    n = t0.shape[3]
    blocks, m = t0.shape[0], t0.shape[2]

    def body(step):
        parts = [d[0:n, :].astype(BF) for d in (d0, d1, d2, d3)]
        gain = d0[n:n + 8, :] + d1[n:n + 8, :] + d2[n:n + 8, :] + d3[n:n + 8, :]
        for i in range(2):
            out = send[2 * step + i]
            at = jnp.bitwise_xor(jnp.bitwise_and(y_ref[0], 1), i)
            res = jnp.zeros((blocks * m, d0.shape[1]), F32)
            for j, t in enumerate((t0, t1, t2, t3)):
                turned = t[:, at].reshape(blocks * m, n).astype(BF)
                all_o[:, at, :, n * j:n * j + n] = turned.reshape(blocks, m, n)
                res = res + dot(turned, parts[j])
            out[:, 0:m, :] = res.reshape(blocks, m, res.shape[1])
            for block in range(blocks):
                out[block, m:m + 8, :] = gain

    each_step(body)


def sum_y_kernel(x_ref, v0, v1, v2, v3, *send):
    for k, out in enumerate(send):
        at = jnp.bitwise_xor(x_ref[0], k)
        out[...] = v0[at] + v1[at] + v2[at] + v3[at]


def wgrad_k_kernel(t, d0, d1, d2, d3, out):
    k, m, w = out.shape
    d = jnp.concatenate([v[...].astype(BF) for v in (d0, d1, d2, d3)], axis=0)
    out[...] = dot(t[...], d).reshape(k, m, w)


def prefix_kernel(backward, v, out):
    count = v.shape[0]
    order = range(count - 1, -1, -1) if backward else range(count)
    total = jnp.zeros(v.shape[1:], F32)
    for i in order:
        out[i] = total
        total = total + v[i]


def join_kernel(q0, q1, q2, q3, k, out):
    total = k[0]
    for i in range(1, k.shape[0]):
        total = total + k[i]
    height, width = total.shape
    each = out.shape[1] // 2
    q = q0[...] + q1[...] + q2[...] + q3[...]
    gain = jnp.sum(q[height:height + 8], axis=0, keepdims=True)
    parts = [gain[:, 128 * i:128 * i + 128] for i in range(width // 128)]
    parts.append(jnp.zeros((2 * each - len(parts), 128), F32))
    tile = jnp.concatenate(parts, axis=0)
    for j in range(out.shape[0]):
        out[j, 0:each, 0:width] = q[each * j:each * j + each]
        out[j, each:2 * each, 0:width] = total[each * j:each * j + each]
        out[j, :, width:width + 128] = tile


def final_kernel(v, dw_o, dg_o):
    width = v.shape[2] - 128
    each = v.shape[1] // 2
    for c in range(2):
        for b in range(2):
            g = 2 * c + b
            total = v[8 * c + b]
            for w in range(1, 4):
                total = total + v[8 * c + 2 * w + b]
            for which in range(2):
                for i in range(each):
                    r = which * each + i
                    at = 4 * width * i + width * g
                    dw_o[which:which + 1, at:at + width] = total[r:r + 1, 0:width]
            dg_o[2 * g:2 * g + 2, :] = total[0:2, width:width + 128]


def call(kernel, grid, in_specs, outs, name, flops, scratch=()):
    out_shape = [jax.ShapeDtypeStruct(s, d) for s, d, _ in outs]
    return pl.pallas_call(
        kernel,
        grid=grid,
        in_specs=in_specs,
        out_specs=[spec for _, _, spec in outs],
        out_shape=out_shape,
        scratch_shapes=list(scratch),
        name=name,
        cost_estimate=pl.CostEstimate(flops=flops, bytes_accessed=4 << 20, transcendentals=0),
        compiler_params=pltpu.CompilerParams(vmem_limit_bytes=GRANT.get(name, VMEM_LIMIT)),
    )


def call_mine(kernel, in_specs, outs, name, flops, steps=2):
    return pl.pallas_call(
        kernel,
        grid_spec=pltpu.PrefetchScalarGridSpec(
            num_scalar_prefetch=1,
            grid=(steps,),
            in_specs=in_specs,
            out_specs=[spec for _, _, spec in outs],
        ),
        out_shape=[jax.ShapeDtypeStruct(s, d) for s, d, _ in outs],
        name=name,
        cost_estimate=pl.CostEstimate(flops=flops, bytes_accessed=4 << 20, transcendentals=0),
        compiler_params=pltpu.CompilerParams(vmem_limit_bytes=GRANT.get(name, VMEM_LIMIT)),
    )


SMEM = pl.BlockSpec(memory_space=pltpu.SMEM)


def whole(shape):
    return pl.BlockSpec(shape, lambda *_: (0,) * len(shape))


def col(r, w=GL):
    return pl.BlockSpec((r, w), lambda g: (0, g))


def row(r, w):
    return pl.BlockSpec((r, w), lambda g: (g, 0))


def pair_at(step, me):
    return jnp.bitwise_xor(jnp.right_shift(me[0], 1), step)


def col_mine(r, w):
    return pl.BlockSpec((r, w), lambda step, me: (0, pair_at(step, me)))


def row_mine(r, w):
    return pl.BlockSpec((r, w), lambda step, me: (pair_at(step, me), 0))


def on_device(tokens, w_query, w_key, w_value, w_out, norm_gain, lengths, d_mixed):
    _, n, d = tokens.shape
    tok = tokens.reshape(n, d)
    dm = d_mixed.reshape(n, d)
    w = 2 * GL
    halves = d // w
    nseq = lax.axis_size(SEQ)
    nxy = lax.axis_size(("x", "y"))
    ngroup = lax.axis_size(GROUP)
    nv = lengths - lax.axis_index(SEQ) * n
    own = lambda axes: jnp.full((1,), lax.axis_index(axes), jnp.int32)
    me = own(GROUP)
    gain = norm_gain.reshape(1, d)
    act = lambda dt: ((n, d), dt, col(n, w))
    st_rows = d // 2
    st_spec = row(w // 2, 128)
    state = ((st_rows, 128), F32, st_spec)
    big = 2 * n * d * d

    fk, fv, sk, st1 = call(
        kv_kernel, (halves,), [SMEM, whole((n, d)), col(d, w), col(d, w)],
        [act(BF), act(BF), act(F32), state], "kv", 2 * big,
    )(nv, tok, w_key, w_value)

    tie = lax.optimization_barrier

    def to_parts(st):
        return lax.all_to_all(st.reshape(nseq, st_rows // nseq, 128), SEQ, 0, 0, tiled=True)

    def run(parts, backward, name):
        shape = parts.shape
        (mine,) = call(
            functools.partial(prefix_kernel, backward), (), [whole(shape)],
            [(shape, F32, whole(shape))], name, 1 << 20,
        )(parts)
        return mine

    def from_parts(mine):
        return lax.all_to_all(mine, SEQ, 0, 0, tiled=True).reshape(st_rows, 128)

    def swap(v, k):
        return lax.ppermute(v, GROUP, [(i, i ^ k) for i in range(ngroup)])

    def turn_about(axis, v, k):
        return lax.ppermute(v, axis, [(i, i ^ k) for i in range(lax.axis_size(axis))])

    parts = to_parts(st1)
    tok_1, _ = tie((tok, st1))
    t0, t32 = call(
        turn_kernel, (halves,), [col(n, w)],
        [((d, n), BF, row(w, n)), ((d, n), F32, row(w, n))], "turn", big // 4,
    )(tok_1)
    fq, fqt, sq = call(
        q_kernel, (halves,), [whole((n, d)), col(d, w)],
        [act(BF), ((d, n), BF, row(w, n)), act(F32)], "query", big,
    )(tok_1, w_query)
    parts, fq, t0 = tie((parts, fq, t0))
    mine = run(parts, False, "prefix")

    t32, _ = tie((t32, mine))
    t1 = swap(t32, 1)
    t2 = swap(t32, 2)

    st_in = from_parts(mine)
    fq_2, _ = tie((fq, mine))
    nl, do = call(
        numer_kernel, (halves,),
        [col(n, w), col(n, w), col(n, w), whole((n, d)), row(w, d)],
        [act(F32), act(F32)], "numer", 2 * big,
    )(fq_2, fk, fv, dm, w_out)

    at, dn, rs, gp = call(
        norm_kernel, (halves,),
        [SMEM, col(n, w), st_spec, col(n, w), row(w, n), col(n, w), col(1, w)],
        [act(BF), act(F32), state, ((8, d), F32, col(8, w))], "norm", big,
    )(nv, nl, st_in, fq, fqt, do, gain)

    parts = to_parts(rs)
    dn_3, _ = tie((dn, rs))
    mine_act = ((n, d), BF, col_mine(n, w))
    one = ((n + 8, GL), F32, whole((n + 8, GL)))
    two = ((2, n + 8, GL), F32, whole((2, n + 8, GL)))
    dq, dq_own, dq_near, dq_far = call_mine(
        dq_kernel,
        [col_mine(n, w), row_mine(w // 2, 128)] + [col_mine(n, w)] * 3 + [col_mine(8, w)],
        [mine_act, one, one, two], "dquery", 2 * big,
    )(me, dn_3, st_in, fk, fv, sq, gp)
    parts, dq = tie((parts, dq))
    dq_far = swap(dq_far, 1)
    dq_near = swap(dq_near, 2)
    mine = run(parts, True, "suffix")

    r_in = from_parts(mine)
    dn_4, t1, _ = tie((dn, t1, mine))
    t3 = swap(t1, 2)
    (lk,) = call(
        local_k_kernel, (halves,), [col(n, w), col(n, w), col(n, w)], [act(F32)], "localk", 1,
    )(dn_4, fq, fv)
    lk, dq_near, t2, t3 = tie((lk, dq_near, t2, t3))
    dk, *dk_send = call_mine(
        dk_kernel,
        [col_mine(n, w), col_mine(n, w), row_mine(w // 2, 128), col_mine(n, w)],
        [mine_act] + [((n, GL), F32, whole((n, GL)))] * ngroup,
        "dkey", 1,
    )(me, lk, fv, r_in, sk)

    dk_got = [dk_send[0]] + [swap(dk_send[k], k) for k in range(1, ngroup)]
    side = lax.axis_size("x")
    per = d // nxy
    dq_far, _ = tie((dq_far, dk))
    dq_got = [dq_own, dq_far, dq_near, swap(dq_far, 2)]
    at_y = lambda depth: pl.BlockSpec(
        (side, 2, per, depth), lambda step, y: (0, pair_at(step, y), 0, 0)
    )
    by_xy = lambda v: v.reshape(side, side, per, v.shape[-1])
    qshape = (side, per + 8, GL)
    tall, *gq_send = call_mine(
        wgrad_q_kernel,
        [at_y(n)] * 4 + [
            whole((n + 8, GL)),
            pl.BlockSpec((1, n + 8, GL), lambda *_: (0, 0, 0)),
            whole((n + 8, GL)),
            pl.BlockSpec((1, n + 8, GL), lambda *_: (1, 0, 0)),
        ],
        [((side, side, per, 4 * n), BF, at_y(4 * n))] + [(qshape, F32, whole(qshape))] * side,
        "wgradq", 2 * big,
    )(own("y"), by_xy(t0), by_xy(t1), by_xy(t2), by_xy(t3), *dq_got)
    gq_got = [gq_send[0]] + [turn_about("y", gq_send[k], k) for k in range(1, side)]

    steps = 2
    kshape = (nxy, per, GL)
    (gk,) = call(
        wgrad_k_kernel, (steps,), [row(d // steps, 4 * n)] + [whole((n, GL))] * 4,
        [(kshape, F32, pl.BlockSpec((nxy // steps,) + kshape[1:], lambda g: (g, 0, 0)))],
        "wgradk", 400 * big,
    )(tall.reshape(d, 4 * n), *dk_got)
    gk_parts = lax.all_to_all(gk, ("x", "y"), 0, 0, tiled=True)

    dn_5, _ = tie((dn, gk))
    mo, lv = call(
        local_v_kernel, (halves,),
        [whole((n, d)), col(d, w), col(n, w), col(n, w), col(n, w)], [act(BF), act(F32)], "localv", 400 * big,
    )(at, w_out, dn_5, fq, fk)
    gq_got, _ = tie((gq_got, gk))
    gq_send = call(
        sum_y_kernel, (), [SMEM] + [whole(qshape)] * side,
        [(qshape[1:], F32, whole(qshape[1:]))] * side, "sumy", 1 << 22,
    )(own("x"), *gq_got)
    gq_got = [gq_send[0]] + [turn_about("x", gq_send[k], k) for k in range(1, side)]
    gk_parts, mo, lv, gq_got = tie((gk_parts, mo, lv, gq_got))

    last = ("c", "w", "b")
    nlast = lax.axis_size(last)
    each = per // nlast
    jshape = (nlast, 2 * each, GL + 128)
    (both,) = call(
        join_kernel, (), [whole(qshape[1:])] * side + [whole(kshape)],
        [(jshape, F32, whole(jshape))], "join", 1 << 22,
    )(*gq_got, gk_parts)
    dk_6, _ = tie((dk, both))
    both = lax.all_to_all(both, last, 0, 0, tiled=True)

    (dt,) = call(
        dtok_kernel, (halves,),
        [col(n, w), col(n, w), st_spec, col(n, w), col(n, w), col(d, w), col(d, w), col(d, w)],
        [((n, d), BF, whole((n, d)))], "dtok", 1,
        scratch=[pltpu.VMEM((n, d), F32)],
    )(lv, fk, r_in, dq, dk_6, w_query, w_key, w_value)
    dw, dg = call(
        final_kernel, (), [whole(jshape)],
        [((2, each * d), F32, whole((2, each * d))), ((8, 128), F32, whole((8, 128)))],
        "final", 1 << 20,
    )(both)
    return mo.reshape(1, n, d), dt.reshape(1, n, d), dw, dg.reshape(d)


def solution(mesh):
    fine = Mesh(mesh.devices.reshape(4, 4, 2, 4, 2), ("x", "y", "c", "w", "b"))
    acts = P(("w", "b"), SEQ, None)
    placed = (acts, P(), P(), P(), P(), P(), P(("w", "b")), acts)
    return jax.shard_map(
        on_device,
        mesh=fine,
        in_specs=placed,
        out_specs=(acts, acts, P(None, ("x", "y", "c", "w", "b")), P()),
        check_vma=False,
    )
```

```python
import functools

import jax
import jax.numpy as jnp
from jax import lax
from jax.experimental import pallas as pl
from jax.experimental.pallas import tpu as pltpu
from jax.sharding import Mesh, PartitionSpec as P

EPS = 1e-05
HD = 64
GL = 256
F32 = jnp.float32
BF = jnp.bfloat16
NN = (((1,), (0,)), ((), ()))
NT = (((1,), (1,)), ((), ()))
TN = (((0,), (0,)), ((), ()))
SEQ = ("x", "y", "c")
GROUP = ("c", "b")
VMEM_LIMIT = 64 * 1024 * 1024
GRANT = {name: 58 << 20 for name in ("turn", "query", "dquery")}
GRANT.update({name: 4 << 20 for name in ("prefix", "suffix", "final")})


def dot(a, b, dims=NN):
    return lax.dot_general(a, b, dims, preferred_element_type=F32)


def split(v):
    hi = v.astype(BF)
    return hi, (v - hi.astype(F32)).astype(BF)


def lanes(shape):
    return lax.broadcasted_iota(jnp.int32, shape, 1)


def rows(shape):
    return lax.broadcasted_iota(jnp.int32, shape, 0)


def head_masks(shape):
    which = lanes(shape) // HD
    return [which == h for h in range(GL // HD)]


def pick(mask, v):
    return jnp.where(mask, v, jnp.zeros_like(v))


def pack_state(full):
    out = []
    for p in range(GL // 128):
        blk = full[128 * p:128 * p + 128, 128 * p:128 * p + 128]
        out.append(jnp.where(lanes((HD, 128)) < HD, blk[:HD], blk[HD:]))
    return jnp.concatenate(out, axis=0)


def unpack_state(st):
    zero = jnp.zeros((128, 128), st.dtype)
    blks = []
    for p in range(GL // 128):
        a = st[HD * p:HD * p + HD]
        first = lanes((HD, 128)) < HD
        blks.append(jnp.concatenate([pick(first, a), pick(~first, a)], axis=0))
    return jnp.concatenate(
        [
            jnp.concatenate([blks[0], zero], axis=1),
            jnp.concatenate([zero, blks[1]], axis=1),
        ],
        axis=0,
    )


def valid_rows(nv_ref, count):
    return (rows((count, 1)) < nv_ref[0]).astype(F32)


def features(raw):
    ex = jnp.exp(jnp.minimum(raw, 0.0))
    up = raw > 0
    return jnp.where(up, raw + 1.0, ex), jnp.where(up, 1.0, ex)


def head_mean(*parts):
    same = (rows((GL, GL)) // HD == lanes((GL, GL)) // HD).astype(BF)
    total = dot(parts[0], same)
    for p in parts[1:]:
        total = total + dot(p, same)
    return total * (1.0 / HD)


def groups_of(ref):
    return [(j, slice(GL * j, GL * j + GL)) for j in range(ref.shape[-1] // GL)]


def my_groups(me_ref, step):
    for i in range(2):
        at = jnp.bitwise_xor(jnp.bitwise_and(me_ref[0], 1), i)
        yield (
            2 * step + i,
            pl.ds(pl.multiple_of(at * GL, GL), GL),
            pl.ds(pl.multiple_of(at * 128, 128), 128),
        )


def each_step(body):
    for step in range(2):
        pl.when(pl.program_id(0) == step)(functools.partial(body, step))


def kv_kernel(nv_ref, tok, wk, wv, fk_o, fv_o, sk_o, st_o):
    n = tok.shape[0]
    valid = valid_rows(nv_ref, n)
    feat, slope = features(dot(tok[...], wk[...]))
    fk = (feat * valid).astype(BF)
    fv = dot(tok[...], wv[...]).astype(BF)
    fk_o[...] = fk
    fv_o[...] = fv
    sk_o[...] = slope * valid
    for j, c in groups_of(fk):
        st_o[128 * j:128 * j + 128, :] = pack_state(dot(fk[:, c], fv[:, c], TN))


def turn_kernel(tok, t16_o, t32_o):
    n = tok.shape[0]
    eye = (rows((n, n)) == lanes((n, n))).astype(BF)
    res = dot(tok[...], eye, TN)
    t16_o[...] = res.astype(BF)
    t32_o[...] = res


def q_kernel(tok, wq, fq_o, fqt_o, sq_o):
    feat, slope = features(dot(tok[...], wq[...]))
    fq = feat.astype(BF)
    fq_o[...] = fq
    sq_o[...] = slope
    eye = (rows((GL, GL)) == lanes((GL, GL))).astype(BF)
    for _, c in groups_of(fq):
        fqt_o[c, :] = dot(eye, fq[:, c], NT).astype(BF)


def numer_kernel(fq, fk, fv, dm, wo, nl_o, do_o):
    n = fq.shape[0]
    do_o[...] = dot(dm[...], wo[...], NT)
    causal = rows((n, n)) >= lanes((n, n))
    for _, c in groups_of(fq):
        total = jnp.zeros((n, GL), F32)
        for m in head_masks((n, GL)):
            s = pick(causal, dot(pick(m, fq[:, c]), fk[:, c], NT)).astype(BF)
            total = total + dot(s, pick(m, fv[:, c]))
        nl_o[:, c] = total


def norm_kernel(nv_ref, nl, st, fq, fqt, do, gain, at_o, dn_o, rs_o, gp_o):
    n = nl.shape[0]
    valid = valid_rows(nv_ref, n)
    for j, c in groups_of(nl):
        r = slice(128 * j, 128 * j + 128)
        s_hi, s_lo = split(unpack_state(st[r, :]))
        numer = nl[:, c] + dot(fq[:, c], s_hi) + dot(fq[:, c], s_lo)
        inv = lax.rsqrt(head_mean((numer * numer).astype(BF)) + EPS)
        normed = numer * inv
        scale = gain[:, c]
        at_o[:, c] = (normed * scale * valid).astype(BF)
        dov = do[:, c] * valid
        gp_o[:, c] = jnp.sum((dov * normed).reshape(n // 8, 8, GL), axis=0)
        g = dov * scale
        dn = inv * (g - normed * head_mean(*split(g * normed)))
        dn_o[:, c] = dn
        d_hi, d_lo = split(dn)
        rs_o[r, :] = pack_state(dot(fqt[c, :], d_hi) + dot(fqt[c, :], d_lo))


def dq_kernel(me_ref, dn, st, fk, fv, sq, gp, dq_o, mine, near, far):
    n = dn.shape[0]

    def body(step):
        causal = rows((n, n)) >= lanes((n, n))
        for k, c, r in my_groups(me_ref, step):
            s_hi, s_lo = split(unpack_state(st[r, :]))
            d_hi, d_lo = split(dn[:, c])
            total = dot(d_hi, s_hi, NT) + dot(d_lo, s_hi, NT) + dot(d_hi, s_lo, NT)
            keys, values = fk[:, c], fv[:, c]
            for m in head_masks((n, GL)):
                vm = pick(m, values)
                w = pick(causal, dot(d_hi, vm, NT) + dot(d_lo, vm, NT)).astype(BF)
                total = total + dot(w, pick(m, keys))
            dq = (total * sq[:, c]).astype(BF)
            dq_o[:, c] = dq
            out = (mine, far.at[0], near, far.at[1])[k]
            out[0:n, :] = dq.astype(F32)
            out[n:n + 8, :] = gp[:, c]

    each_step(body)


def local_k_kernel(dn, fq, fv, lk_o):
    n = dn.shape[0]
    later = lanes((n, n)) >= rows((n, n))
    for _, c in groups_of(dn):
        d_hi, d_lo = split(dn[:, c])
        total = jnp.zeros((n, GL), F32)
        for m in head_masks((n, GL)):
            vm = pick(m, fv[:, c])
            w = pick(later, dot(vm, d_hi, NT) + dot(vm, d_lo, NT)).astype(BF)
            total = total + dot(w, pick(m, fq[:, c]))
        lk_o[:, c] = total


def local_v_kernel(at, wo, dn, fq, fk, mo_o, lv_o):
    n = dn.shape[0]
    mo_o[...] = dot(at[...], wo[...]).astype(BF)
    later = lanes((n, n)) >= rows((n, n))
    for _, c in groups_of(dn):
        d_hi = dn[:, c].astype(BF)
        total = jnp.zeros((n, GL), F32)
        for m in head_masks((n, GL)):
            s = pick(later, dot(pick(m, fk[:, c]), fq[:, c], NT)).astype(BF)
            total = total + dot(s, pick(m, d_hi))
        lv_o[:, c] = total


def dk_kernel(me_ref, lk, fv, st, sk, dk_o, *send):
    def body(step):
        for k, c, r in my_groups(me_ref, step):
            r_hi, r_lo = split(unpack_state(st[r, :]))
            total = lk[:, c] + dot(fv[:, c], r_hi, NT) + dot(fv[:, c], r_lo, NT)
            dk = (total * sk[:, c]).astype(BF)
            dk_o[:, c] = dk
            send[k][...] = dk.astype(F32)

    each_step(body)


def dtok_kernel(lv, fk, st, dq, dk, wq, wk, wv, dt_o, acc):
    term = dot(dq[...], wq[...], NT) + dot(dk[...], wk[...], NT)
    dv = []
    for j, c in groups_of(lv):
        r_hi, r_lo = split(unpack_state(st[128 * j:128 * j + 128, :]))
        dv.append((lv[:, c] + dot(fk[:, c], r_hi) + dot(fk[:, c], r_lo)).astype(BF))
    term = term + dot(jnp.concatenate(dv, axis=1), wv[...], NT)

    @pl.when(pl.program_id(0) == 0)
    def _():
        acc[...] = term

    @pl.when(pl.program_id(0) > 0)
    def _():
        acc[...] += term

    @pl.when(pl.program_id(0) == pl.num_programs(0) - 1)
    def _():
        dt_o[...] = acc[...].astype(BF)


def wgrad_q_kernel(y_ref, t0, t1, t2, t3, d0, d1, d2, d3, all_o, *send):
    d1, d3 = d1.at[0], d3.at[0]
    n = t0.shape[3]
    blocks, m = t0.shape[0], t0.shape[2]

    def body(step):
        parts = [d[0:n, :].astype(BF) for d in (d0, d1, d2, d3)]
        gain = d0[n:n + 8, :] + d1[n:n + 8, :] + d2[n:n + 8, :] + d3[n:n + 8, :]
        for i in range(2):
            out = send[2 * step + i]
            at = jnp.bitwise_xor(jnp.bitwise_and(y_ref[0], 1), i)
            res = jnp.zeros((blocks * m, d0.shape[1]), F32)
            for j, t in enumerate((t0, t1, t2, t3)):
                turned = t[:, at].reshape(blocks * m, n).astype(BF)
                all_o[:, at, :, n * j:n * j + n] = turned.reshape(blocks, m, n)
                res = res + dot(turned, parts[j])
            out[:, 0:m, :] = res.reshape(blocks, m, res.shape[1])
            for block in range(blocks):
                out[block, m:m + 8, :] = gain

    each_step(body)


def sum_y_kernel(x_ref, v0, v1, v2, v3, *send):
    for k, out in enumerate(send):
        at = jnp.bitwise_xor(x_ref[0], k)
        out[...] = v0[at] + v1[at] + v2[at] + v3[at]


def wgrad_k_kernel(t, d0, d1, d2, d3, out):
    k, m, w = out.shape
    d = jnp.concatenate([v[...].astype(BF) for v in (d0, d1, d2, d3)], axis=0)
    out[...] = dot(t[...], d).reshape(k, m, w)


def prefix_kernel(backward, v, out):
    count = v.shape[0]
    order = range(count - 1, -1, -1) if backward else range(count)
    total = jnp.zeros(v.shape[1:], F32)
    for i in order:
        out[i] = total
        total = total + v[i]


def join_kernel(q0, q1, q2, q3, k, out):
    total = k[0]
    for i in range(1, k.shape[0]):
        total = total + k[i]
    height, width = total.shape
    each = height // out.shape[0]
    q = q0[...] + q1[...] + q2[...] + q3[...]
    gain = jnp.sum(q[height:height + 8], axis=0, keepdims=True)
    for j in range(out.shape[0]):
        for i in range(each):
            r = each * j + i
            out[j, :, width * i:width * i + width] = q[r:r + 1]
            at = width * (each + i)
            out[j, :, at:at + width] = total[r:r + 1]
        out[j, :, 2 * each * width:] = gain


def final_kernel(v, dw_o, dg_o):
    width = GL
    each = (v.shape[2] // width - 1) // 2
    for c in range(2):
        for b in range(2):
            g = 2 * c + b
            total = v[8 * c + b]
            for w in range(1, 4):
                total = total + v[8 * c + 2 * w + b]
            for which in range(2):
                for i in range(each):
                    r = width * (which * each + i)
                    at = 4 * width * i + width * g
                    dw_o[which:which + 1, at:at + width] = total[:, r:r + width]
            for i in range(2):
                r = width * 2 * each + 128 * i
                dg_o[2 * g + i:2 * g + i + 1, :] = total[:, r:r + 128]


def call(kernel, grid, in_specs, outs, name, flops, scratch=()):
    out_shape = [jax.ShapeDtypeStruct(s, d) for s, d, _ in outs]
    return pl.pallas_call(
        kernel,
        grid=grid,
        in_specs=in_specs,
        out_specs=[spec for _, _, spec in outs],
        out_shape=out_shape,
        scratch_shapes=list(scratch),
        name=name,
        cost_estimate=pl.CostEstimate(flops=flops, bytes_accessed=4 << 20, transcendentals=0),
        compiler_params=pltpu.CompilerParams(vmem_limit_bytes=GRANT.get(name, VMEM_LIMIT)),
    )


def call_mine(kernel, in_specs, outs, name, flops, steps=2):
    return pl.pallas_call(
        kernel,
        grid_spec=pltpu.PrefetchScalarGridSpec(
            num_scalar_prefetch=1,
            grid=(steps,),
            in_specs=in_specs,
            out_specs=[spec for _, _, spec in outs],
        ),
        out_shape=[jax.ShapeDtypeStruct(s, d) for s, d, _ in outs],
        name=name,
        cost_estimate=pl.CostEstimate(flops=flops, bytes_accessed=4 << 20, transcendentals=0),
        compiler_params=pltpu.CompilerParams(vmem_limit_bytes=GRANT.get(name, VMEM_LIMIT)),
    )


SMEM = pl.BlockSpec(memory_space=pltpu.SMEM)


def whole(shape):
    return pl.BlockSpec(shape, lambda *_: (0,) * len(shape))


def col(r, w=GL):
    return pl.BlockSpec((r, w), lambda g: (0, g))


def row(r, w):
    return pl.BlockSpec((r, w), lambda g: (g, 0))


def pair_at(step, me):
    return jnp.bitwise_xor(jnp.right_shift(me[0], 1), step)


def col_mine(r, w):
    return pl.BlockSpec((r, w), lambda step, me: (0, pair_at(step, me)))


def row_mine(r, w):
    return pl.BlockSpec((r, w), lambda step, me: (pair_at(step, me), 0))


def on_device(tokens, w_query, w_key, w_value, w_out, norm_gain, lengths, d_mixed):
    _, n, d = tokens.shape
    tok = tokens.reshape(n, d)
    dm = d_mixed.reshape(n, d)
    w = 2 * GL
    halves = d // w
    nseq = lax.axis_size(SEQ)
    nxy = lax.axis_size(("x", "y"))
    ngroup = lax.axis_size(GROUP)
    nv = lengths - lax.axis_index(SEQ) * n
    own = lambda axes: jnp.full((1,), lax.axis_index(axes), jnp.int32)
    me = own(GROUP)
    gain = norm_gain.reshape(1, d)
    act = lambda dt: ((n, d), dt, col(n, w))
    st_rows = d // 2
    st_spec = row(w // 2, 128)
    state = ((st_rows, 128), F32, st_spec)
    big = 2 * n * d * d

    fk, fv, sk, st1 = call(
        kv_kernel, (halves,), [SMEM, whole((n, d)), col(d, w), col(d, w)],
        [act(BF), act(BF), act(F32), state], "kv", 2 * big,
    )(nv, tok, w_key, w_value)

    tie = lax.optimization_barrier

    def to_parts(st):
        return lax.all_to_all(st.reshape(nseq, st_rows // nseq, 128), SEQ, 0, 0, tiled=True)

    def run(parts, backward, name):
        shape = parts.shape
        (mine,) = call(
            functools.partial(prefix_kernel, backward), (), [whole(shape)],
            [(shape, F32, whole(shape))], name, 1 << 20,
        )(parts)
        return mine

    def from_parts(mine):
        return lax.all_to_all(mine, SEQ, 0, 0, tiled=True).reshape(st_rows, 128)

    def swap(v, k):
        return lax.ppermute(v, GROUP, [(i, i ^ k) for i in range(ngroup)])

    def turn_about(axis, v, k):
        return lax.ppermute(v, axis, [(i, i ^ k) for i in range(lax.axis_size(axis))])

    parts = to_parts(st1)
    tok_1, _ = tie((tok, st1))
    t0, t32 = call(
        turn_kernel, (halves,), [col(n, w)],
        [((d, n), BF, row(w, n)), ((d, n), F32, row(w, n))], "turn", big // 4,
    )(tok_1)
    fq, fqt, sq = call(
        q_kernel, (halves,), [whole((n, d)), col(d, w)],
        [act(BF), ((d, n), BF, row(w, n)), act(F32)], "query", big,
    )(tok_1, w_query)
    parts, fq, t0 = tie((parts, fq, t0))
    mine = run(parts, False, "prefix")

    t32, _ = tie((t32, mine))
    t1 = swap(t32, 1)
    t2 = swap(t32, 2)

    st_in = from_parts(mine)
    fq_2, _ = tie((fq, mine))
    nl, do = call(
        numer_kernel, (halves,),
        [col(n, w), col(n, w), col(n, w), whole((n, d)), row(w, d)],
        [act(F32), act(F32)], "numer", 2 * big,
    )(fq_2, fk, fv, dm, w_out)

    at, dn, rs, gp = call(
        norm_kernel, (halves,),
        [SMEM, col(n, w), st_spec, col(n, w), row(w, n), col(n, w), col(1, w)],
        [act(BF), act(F32), state, ((8, d), F32, col(8, w))], "norm", big,
    )(nv, nl, st_in, fq, fqt, do, gain)

    parts = to_parts(rs)
    dn_3, _ = tie((dn, rs))
    mine_act = ((n, d), BF, col_mine(n, w))
    one = ((n + 8, GL), F32, whole((n + 8, GL)))
    two = ((2, n + 8, GL), F32, whole((2, n + 8, GL)))
    dq, dq_own, dq_near, dq_far = call_mine(
        dq_kernel,
        [col_mine(n, w), row_mine(w // 2, 128)] + [col_mine(n, w)] * 3 + [col_mine(8, w)],
        [mine_act, one, one, two], "dquery", 2 * big,
    )(me, dn_3, st_in, fk, fv, sq, gp)
    parts, dq = tie((parts, dq))
    dq_far = swap(dq_far, 1)
    dq_near = swap(dq_near, 2)
    mine = run(parts, True, "suffix")

    r_in = from_parts(mine)
    dn_4, t1, _ = tie((dn, t1, mine))
    t3 = swap(t1, 2)
    (lk,) = call(
        local_k_kernel, (halves,), [col(n, w), col(n, w), col(n, w)], [act(F32)], "localk", 1,
    )(dn_4, fq, fv)
    lk, dq_near, t2, t3 = tie((lk, dq_near, t2, t3))
    dk, *dk_send = call_mine(
        dk_kernel,
        [col_mine(n, w), col_mine(n, w), row_mine(w // 2, 128), col_mine(n, w)],
        [mine_act] + [((n, GL), F32, whole((n, GL)))] * ngroup,
        "dkey", 1,
    )(me, lk, fv, r_in, sk)

    dk_got = [dk_send[0]] + [swap(dk_send[k], k) for k in range(1, ngroup)]
    side = lax.axis_size("x")
    per = d // nxy
    dq_far, _ = tie((dq_far, dk))
    dq_got = [dq_own, dq_far, dq_near, swap(dq_far, 2)]
    at_y = lambda depth: pl.BlockSpec(
        (side, 2, per, depth), lambda step, y: (0, pair_at(step, y), 0, 0)
    )
    by_xy = lambda v: v.reshape(side, side, per, v.shape[-1])
    qshape = (side, per + 8, GL)
    tall, *gq_send = call_mine(
        wgrad_q_kernel,
        [at_y(n)] * 4 + [
            whole((n + 8, GL)),
            pl.BlockSpec((1, n + 8, GL), lambda *_: (0, 0, 0)),
            whole((n + 8, GL)),
            pl.BlockSpec((1, n + 8, GL), lambda *_: (1, 0, 0)),
        ],
        [((side, side, per, 4 * n), BF, at_y(4 * n))] + [(qshape, F32, whole(qshape))] * side,
        "wgradq", 2 * big,
    )(own("y"), by_xy(t0), by_xy(t1), by_xy(t2), by_xy(t3), *dq_got)
    gq_got = [gq_send[0]] + [turn_about("y", gq_send[k], k) for k in range(1, side)]

    steps = 2
    kshape = (nxy, per, GL)
    (gk,) = call(
        wgrad_k_kernel, (steps,), [row(d // steps, 4 * n)] + [whole((n, GL))] * 4,
        [(kshape, F32, pl.BlockSpec((nxy // steps,) + kshape[1:], lambda g: (g, 0, 0)))],
        "wgradk", 400 * big,
    )(tall.reshape(d, 4 * n), *dk_got)
    gk_parts = lax.all_to_all(gk, ("x", "y"), 0, 0, tiled=True)

    dn_5, _ = tie((dn, gk))
    mo, lv = call(
        local_v_kernel, (halves,),
        [whole((n, d)), col(d, w), col(n, w), col(n, w), col(n, w)], [act(BF), act(F32)], "localv", 400 * big,
    )(at, w_out, dn_5, fq, fk)
    gq_got, _ = tie((gq_got, gk))
    gq_send = call(
        sum_y_kernel, (), [SMEM] + [whole(qshape)] * side,
        [(qshape[1:], F32, whole(qshape[1:]))] * side, "sumy", 1 << 22,
    )(own("x"), *gq_got)
    gq_got = [gq_send[0]] + [turn_about("x", gq_send[k], k) for k in range(1, side)]
    gk_parts, mo, lv, gq_got = tie((gk_parts, mo, lv, gq_got))

    last = ("c", "w", "b")
    nlast = lax.axis_size(last)
    each = per // nlast
    jshape = (nlast, 1, (2 * each + 1) * GL)
    (both,) = call(
        join_kernel, (), [whole(qshape[1:])] * side + [whole(kshape)],
        [(jshape, F32, whole(jshape))], "join", 1 << 22,
    )(*gq_got, gk_parts)
    dk_6, _ = tie((dk, both))
    both = lax.all_to_all(both, last, 0, 0, tiled=True)

    (dt,) = call(
        dtok_kernel, (halves,),
        [col(n, w), col(n, w), st_spec, col(n, w), col(n, w), col(d, w), col(d, w), col(d, w)],
        [((n, d), BF, whole((n, d)))], "dtok", 1,
        scratch=[pltpu.VMEM((n, d), F32)],
    )(lv, fk, r_in, dq, dk_6, w_query, w_key, w_value)
    dw, dg = call(
        final_kernel, (), [whole(jshape)],
        [((2, each * d), F32, whole((2, each * d))), ((8, 128), F32, whole((8, 128)))],
        "final", 1 << 20,
    )(both)
    return mo.reshape(1, n, d), dt.reshape(1, n, d), dw, dg.reshape(d)


def solution(mesh):
    fine = Mesh(mesh.devices.reshape(4, 4, 2, 4, 2), ("x", "y", "c", "w", "b"))
    acts = P(("w", "b"), SEQ, None)
    placed = (acts, P(), P(), P(), P(), P(), P(("w", "b")), acts)
    return jax.shard_map(
        on_device,
        mesh=fine,
        in_specs=placed,
        out_specs=(acts, acts, P(None, ("x", "y", "c", "w", "b")), P()),
        check_vma=False,
    )
```

```python
import functools

import jax
import jax.numpy as jnp
from jax import lax
from jax.experimental import pallas as pl
from jax.experimental.pallas import tpu as pltpu
from jax.sharding import Mesh, PartitionSpec as P

EPS = 1e-05
HD = 64
GL = 256
F32 = jnp.float32
BF = jnp.bfloat16
NN = (((1,), (0,)), ((), ()))
NT = (((1,), (1,)), ((), ()))
TN = (((0,), (0,)), ((), ()))
SEQ = ("x", "y", "c")
GROUP = ("c", "b")
VMEM_LIMIT = 64 * 1024 * 1024
GRANT = {name: 58 << 20 for name in ("turn", "query", "dquery")}
GRANT.update({name: 4 << 20 for name in ("prefix", "suffix", "final")})


def dot(a, b, dims=NN):
    return lax.dot_general(a, b, dims, preferred_element_type=F32)


def split(v):
    hi = v.astype(BF)
    return hi, (v - hi.astype(F32)).astype(BF)


def lanes(shape):
    return lax.broadcasted_iota(jnp.int32, shape, 1)


def rows(shape):
    return lax.broadcasted_iota(jnp.int32, shape, 0)


def head_masks(shape):
    which = lanes(shape) // HD
    return [which == h for h in range(GL // HD)]


def pick(mask, v):
    return jnp.where(mask, v, jnp.zeros_like(v))


def pack_state(full):
    out = []
    for p in range(GL // 128):
        blk = full[128 * p:128 * p + 128, 128 * p:128 * p + 128]
        out.append(jnp.where(lanes((HD, 128)) < HD, blk[:HD], blk[HD:]))
    return jnp.concatenate(out, axis=0)


def unpack_state(st):
    zero = jnp.zeros((128, 128), st.dtype)
    blks = []
    for p in range(GL // 128):
        a = st[HD * p:HD * p + HD]
        first = lanes((HD, 128)) < HD
        blks.append(jnp.concatenate([pick(first, a), pick(~first, a)], axis=0))
    return jnp.concatenate(
        [
            jnp.concatenate([blks[0], zero], axis=1),
            jnp.concatenate([zero, blks[1]], axis=1),
        ],
        axis=0,
    )


def valid_rows(nv_ref, count):
    return (rows((count, 1)) < nv_ref[0]).astype(F32)


def features(raw):
    ex = jnp.exp(jnp.minimum(raw, 0.0))
    up = raw > 0
    return jnp.where(up, raw + 1.0, ex), jnp.where(up, 1.0, ex)


def head_mean(*parts):
    same = (rows((GL, GL)) // HD == lanes((GL, GL)) // HD).astype(BF)
    total = dot(parts[0], same)
    for p in parts[1:]:
        total = total + dot(p, same)
    return total * (1.0 / HD)


def groups_of(ref):
    return [(j, slice(GL * j, GL * j + GL)) for j in range(ref.shape[-1] // GL)]


def my_groups(me_ref, step):
    for i in range(2):
        at = jnp.bitwise_xor(jnp.bitwise_and(me_ref[0], 1), i)
        yield (
            2 * step + i,
            pl.ds(pl.multiple_of(at * GL, GL), GL),
            pl.ds(pl.multiple_of(at * 128, 128), 128),
        )


def each_step(body):
    for step in range(2):
        pl.when(pl.program_id(0) == step)(functools.partial(body, step))


def kv_kernel(nv_ref, tok, wk, wv, fk_o, fv_o, sk_o, st_o):
    n = tok.shape[0]
    valid = valid_rows(nv_ref, n)
    feat, slope = features(dot(tok[...], wk[...]))
    fk = (feat * valid).astype(BF)
    fv = dot(tok[...], wv[...]).astype(BF)
    fk_o[...] = fk
    fv_o[...] = fv
    sk_o[...] = slope * valid
    for j, c in groups_of(fk):
        st_o[128 * j:128 * j + 128, :] = pack_state(dot(fk[:, c], fv[:, c], TN))


def turn_kernel(tok, t16_o, t32_o):
    n = tok.shape[0]
    eye = (rows((n, n)) == lanes((n, n))).astype(BF)
    res = dot(tok[...], eye, TN)
    t16_o[...] = res.astype(BF)
    t32_o[...] = res


def q_kernel(tok, wq, fq_o, fqt_o, sq_o):
    feat, slope = features(dot(tok[...], wq[...]))
    fq = feat.astype(BF)
    fq_o[...] = fq
    sq_o[...] = slope
    eye = (rows((GL, GL)) == lanes((GL, GL))).astype(BF)
    for _, c in groups_of(fq):
        fqt_o[c, :] = dot(eye, fq[:, c], NT).astype(BF)


def numer_kernel(fq, fk, fv, dm, wo, nl_o, do_o):
    n = fq.shape[0]
    do_o[...] = dot(dm[...], wo[...], NT)
    causal = rows((n, n)) >= lanes((n, n))
    for _, c in groups_of(fq):
        total = jnp.zeros((n, GL), F32)
        for m in head_masks((n, GL)):
            s = pick(causal, dot(pick(m, fq[:, c]), fk[:, c], NT)).astype(BF)
            total = total + dot(s, pick(m, fv[:, c]))
        nl_o[:, c] = total


def norm_kernel(nv_ref, nl, st, fq, fqt, do, gain, at_o, dn_o, rs_o, gp_o):
    n = nl.shape[0]
    valid = valid_rows(nv_ref, n)
    for j, c in groups_of(nl):
        r = slice(128 * j, 128 * j + 128)
        s_hi, s_lo = split(unpack_state(st[r, :]))
        numer = nl[:, c] + dot(fq[:, c], s_hi) + dot(fq[:, c], s_lo)
        inv = lax.rsqrt(head_mean((numer * numer).astype(BF)) + EPS)
        normed = numer * inv
        scale = gain[:, c]
        at_o[:, c] = (normed * scale * valid).astype(BF)
        dov = do[:, c] * valid
        gp_o[:, c] = jnp.sum((dov * normed).reshape(n // 8, 8, GL), axis=0)
        g = dov * scale
        dn = inv * (g - normed * head_mean(*split(g * normed)))
        dn_o[:, c] = dn
        d_hi, d_lo = split(dn)
        rs_o[r, :] = pack_state(dot(fqt[c, :], d_hi) + dot(fqt[c, :], d_lo))


def dq_kernel(me_ref, dn, st, fk, fv, sq, gp, dq_o, mine, near, far):
    n = dn.shape[0]

    def body(step):
        causal = rows((n, n)) >= lanes((n, n))
        for k, c, r in my_groups(me_ref, step):
            s_hi, s_lo = split(unpack_state(st[r, :]))
            d_hi, d_lo = split(dn[:, c])
            total = dot(d_hi, s_hi, NT) + dot(d_lo, s_hi, NT) + dot(d_hi, s_lo, NT)
            keys, values = fk[:, c], fv[:, c]
            for m in head_masks((n, GL)):
                vm = pick(m, values)
                w = pick(causal, dot(d_hi, vm, NT) + dot(d_lo, vm, NT)).astype(BF)
                total = total + dot(w, pick(m, keys))
            dq = (total * sq[:, c]).astype(BF)
            dq_o[:, c] = dq
            out = (mine, far.at[0], near, far.at[1])[k]
            out[0:n, :] = dq.astype(F32)
            out[n:n + 8, :] = gp[:, c]

    each_step(body)


def local_k_kernel(dn, fq, fv, lk_o):
    n = dn.shape[0]
    later = lanes((n, n)) >= rows((n, n))
    for _, c in groups_of(dn):
        d_hi, d_lo = split(dn[:, c])
        total = jnp.zeros((n, GL), F32)
        for m in head_masks((n, GL)):
            vm = pick(m, fv[:, c])
            w = pick(later, dot(vm, d_hi, NT) + dot(vm, d_lo, NT)).astype(BF)
            total = total + dot(w, pick(m, fq[:, c]))
        lk_o[:, c] = total


def local_v_kernel(at, wo, dn, fq, fk, mo_o, lv_o):
    n = dn.shape[0]
    mo_o[...] = dot(at[...], wo[...]).astype(BF)
    later = lanes((n, n)) >= rows((n, n))
    for _, c in groups_of(dn):
        d_hi = dn[:, c].astype(BF)
        total = jnp.zeros((n, GL), F32)
        for m in head_masks((n, GL)):
            s = pick(later, dot(pick(m, fk[:, c]), fq[:, c], NT)).astype(BF)
            total = total + dot(s, pick(m, d_hi))
        lv_o[:, c] = total


def dk_kernel(me_ref, lk, fv, st, sk, dk_o, *send):
    def body(step):
        for k, c, r in my_groups(me_ref, step):
            r_hi, r_lo = split(unpack_state(st[r, :]))
            total = lk[:, c] + dot(fv[:, c], r_hi, NT) + dot(fv[:, c], r_lo, NT)
            dk = (total * sk[:, c]).astype(BF)
            dk_o[:, c] = dk
            send[k][...] = dk.astype(F32)

    each_step(body)


def dtok_kernel(lv, fk, st, dq, dk, wq, wk, wv, dt_o, acc):
    term = dot(dq[...], wq[...], NT) + dot(dk[...], wk[...], NT)
    dv = []
    for j, c in groups_of(lv):
        r_hi, r_lo = split(unpack_state(st[128 * j:128 * j + 128, :]))
        dv.append((lv[:, c] + dot(fk[:, c], r_hi) + dot(fk[:, c], r_lo)).astype(BF))
    term = term + dot(jnp.concatenate(dv, axis=1), wv[...], NT)

    @pl.when(pl.program_id(0) == 0)
    def _():
        acc[...] = term

    @pl.when(pl.program_id(0) > 0)
    def _():
        acc[...] += term

    @pl.when(pl.program_id(0) == pl.num_programs(0) - 1)
    def _():
        dt_o[...] = acc[...].astype(BF)


def wgrad_q_kernel(x_ref, t0, t1, t2, t3, d0, d1, d2, d3, all_o, *send):
    d1, d3 = d1.at[0], d3.at[0]
    n = t0.shape[3]
    blocks, m = t0.shape[1], t0.shape[2]

    def body(step):
        parts = [d[0:n, :].astype(BF) for d in (d0, d1, d2, d3)]
        gain = d0[n:n + 8, :] + d1[n:n + 8, :] + d2[n:n + 8, :] + d3[n:n + 8, :]
        for i in range(2):
            out = send[2 * step + i]
            at = jnp.bitwise_xor(jnp.bitwise_and(x_ref[0], 1), i)
            res = jnp.zeros((blocks * m, d0.shape[1]), F32)
            for j, t in enumerate((t0, t1, t2, t3)):
                turned = t[at].reshape(blocks * m, n).astype(BF)
                all_o[at, :, :, n * j:n * j + n] = turned.reshape(blocks, m, n)
                res = res + dot(turned, parts[j])
            out[:, 0:m, :] = res.reshape(blocks, m, res.shape[1])
            for block in range(blocks):
                out[block, m:m + 8, :] = gain

    each_step(body)


def sum_x_kernel(y_ref, v0, v1, v2, v3, *send):
    for k, out in enumerate(send):
        at = jnp.bitwise_xor(y_ref[0], k)
        out[...] = v0[at] + v1[at] + v2[at] + v3[at]


def wgrad_k_kernel(t, d0, d1, d2, d3, out):
    k, m, w = out.shape
    d = jnp.concatenate([v[...].astype(BF) for v in (d0, d1, d2, d3)], axis=0)
    out[...] = dot(t[...], d).reshape(k, m, w)


def prefix_kernel(backward, v, out):
    count = v.shape[0]
    order = range(count - 1, -1, -1) if backward else range(count)
    total = jnp.zeros(v.shape[1:], F32)
    for i in order:
        out[i] = total
        total = total + v[i]


def join_kernel(q0, q1, q2, q3, k, out):
    total = k[0]
    for i in range(1, k.shape[0]):
        total = total + k[i]
    height, width = total.shape
    each = height // out.shape[0]
    q = q0[...] + q1[...] + q2[...] + q3[...]
    gain = jnp.sum(q[height:height + 8], axis=0, keepdims=True)
    for j in range(out.shape[0]):
        for i in range(each):
            r = each * j + i
            out[j, :, width * i:width * i + width] = q[r:r + 1]
            at = width * (each + i)
            out[j, :, at:at + width] = total[r:r + 1]
        out[j, :, 2 * each * width:] = gain


def final_kernel(v, dw_o, dg_o):
    width = GL
    each = (v.shape[2] // width - 1) // 2
    for c in range(2):
        for b in range(2):
            g = 2 * c + b
            total = v[8 * c + b]
            for w in range(1, 4):
                total = total + v[8 * c + 2 * w + b]
            for which in range(2):
                for i in range(each):
                    r = width * (which * each + i)
                    at = 4 * width * i + width * g
                    dw_o[which:which + 1, at:at + width] = total[:, r:r + width]
            for i in range(2):
                r = width * 2 * each + 128 * i
                dg_o[2 * g + i:2 * g + i + 1, :] = total[:, r:r + 128]


def call(kernel, grid, in_specs, outs, name, flops, scratch=()):
    out_shape = [jax.ShapeDtypeStruct(s, d) for s, d, _ in outs]
    return pl.pallas_call(
        kernel,
        grid=grid,
        in_specs=in_specs,
        out_specs=[spec for _, _, spec in outs],
        out_shape=out_shape,
        scratch_shapes=list(scratch),
        name=name,
        cost_estimate=pl.CostEstimate(flops=flops, bytes_accessed=4 << 20, transcendentals=0),
        compiler_params=pltpu.CompilerParams(vmem_limit_bytes=GRANT.get(name, VMEM_LIMIT)),
    )


def call_mine(kernel, in_specs, outs, name, flops, steps=2):
    return pl.pallas_call(
        kernel,
        grid_spec=pltpu.PrefetchScalarGridSpec(
            num_scalar_prefetch=1,
            grid=(steps,),
            in_specs=in_specs,
            out_specs=[spec for _, _, spec in outs],
        ),
        out_shape=[jax.ShapeDtypeStruct(s, d) for s, d, _ in outs],
        name=name,
        cost_estimate=pl.CostEstimate(flops=flops, bytes_accessed=4 << 20, transcendentals=0),
        compiler_params=pltpu.CompilerParams(vmem_limit_bytes=GRANT.get(name, VMEM_LIMIT)),
    )


SMEM = pl.BlockSpec(memory_space=pltpu.SMEM)


def whole(shape):
    return pl.BlockSpec(shape, lambda *_: (0,) * len(shape))


def col(r, w=GL):
    return pl.BlockSpec((r, w), lambda g: (0, g))


def row(r, w):
    return pl.BlockSpec((r, w), lambda g: (g, 0))


def pair_at(step, me):
    return jnp.bitwise_xor(jnp.right_shift(me[0], 1), step)


def col_mine(r, w):
    return pl.BlockSpec((r, w), lambda step, me: (0, pair_at(step, me)))


def row_mine(r, w):
    return pl.BlockSpec((r, w), lambda step, me: (pair_at(step, me), 0))


def on_device(tokens, w_query, w_key, w_value, w_out, norm_gain, lengths, d_mixed):
    _, n, d = tokens.shape
    tok = tokens.reshape(n, d)
    dm = d_mixed.reshape(n, d)
    w = 2 * GL
    halves = d // w
    nseq = lax.axis_size(SEQ)
    nxy = lax.axis_size(("x", "y"))
    ngroup = lax.axis_size(GROUP)
    nv = lengths - lax.axis_index(SEQ) * n
    own = lambda axes: jnp.full((1,), lax.axis_index(axes), jnp.int32)
    me = own(GROUP)
    gain = norm_gain.reshape(1, d)
    act = lambda dt: ((n, d), dt, col(n, w))
    st_rows = d // 2
    st_spec = row(w // 2, 128)
    state = ((st_rows, 128), F32, st_spec)
    big = 2 * n * d * d

    fk, fv, sk, st1 = call(
        kv_kernel, (halves,), [SMEM, whole((n, d)), col(d, w), col(d, w)],
        [act(BF), act(BF), act(F32), state], "kv", 2 * big,
    )(nv, tok, w_key, w_value)

    tie = lax.optimization_barrier

    def to_parts(st):
        return lax.all_to_all(st.reshape(nseq, st_rows // nseq, 128), SEQ, 0, 0, tiled=True)

    def run(parts, backward, name):
        shape = parts.shape
        (mine,) = call(
            functools.partial(prefix_kernel, backward), (), [whole(shape)],
            [(shape, F32, whole(shape))], name, 1 << 20,
        )(parts)
        return mine

    def from_parts(mine):
        return lax.all_to_all(mine, SEQ, 0, 0, tiled=True).reshape(st_rows, 128)

    def swap(v, k):
        return lax.ppermute(v, GROUP, [(i, i ^ k) for i in range(ngroup)])

    def turn_about(axis, v, k):
        return lax.ppermute(v, axis, [(i, i ^ k) for i in range(lax.axis_size(axis))])

    parts = to_parts(st1)
    tok_1, _ = tie((tok, st1))
    t0, t32 = call(
        turn_kernel, (halves,), [col(n, w)],
        [((d, n), BF, row(w, n)), ((d, n), F32, row(w, n))], "turn", big // 4,
    )(tok_1)
    fq, fqt, sq = call(
        q_kernel, (halves,), [whole((n, d)), col(d, w)],
        [act(BF), ((d, n), BF, row(w, n)), act(F32)], "query", big,
    )(tok_1, w_query)
    parts, fq, t0 = tie((parts, fq, t0))
    mine = run(parts, False, "prefix")

    t32, _ = tie((t32, mine))
    t1 = swap(t32, 1)
    t2 = swap(t32, 2)

    st_in = from_parts(mine)
    fq_2, _ = tie((fq, mine))
    nl, do = call(
        numer_kernel, (halves,),
        [col(n, w), col(n, w), col(n, w), whole((n, d)), row(w, d)],
        [act(F32), act(F32)], "numer", 2 * big,
    )(fq_2, fk, fv, dm, w_out)

    at, dn, rs, gp = call(
        norm_kernel, (halves,),
        [SMEM, col(n, w), st_spec, col(n, w), row(w, n), col(n, w), col(1, w)],
        [act(BF), act(F32), state, ((8, d), F32, col(8, w))], "norm", big,
    )(nv, nl, st_in, fq, fqt, do, gain)

    parts = to_parts(rs)
    dn_3, _ = tie((dn, rs))
    mine_act = ((n, d), BF, col_mine(n, w))
    one = ((n + 8, GL), F32, whole((n + 8, GL)))
    two = ((2, n + 8, GL), F32, whole((2, n + 8, GL)))
    dq, dq_own, dq_near, dq_far = call_mine(
        dq_kernel,
        [col_mine(n, w), row_mine(w // 2, 128)] + [col_mine(n, w)] * 3 + [col_mine(8, w)],
        [mine_act, one, one, two], "dquery", 2 * big,
    )(me, dn_3, st_in, fk, fv, sq, gp)
    parts, dq = tie((parts, dq))
    dq_far = swap(dq_far, 1)
    dq_near = swap(dq_near, 2)
    mine = run(parts, True, "suffix")

    r_in = from_parts(mine)
    dn_4, t1, _ = tie((dn, t1, mine))
    t3 = swap(t1, 2)
    (lk,) = call(
        local_k_kernel, (halves,), [col(n, w), col(n, w), col(n, w)], [act(F32)], "localk", 1,
    )(dn_4, fq, fv)
    lk, dq_near, t2, t3 = tie((lk, dq_near, t2, t3))
    dk, *dk_send = call_mine(
        dk_kernel,
        [col_mine(n, w), col_mine(n, w), row_mine(w // 2, 128), col_mine(n, w)],
        [mine_act] + [((n, GL), F32, whole((n, GL)))] * ngroup,
        "dkey", 1,
    )(me, lk, fv, r_in, sk)

    dk_got = [dk_send[0]] + [swap(dk_send[k], k) for k in range(1, ngroup)]
    side = lax.axis_size("x")
    per = d // nxy
    dq_far, _ = tie((dq_far, dk))
    dq_got = [dq_own, dq_far, dq_near, swap(dq_far, 2)]
    at_x = lambda depth: pl.BlockSpec(
        (2, side, per, depth), lambda step, x: (pair_at(step, x), 0, 0, 0)
    )
    by_xy = lambda v: v.reshape(side, side, per, v.shape[-1])
    qshape = (side, per + 8, GL)
    tall, *gq_send = call_mine(
        wgrad_q_kernel,
        [at_x(n)] * 4 + [
            whole((n + 8, GL)),
            pl.BlockSpec((1, n + 8, GL), lambda *_: (0, 0, 0)),
            whole((n + 8, GL)),
            pl.BlockSpec((1, n + 8, GL), lambda *_: (1, 0, 0)),
        ],
        [((side, side, per, 4 * n), BF, at_x(4 * n))] + [(qshape, F32, whole(qshape))] * side,
        "wgradq", 2 * big,
    )(own("x"), by_xy(t0), by_xy(t1), by_xy(t2), by_xy(t3), *dq_got)
    gq_got = [gq_send[0]] + [turn_about("x", gq_send[k], k) for k in range(1, side)]

    steps = 2
    kshape = (nxy, per, GL)
    (gk,) = call(
        wgrad_k_kernel, (steps,), [row(d // steps, 4 * n)] + [whole((n, GL))] * 4,
        [(kshape, F32, pl.BlockSpec((nxy // steps,) + kshape[1:], lambda g: (g, 0, 0)))],
        "wgradk", 400 * big,
    )(tall.reshape(d, 4 * n), *dk_got)
    gk_parts = lax.all_to_all(gk, ("x", "y"), 0, 0, tiled=True)

    dn_5, _ = tie((dn, gk))
    mo, lv = call(
        local_v_kernel, (halves,),
        [whole((n, d)), col(d, w), col(n, w), col(n, w), col(n, w)], [act(BF), act(F32)], "localv", 400 * big,
    )(at, w_out, dn_5, fq, fk)
    gq_got, _ = tie((gq_got, gk))
    gq_send = call(
        sum_x_kernel, (), [SMEM] + [whole(qshape)] * side,
        [(qshape[1:], F32, whole(qshape[1:]))] * side, "sumx", 1 << 22,
    )(own("y"), *gq_got)
    gq_got = [gq_send[0]] + [turn_about("y", gq_send[k], k) for k in range(1, side)]
    gk_parts, mo, lv, gq_got = tie((gk_parts, mo, lv, gq_got))

    last = ("c", "w", "b")
    nlast = lax.axis_size(last)
    each = per // nlast
    jshape = (nlast, 1, (2 * each + 1) * GL)
    (both,) = call(
        join_kernel, (), [whole(qshape[1:])] * side + [whole(kshape)],
        [(jshape, F32, whole(jshape))], "join", 1 << 22,
    )(*gq_got, gk_parts)
    dk_6, _ = tie((dk, both))
    both = lax.all_to_all(both, last, 0, 0, tiled=True)

    (dt,) = call(
        dtok_kernel, (halves,),
        [col(n, w), col(n, w), st_spec, col(n, w), col(n, w), col(d, w), col(d, w), col(d, w)],
        [((n, d), BF, whole((n, d)))], "dtok", 1,
        scratch=[pltpu.VMEM((n, d), F32)],
    )(lv, fk, r_in, dq, dk_6, w_query, w_key, w_value)
    dw, dg = call(
        final_kernel, (), [whole(jshape)],
        [((2, each * d), F32, whole((2, each * d))), ((8, 128), F32, whole((8, 128)))],
        "final", 1 << 20,
    )(both)
    return mo.reshape(1, n, d), dt.reshape(1, n, d), dw, dg.reshape(d)


def solution(mesh):
    fine = Mesh(mesh.devices.reshape(4, 4, 2, 4, 2), ("x", "y", "c", "w", "b"))
    acts = P(("w", "b"), SEQ, None)
    placed = (acts, P(), P(), P(), P(), P(), P(("w", "b")), acts)
    return jax.shard_map(
        on_device,
        mesh=fine,
        in_specs=placed,
        out_specs=(acts, acts, P(None, ("x", "y", "c", "w", "b")), P()),
        check_vma=False,
    )
```

```python
import functools

import jax
import jax.numpy as jnp
from jax import lax
from jax.experimental import pallas as pl
from jax.experimental.pallas import tpu as pltpu
from jax.sharding import Mesh, PartitionSpec as P

EPS = 1e-05
HD = 64
GL = 256
F32 = jnp.float32
BF = jnp.bfloat16
NN = (((1,), (0,)), ((), ()))
NT = (((1,), (1,)), ((), ()))
TN = (((0,), (0,)), ((), ()))
SEQ = ("x", "y", "c")
GROUP = ("c", "b")
VMEM_LIMIT = 64 * 1024 * 1024
GRANT = {name: 58 << 20 for name in ("turn", "query", "dquery", "localv", "sumy")}
GRANT.update({name: 4 << 20 for name in ("prefix", "suffix", "final")})
GRANT["join"] = 8 << 20


def dot(a, b, dims=NN):
    return lax.dot_general(a, b, dims, preferred_element_type=F32)


def split(v):
    hi = v.astype(BF)
    return hi, (v - hi.astype(F32)).astype(BF)


def lanes(shape):
    return lax.broadcasted_iota(jnp.int32, shape, 1)


def rows(shape):
    return lax.broadcasted_iota(jnp.int32, shape, 0)


def head_masks(shape):
    which = lanes(shape) // HD
    return [which == h for h in range(GL // HD)]


def pick(mask, v):
    return jnp.where(mask, v, jnp.zeros_like(v))


def pack_state(full):
    out = []
    for p in range(GL // 128):
        blk = full[128 * p:128 * p + 128, 128 * p:128 * p + 128]
        out.append(jnp.where(lanes((HD, 128)) < HD, blk[:HD], blk[HD:]))
    return jnp.concatenate(out, axis=0)


def unpack_state(st):
    zero = jnp.zeros((128, 128), st.dtype)
    blks = []
    for p in range(GL // 128):
        a = st[HD * p:HD * p + HD]
        first = lanes((HD, 128)) < HD
        blks.append(jnp.concatenate([pick(first, a), pick(~first, a)], axis=0))
    return jnp.concatenate(
        [
            jnp.concatenate([blks[0], zero], axis=1),
            jnp.concatenate([zero, blks[1]], axis=1),
        ],
        axis=0,
    )


def valid_rows(nv_ref, count):
    return (rows((count, 1)) < nv_ref[0]).astype(F32)


def features(raw):
    ex = jnp.exp(jnp.minimum(raw, 0.0))
    up = raw > 0
    return jnp.where(up, raw + 1.0, ex), jnp.where(up, 1.0, ex)


def head_mean(*parts):
    same = (rows((GL, GL)) // HD == lanes((GL, GL)) // HD).astype(BF)
    total = dot(parts[0], same)
    for p in parts[1:]:
        total = total + dot(p, same)
    return total * (1.0 / HD)


def groups_of(ref):
    return [(j, slice(GL * j, GL * j + GL)) for j in range(ref.shape[-1] // GL)]


def my_groups(me_ref, step):
    for i in range(2):
        at = jnp.bitwise_xor(jnp.bitwise_and(me_ref[0], 1), i)
        yield (
            2 * step + i,
            pl.ds(pl.multiple_of(at * GL, GL), GL),
            pl.ds(pl.multiple_of(at * 128, 128), 128),
        )


def each_step(body):
    for step in range(2):
        pl.when(pl.program_id(0) == step)(functools.partial(body, step))


def kv_kernel(nv_ref, tok, wk, wv, fk_o, fv_o, sk_o, st_o):
    n = tok.shape[0]
    valid = valid_rows(nv_ref, n)
    feat, slope = features(dot(tok[...], wk[...]))
    fk = (feat * valid).astype(BF)
    fv = dot(tok[...], wv[...]).astype(BF)
    fk_o[...] = fk
    fv_o[...] = fv
    sk_o[...] = slope * valid
    for j, c in groups_of(fk):
        st_o[128 * j:128 * j + 128, :] = pack_state(dot(fk[:, c], fv[:, c], TN))


def turn_kernel(tok, t16_o, t32_o):
    n = tok.shape[0]
    eye = (rows((n, n)) == lanes((n, n))).astype(BF)
    res = dot(tok[...], eye, TN)
    t16_o[...] = res.astype(BF)
    t32_o[...] = res


def q_kernel(tok, wq, fq_o, fqt_o, sq_o):
    feat, slope = features(dot(tok[...], wq[...]))
    fq = feat.astype(BF)
    fq_o[...] = fq
    sq_o[...] = slope
    eye = (rows((GL, GL)) == lanes((GL, GL))).astype(BF)
    for _, c in groups_of(fq):
        fqt_o[c, :] = dot(eye, fq[:, c], NT).astype(BF)


def numer_kernel(fq, fk, fv, dm, wo, nl_o, do_o):
    n = fq.shape[0]
    do_o[...] = dot(dm[...], wo[...], NT)
    causal = rows((n, n)) >= lanes((n, n))
    for _, c in groups_of(fq):
        total = jnp.zeros((n, GL), F32)
        for m in head_masks((n, GL)):
            s = pick(causal, dot(pick(m, fq[:, c]), fk[:, c], NT)).astype(BF)
            total = total + dot(s, pick(m, fv[:, c]))
        nl_o[:, c] = total


def norm_kernel(nv_ref, nl, st, fq, fqt, do, gain, at_o, dn_o, rs_o, gp_o):
    n = nl.shape[0]
    valid = valid_rows(nv_ref, n)
    for j, c in groups_of(nl):
        r = slice(128 * j, 128 * j + 128)
        s_hi, s_lo = split(unpack_state(st[r, :]))
        numer = nl[:, c] + dot(fq[:, c], s_hi) + dot(fq[:, c], s_lo)
        inv = lax.rsqrt(head_mean((numer * numer).astype(BF)) + EPS)
        normed = numer * inv
        scale = gain[:, c]
        at_o[:, c] = (normed * scale * valid).astype(BF)
        dov = do[:, c] * valid
        gp_o[:, c] = jnp.sum((dov * normed).reshape(n // 8, 8, GL), axis=0)
        g = dov * scale
        dn = inv * (g - normed * head_mean(*split(g * normed)))
        dn_o[:, c] = dn
        d_hi, d_lo = split(dn)
        rs_o[r, :] = pack_state(dot(fqt[c, :], d_hi) + dot(fqt[c, :], d_lo))


def dq_kernel(me_ref, dn, st, fk, fv, sq, gp, dq_o, mine, near, far):
    n = dn.shape[0]

    def body(step):
        causal = rows((n, n)) >= lanes((n, n))
        for k, c, r in my_groups(me_ref, step):
            s_hi, s_lo = split(unpack_state(st[r, :]))
            d_hi, d_lo = split(dn[:, c])
            total = dot(d_hi, s_hi, NT) + dot(d_lo, s_hi, NT) + dot(d_hi, s_lo, NT)
            keys, values = fk[:, c], fv[:, c]
            for m in head_masks((n, GL)):
                vm = pick(m, values)
                w = pick(causal, dot(d_hi, vm, NT) + dot(d_lo, vm, NT)).astype(BF)
                total = total + dot(w, pick(m, keys))
            dq = (total * sq[:, c]).astype(BF)
            dq_o[:, c] = dq
            out = (mine, far.at[0], near, far.at[1])[k]
            out[0:n, :] = dq.astype(F32)
            out[n:n + 8, :] = gp[:, c]

    each_step(body)


def local_k_kernel(dn, fq, fv, lk_o):
    n = dn.shape[0]
    later = lanes((n, n)) >= rows((n, n))
    for _, c in groups_of(dn):
        d_hi, d_lo = split(dn[:, c])
        total = jnp.zeros((n, GL), F32)
        for m in head_masks((n, GL)):
            vm = pick(m, fv[:, c])
            w = pick(later, dot(vm, d_hi, NT) + dot(vm, d_lo, NT)).astype(BF)
            total = total + dot(w, pick(m, fq[:, c]))
        lk_o[:, c] = total


def local_v_kernel(at, wo, dn, fq, fk, mo_o, lv_o):
    n = dn.shape[0]
    mo_o[...] = dot(at[...], wo[...]).astype(BF)
    later = lanes((n, n)) >= rows((n, n))
    for _, c in groups_of(dn):
        d_hi = dn[:, c].astype(BF)
        total = jnp.zeros((n, GL), F32)
        for m in head_masks((n, GL)):
            s = pick(later, dot(pick(m, fk[:, c]), fq[:, c], NT)).astype(BF)
            total = total + dot(s, pick(m, d_hi))
        lv_o[:, c] = total


def dk_kernel(me_ref, lk, fv, st, sk, dk_o, *send):
    def body(step):
        for k, c, r in my_groups(me_ref, step):
            r_hi, r_lo = split(unpack_state(st[r, :]))
            total = lk[:, c] + dot(fv[:, c], r_hi, NT) + dot(fv[:, c], r_lo, NT)
            dk = (total * sk[:, c]).astype(BF)
            dk_o[:, c] = dk
            send[k][...] = dk.astype(F32)

    each_step(body)


def dtok_kernel(lv, fk, st, dq, dk, wq, wk, wv, dt_o, acc):
    term = dot(dq[...], wq[...], NT) + dot(dk[...], wk[...], NT)
    dv = []
    for j, c in groups_of(lv):
        r_hi, r_lo = split(unpack_state(st[128 * j:128 * j + 128, :]))
        dv.append((lv[:, c] + dot(fk[:, c], r_hi) + dot(fk[:, c], r_lo)).astype(BF))
    term = term + dot(jnp.concatenate(dv, axis=1), wv[...], NT)

    @pl.when(pl.program_id(0) == 0)
    def _():
        acc[...] = term

    @pl.when(pl.program_id(0) > 0)
    def _():
        acc[...] += term

    @pl.when(pl.program_id(0) == pl.num_programs(0) - 1)
    def _():
        dt_o[...] = acc[...].astype(BF)


def wgrad_q_kernel(y_ref, t0, t1, t2, t3, d0, d1, d2, d3, all_o, *send):
    d1, d3 = d1.at[0], d3.at[0]
    n = t0.shape[3]
    blocks, m = t0.shape[0], t0.shape[2]

    def body(step):
        parts = [d[0:n, :].astype(BF) for d in (d0, d1, d2, d3)]
        gain = d0[n:n + 8, :] + d1[n:n + 8, :] + d2[n:n + 8, :] + d3[n:n + 8, :]
        for i in range(2):
            out = send[2 * step + i]
            at = jnp.bitwise_xor(jnp.bitwise_and(y_ref[0], 1), i)
            res = jnp.zeros((blocks * m, d0.shape[1]), F32)
            for j, t in enumerate((t0, t1, t2, t3)):
                turned = t[:, at].reshape(blocks * m, n).astype(BF)
                all_o[:, at, :, n * j:n * j + n] = turned.reshape(blocks, m, n)
                res = res + dot(turned, parts[j])
            out[:, 0:m, :] = res.reshape(blocks, m, res.shape[1])
            for block in range(blocks):
                out[block, m:m + 8, :] = gain

    each_step(body)


def sum_y_kernel(x_ref, v0, v1, v2, v3, *send):
    for k, out in enumerate(send):
        at = jnp.bitwise_xor(x_ref[0], k)
        out[...] = v0[at] + v1[at] + v2[at] + v3[at]


def wgrad_k_kernel(t, d0, d1, d2, d3, out):
    k, m, w = out.shape
    d = jnp.concatenate([v[...].astype(BF) for v in (d0, d1, d2, d3)], axis=0)
    out[...] = dot(t[...], d).reshape(k, m, w)


def prefix_kernel(backward, v, out):
    count = v.shape[0]
    order = range(count - 1, -1, -1) if backward else range(count)
    total = jnp.zeros(v.shape[1:], F32)
    for i in order:
        out[i] = total
        total = total + v[i]


def join_kernel(q0, q1, q2, q3, k, out):
    total = k[0]
    for i in range(1, k.shape[0]):
        total = total + k[i]
    height, width = total.shape
    each = height // out.shape[0]
    q = q0[...] + q1[...] + q2[...] + q3[...]
    gain = jnp.sum(q[height:height + 8], axis=0, keepdims=True)
    for j in range(out.shape[0]):
        for i in range(each):
            r = each * j + i
            out[j, :, width * i:width * i + width] = q[r:r + 1]
            at = width * (each + i)
            out[j, :, at:at + width] = total[r:r + 1]
        out[j, :, 2 * each * width:] = gain


def final_kernel(v, dw_o, dg_o):
    width = GL
    each = (v.shape[2] // width - 1) // 2
    for c in range(2):
        for b in range(2):
            g = 2 * c + b
            total = v[8 * c + b]
            for w in range(1, 4):
                total = total + v[8 * c + 2 * w + b]
            for which in range(2):
                for i in range(each):
                    r = width * (which * each + i)
                    at = 4 * width * i + width * g
                    dw_o[which:which + 1, at:at + width] = total[:, r:r + width]
            for i in range(2):
                r = width * 2 * each + 128 * i
                dg_o[2 * g + i:2 * g + i + 1, :] = total[:, r:r + 128]


def call(kernel, grid, in_specs, outs, name, flops, scratch=()):
    out_shape = [jax.ShapeDtypeStruct(s, d) for s, d, _ in outs]
    return pl.pallas_call(
        kernel,
        grid=grid,
        in_specs=in_specs,
        out_specs=[spec for _, _, spec in outs],
        out_shape=out_shape,
        scratch_shapes=list(scratch),
        name=name,
        cost_estimate=pl.CostEstimate(flops=flops, bytes_accessed=4 << 20, transcendentals=0),
        compiler_params=pltpu.CompilerParams(vmem_limit_bytes=GRANT.get(name, VMEM_LIMIT)),
    )


def call_mine(kernel, in_specs, outs, name, flops, steps=2):
    return pl.pallas_call(
        kernel,
        grid_spec=pltpu.PrefetchScalarGridSpec(
            num_scalar_prefetch=1,
            grid=(steps,),
            in_specs=in_specs,
            out_specs=[spec for _, _, spec in outs],
        ),
        out_shape=[jax.ShapeDtypeStruct(s, d) for s, d, _ in outs],
        name=name,
        cost_estimate=pl.CostEstimate(flops=flops, bytes_accessed=4 << 20, transcendentals=0),
        compiler_params=pltpu.CompilerParams(vmem_limit_bytes=GRANT.get(name, VMEM_LIMIT)),
    )


SMEM = pl.BlockSpec(memory_space=pltpu.SMEM)


def whole(shape):
    return pl.BlockSpec(shape, lambda *_: (0,) * len(shape))


def col(r, w=GL):
    return pl.BlockSpec((r, w), lambda g: (0, g))


def row(r, w):
    return pl.BlockSpec((r, w), lambda g: (g, 0))


def pair_at(step, me):
    return jnp.bitwise_xor(jnp.right_shift(me[0], 1), step)


def col_mine(r, w):
    return pl.BlockSpec((r, w), lambda step, me: (0, pair_at(step, me)))


def row_mine(r, w):
    return pl.BlockSpec((r, w), lambda step, me: (pair_at(step, me), 0))


def on_device(tokens, w_query, w_key, w_value, w_out, norm_gain, lengths, d_mixed):
    _, n, d = tokens.shape
    tok = tokens.reshape(n, d)
    dm = d_mixed.reshape(n, d)
    w = 2 * GL
    halves = d // w
    nseq = lax.axis_size(SEQ)
    nxy = lax.axis_size(("x", "y"))
    ngroup = lax.axis_size(GROUP)
    nv = lengths - lax.axis_index(SEQ) * n
    own = lambda axes: jnp.full((1,), lax.axis_index(axes), jnp.int32)
    me = own(GROUP)
    gain = norm_gain.reshape(1, d)
    act = lambda dt: ((n, d), dt, col(n, w))
    st_rows = d // 2
    st_spec = row(w // 2, 128)
    state = ((st_rows, 128), F32, st_spec)
    big = 2 * n * d * d

    fk, fv, sk, st1 = call(
        kv_kernel, (halves,), [SMEM, whole((n, d)), col(d, w), col(d, w)],
        [act(BF), act(BF), act(F32), state], "kv", 2 * big,
    )(nv, tok, w_key, w_value)

    tie = lax.optimization_barrier

    def to_parts(st):
        return lax.all_to_all(st.reshape(nseq, st_rows // nseq, 128), SEQ, 0, 0, tiled=True)

    def run(parts, backward, name):
        shape = parts.shape
        (mine,) = call(
            functools.partial(prefix_kernel, backward), (), [whole(shape)],
            [(shape, F32, whole(shape))], name, 1 << 20,
        )(parts)
        return mine

    def from_parts(mine):
        return lax.all_to_all(mine, SEQ, 0, 0, tiled=True).reshape(st_rows, 128)

    def swap(v, k):
        return lax.ppermute(v, GROUP, [(i, i ^ k) for i in range(ngroup)])

    def turn_about(axis, v, k):
        return lax.ppermute(v, axis, [(i, i ^ k) for i in range(lax.axis_size(axis))])

    parts = to_parts(st1)
    tok_1, _ = tie((tok, st1))
    t0, t32 = call(
        turn_kernel, (halves,), [col(n, w)],
        [((d, n), BF, row(w, n)), ((d, n), F32, row(w, n))], "turn", big // 4,
    )(tok_1)
    fq, fqt, sq = call(
        q_kernel, (halves,), [whole((n, d)), col(d, w)],
        [act(BF), ((d, n), BF, row(w, n)), act(F32)], "query", big,
    )(tok_1, w_query)
    parts, fq, t0 = tie((parts, fq, t0))
    mine = run(parts, False, "prefix")

    t32, _ = tie((t32, mine))
    t1 = swap(t32, 1)
    t2 = swap(t32, 2)

    st_in = from_parts(mine)
    fq_2, _ = tie((fq, mine))
    nl, do = call(
        numer_kernel, (halves,),
        [col(n, w), col(n, w), col(n, w), whole((n, d)), row(w, d)],
        [act(F32), act(F32)], "numer", 2 * big,
    )(fq_2, fk, fv, dm, w_out)

    at, dn, rs, gp = call(
        norm_kernel, (halves,),
        [SMEM, col(n, w), st_spec, col(n, w), row(w, n), col(n, w), col(1, w)],
        [act(BF), act(F32), state, ((8, d), F32, col(8, w))], "norm", big,
    )(nv, nl, st_in, fq, fqt, do, gain)

    parts = to_parts(rs)
    dn_3, _ = tie((dn, rs))
    mine_act = ((n, d), BF, col_mine(n, w))
    one = ((n + 8, GL), F32, whole((n + 8, GL)))
    two = ((2, n + 8, GL), F32, whole((2, n + 8, GL)))
    dq, dq_own, dq_near, dq_far = call_mine(
        dq_kernel,
        [col_mine(n, w), row_mine(w // 2, 128)] + [col_mine(n, w)] * 3 + [col_mine(8, w)],
        [mine_act, one, one, two], "dquery", 2 * big,
    )(me, dn_3, st_in, fk, fv, sq, gp)
    parts, dq = tie((parts, dq))
    dq_far = swap(dq_far, 1)
    dq_near = swap(dq_near, 2)
    mine = run(parts, True, "suffix")

    r_in = from_parts(mine)
    dn_4, t1, _ = tie((dn, t1, mine))
    t3 = swap(t1, 2)
    (lk,) = call(
        local_k_kernel, (halves,), [col(n, w), col(n, w), col(n, w)], [act(F32)], "localk", 1,
    )(dn_4, fq, fv)
    lk, dq_near, t2, t3 = tie((lk, dq_near, t2, t3))
    dk, *dk_send = call_mine(
        dk_kernel,
        [col_mine(n, w), col_mine(n, w), row_mine(w // 2, 128), col_mine(n, w)],
        [mine_act] + [((n, GL), F32, whole((n, GL)))] * ngroup,
        "dkey", 1,
    )(me, lk, fv, r_in, sk)

    dk_got = [dk_send[0]] + [swap(dk_send[k], k) for k in range(1, ngroup)]
    side = lax.axis_size("x")
    per = d // nxy
    dq_far, _ = tie((dq_far, dk))
    dq_got = [dq_own, dq_far, dq_near, swap(dq_far, 2)]
    at_y = lambda depth: pl.BlockSpec(
        (side, 2, per, depth), lambda step, y: (0, pair_at(step, y), 0, 0)
    )
    by_xy = lambda v: v.reshape(side, side, per, v.shape[-1])
    qshape = (side, per + 8, GL)
    tall, *gq_send = call_mine(
        wgrad_q_kernel,
        [at_y(n)] * 4 + [
            whole((n + 8, GL)),
            pl.BlockSpec((1, n + 8, GL), lambda *_: (0, 0, 0)),
            whole((n + 8, GL)),
            pl.BlockSpec((1, n + 8, GL), lambda *_: (1, 0, 0)),
        ],
        [((side, side, per, 4 * n), BF, at_y(4 * n))] + [(qshape, F32, whole(qshape))] * side,
        "wgradq", 2 * big,
    )(own("y"), by_xy(t0), by_xy(t1), by_xy(t2), by_xy(t3), *dq_got)
    gq_got = [gq_send[0]] + [turn_about("y", gq_send[k], k) for k in range(1, side)]

    steps = 2
    kshape = (nxy, per, GL)
    (gk,) = call(
        wgrad_k_kernel, (steps,), [row(d // steps, 4 * n)] + [whole((n, GL))] * 4,
        [(kshape, F32, pl.BlockSpec((nxy // steps,) + kshape[1:], lambda g: (g, 0, 0)))],
        "wgradk", 400 * big,
    )(tall.reshape(d, 4 * n), *dk_got)
    gk_parts = lax.all_to_all(gk, ("x", "y"), 0, 0, tiled=True)

    dn_5, _ = tie((dn, gk))
    mo, lv = call(
        local_v_kernel, (halves,),
        [whole((n, d)), col(d, w), col(n, w), col(n, w), col(n, w)], [act(BF), act(F32)], "localv", 400 * big,
    )(at, w_out, dn_5, fq, fk)
    gq_got, _ = tie((gq_got, gk))
    gq_send = call(
        sum_y_kernel, (), [SMEM] + [whole(qshape)] * side,
        [(qshape[1:], F32, whole(qshape[1:]))] * side, "sumy", 1 << 22,
    )(own("x"), *gq_got)
    gq_got = [gq_send[0]] + [turn_about("x", gq_send[k], k) for k in range(1, side)]
    gk_parts, mo, lv, gq_got = tie((gk_parts, mo, lv, gq_got))

    last = ("c", "w", "b")
    nlast = lax.axis_size(last)
    each = per // nlast
    jshape = (nlast, 1, (2 * each + 1) * GL)
    (both,) = call(
        join_kernel, (), [whole(qshape[1:])] * side + [whole(kshape)],
        [(jshape, F32, whole(jshape))], "join", 1 << 22,
    )(*gq_got, gk_parts)
    dk_6, _ = tie((dk, both))
    both = lax.all_to_all(both, last, 0, 0, tiled=True)

    (dt,) = call(
        dtok_kernel, (halves,),
        [col(n, w), col(n, w), st_spec, col(n, w), col(n, w), col(d, w), col(d, w), col(d, w)],
        [((n, d), BF, whole((n, d)))], "dtok", 1,
        scratch=[pltpu.VMEM((n, d), F32)],
    )(lv, fk, r_in, dq, dk_6, w_query, w_key, w_value)
    dw, dg = call(
        final_kernel, (), [whole(jshape)],
        [((2, each * d), F32, whole((2, each * d))), ((8, 128), F32, whole((8, 128)))],
        "final", 1 << 20,
    )(both)
    return mo.reshape(1, n, d), dt.reshape(1, n, d), dw, dg.reshape(d)


def solution(mesh):
    fine = Mesh(mesh.devices.reshape(4, 4, 2, 4, 2), ("x", "y", "c", "w", "b"))
    acts = P(("w", "b"), SEQ, None)
    placed = (acts, P(), P(), P(), P(), P(), P(("w", "b")), acts)
    return jax.shard_map(
        on_device,
        mesh=fine,
        in_specs=placed,
        out_specs=(acts, acts, P(None, ("x", "y", "c", "w", "b")), P()),
        check_vma=False,
    )
```
